32 devices in a mesh: dp: 8 (over y, x, core), seq: 4 (over z).
Axes of the slice: x: 2, y: 2, z: 4, core: 2. Of those that a mesh axis runs over, the one named last changes fastest.
Arguments:
- tokens: bfloat16 [8, 1024, 768], P('dp', 'seq'), may hold values from -6 to 6
- group_ids: int32 [8], P('dp'), may hold values from 0 to 15
- lengths: int32 [8], P('dp'), may hold values from 256 to 1024, as said below
- cotangent: bfloat16 [8, 1024, 768], P('dp', 'seq'), may hold values from -6 to 6
- group_table: float32 [16, 768], replicated, may hold values from -3 to 3
- first_gain: float32 [768], replicated, may hold values from 0.1 to 1.9
- first_shift: float32 [768], replicated, may hold values from -1.8 to 1.8
- qkv_weight: bfloat16 [768, 2304], replicated, may hold values from -0.21875 to 0.21875
- query_value_bias: float32 [2, 768], replicated, may hold values from -1.8 to 1.8
- out_weight: bfloat16 [768, 768], replicated, may hold values from -1.25 to 1.25
- out_bias: float32 [768], replicated, may hold values from -1.8 to 1.8
- second_gain: float32 [768], replicated, may hold values from 0.1 to 1.9
- second_shift: float32 [768], replicated, may hold values from -1.8 to 1.8
- up_weight: bfloat16 [768, 3072], replicated, may hold values from -0.21875 to 0.21875
- up_bias: float32 [3072], replicated, may hold values from -1.8 to 1.8
- down_weight: bfloat16 [3072, 768], replicated, may hold values from -0.109375 to 0.109375
- down_bias: float32 [768], replicated, may hold values from -1.8 to 1.8
Outputs:
- result: bfloat16 [8, 1024, 768], P('dp', 'seq')
- grad_tokens: bfloat16 [8, 1024, 768], P('dp', 'seq')
- grad_group_table: float32 [16, 768], replicated
- grad_first_gain: float32 [768], replicated
- grad_first_shift: float32 [768], replicated
- grad_qkv_weight: float32 [768, 2304], P('dp', 'seq')
- grad_query_value_bias: float32 [2, 768], replicated
- grad_out_weight: float32 [768, 768], P('dp', 'seq')
- grad_out_bias: float32 [768], replicated
- grad_second_gain: float32 [768], replicated
- grad_second_shift: float32 [768], replicated
- grad_up_weight: float32 [768, 3072], P('dp', 'seq')
- grad_up_bias: float32 [3072], replicated
- grad_down_weight: float32 [3072, 768], P('dp', 'seq')
- grad_down_bias: float32 [768], replicated
The draws below stay inside these ranges and needn't reach their ends.
Inputs may be any that keep to these rules, and one draw needn't show every extreme that they name: `lengths`: in each index of dp (sequences k * 1 to k + 1 - 1) one sequence has length 1024.
All inputs are finite; a program needn't handle non-finite values.
Results may differ from the reference program's by a relative error of at most 0.015.
Values may be sent and summed in bfloat16 or wider, within the bound.
A program may use at most 128 MiB of HBM per device.

```python
import math
import jax
import jax.numpy as jnp
from jax import lax

D = 768
HEADS = 12
HEAD = 64
FF = 3072
GROUPS = 16
LEN = 1024
SEQ_GRP = 1
SEQS = 8


def draw_lengths(key, part):
    key = jax.random.fold_in(key, 7)
    first, second = jax.random.split(key)
    uniform_len = jax.random.randint(first, (SEQS,), LEN // 4, LEN + 1)
    chosen = jax.random.randint(second, (SEQS // SEQ_GRP, 1), 0, SEQ_GRP)
    longest = (jnp.arange(SEQ_GRP)[None, :] == chosen).reshape(SEQS)
    return jnp.where(longest, LEN, uniform_len).astype(jnp.int32)


def place_ends(drawn, own_key, low, largest):
    extent = drawn.shape
    place = [jax.random.randint(jax.random.fold_in(own_key, axis), (), 0, extent[axis]) for axis in range(len(extent))]
    drawn = drawn.at[tuple(place)].set(low)
    longest = extent.index(max(extent))
    place[longest] = (place[longest] + 1) % extent[longest]
    return drawn.at[tuple(place)].set(largest)


def shard_levels(stream_key, extent, pieces, low, high):
    level, own = 1.0, jax.random.fold_in(stream_key, 6)
    for dim, shards_of in pieces:
        heights = jnp.exp(jax.random.uniform(jax.random.fold_in(own, dim), (shards_of,), jnp.float32, low / len(pieces), high / len(pieces)))
        level = level * jnp.repeat(heights, extent[dim] // shards_of).reshape([-1 if axis == dim else 1 for axis in range(len(extent))])
    return level


def scatter_about(own_key, shape, scale, most, shards=(), held_as=jnp.bfloat16):
    values = jax.random.normal(own_key, shape, jnp.float32) * scale
    if len(shards) > 0:
        values = shard_levels(own_key, shape, shards, -0.22, 0.18) * values
    return jnp.clip(values, min=-most, max=most).astype(held_as)


def setup_inputs(seed: int = 0) -> dict:
    keys = jax.random.split(jax.random.key(seed), 18)
    tokens = scatter_about(keys[0], (SEQS, LEN, D), 1.0, 6.0, ((0, 8), (1, 4)))
    group_ids = place_ends(jax.random.randint(keys[1], (SEQS,), 0, GROUPS), jax.random.fold_in(keys[1], 1), 0, GROUPS - 1).astype(jnp.int32)
    lengths = draw_lengths(jax.random.fold_in(keys[17], 71), 0)
    cotangent = scatter_about(keys[3], (SEQS, LEN, D), 1.0, 6.0, ((0, 8), (1, 4)))
    group_table = scatter_about(keys[4], (GROUPS, D), 0.5, 3.0, (), jnp.float32)
    first_gain = jnp.clip(1.0 + 0.18 * jax.random.normal(keys[5], (D,), jnp.float32), 0.1, 1.9)
    first_shift = scatter_about(keys[6], (D,), 0.3, 1.8, (), jnp.float32)
    qkv_weight = scatter_about(keys[7], (D, 3 * D), D ** -0.5, 0.21875)
    query_value_bias = scatter_about(keys[8], (2, D), 0.3, 1.8, (), jnp.float32)
    out_weight = scatter_about(keys[9], (D, D), (D // 32) ** -0.5, 1.25)
    out_bias = scatter_about(keys[10], (D,), 0.3, 1.8, (), jnp.float32)
    second_gain = jnp.clip(1.0 + 0.18 * jax.random.normal(keys[11], (D,), jnp.float32), 0.1, 1.9)
    second_shift = scatter_about(keys[12], (D,), 0.3, 1.8, (), jnp.float32)
    up_weight = scatter_about(keys[13], (D, FF), D ** -0.5, 0.21875)
    up_bias = scatter_about(keys[14], (FF,), 0.3, 1.8, (), jnp.float32)
    down_weight = scatter_about(keys[15], (FF, D), FF ** -0.5, 0.109375)
    down_bias = scatter_about(keys[16], (D,), 0.3, 1.8, (), jnp.float32)
    return dict(tokens=tokens, group_ids=group_ids, lengths=lengths, cotangent=cotangent, group_table=group_table, first_gain=first_gain, first_shift=first_shift, qkv_weight=qkv_weight, query_value_bias=query_value_bias, out_weight=out_weight, out_bias=out_bias, second_gain=second_gain, second_shift=second_shift, up_weight=up_weight, up_bias=up_bias, down_weight=down_weight, down_bias=down_bias)


EPSILON = 1e-05
NEG_LARGE = -1e+30
EXACT = lax.Precision.HIGHEST

@jax.custom_vjp
def low(v):
    return lax.optimization_barrier(v.astype(jnp.bfloat16)).astype(jnp.float32)

@jax.custom_vjp
def low_back(v):
    return v

def low_keep(v):
    return (low(v), None)

def low_pass(kept, grad):
    return (grad,)

def back_keep(v):
    return (v, None)

def back_low(kept, grad):
    return (low(grad),)
low.defvjp(low_keep, low_pass)
low_back.defvjp(back_keep, back_low)

def layer_norm(inputs, norm_gain, norm_shift):
    average = lax.optimization_barrier(jnp.mean(inputs, -1, keepdims=True))
    centred = inputs - average
    inverse = lax.rsqrt(lax.optimization_barrier(jnp.mean(centred * centred, -1, keepdims=True)) + EPSILON)
    return centred * inverse * norm_gain + norm_shift

def attend(mixed_rows, lengths):
    batch_size = mixed_rows.shape[0]
    query_rows = mixed_rows[..., :D].reshape(batch_size, LEN, HEADS, HEAD)
    key_heads = mixed_rows[..., D:2 * D].reshape(batch_size, LEN, HEADS, HEAD)
    valued = mixed_rows[..., 2 * D:].reshape(batch_size, LEN, HEADS, HEAD)
    raw_scores = jnp.einsum('bqhe,bkhe->bhqk', query_rows, key_heads, precision=EXACT) * HEAD ** (-0.5)
    raw_scores = low_back(raw_scores)
    position = jnp.arange(LEN)
    allowed = (position[:, None] >= position[None, :])[None] & (position[None, None, :] < lengths[:, None, None])
    masked_scores = jnp.where(allowed[:, None], raw_scores, NEG_LARGE)
    weights = low(jax.nn.softmax(masked_scores, axis=-1))
    attended = jnp.einsum('bhqk,bkhe->bqhe', weights, valued, precision=EXACT)
    return attended.reshape(batch_size * LEN, D)

def layer_block(start_rows, lengths, params):
    first_gain, first_shift, qkv_weight, query_value_bias, out_weight, out_bias, second_gain, second_shift, up_weight, up_bias, down_weight, down_bias = params
    batch_size = start_rows.shape[0]
    flat_rows = start_rows.reshape(batch_size * LEN, D)
    norm_one = low(layer_norm(flat_rows, first_gain, first_shift))
    full_bias = jnp.concatenate([query_value_bias[0], jnp.zeros((D,), jnp.float32), query_value_bias[1]])
    mixed_rows = low(low_back(jnp.dot(norm_one, qkv_weight, precision=EXACT)) + full_bias)
    attended = low(low_back(attend(mixed_rows.reshape(batch_size, LEN, 3 * D), lengths)))
    after_attn = flat_rows + low_back(jnp.dot(attended, out_weight, precision=EXACT)) + out_bias
    norm_two = low(layer_norm(after_attn, second_gain, second_shift))
    up_rows = low_back(jnp.dot(norm_two, up_weight, precision=EXACT)) + up_bias
    activated = low(jax.nn.gelu(up_rows, approximate=True))
    result_rows = after_attn + jnp.dot(activated, down_weight, precision=EXACT) + down_bias
    return result_rows.reshape(batch_size, LEN, D)

def forward(tokens, group_ids, lengths, group_table, params):
    one_hot = (group_ids[:, None] == jnp.arange(GROUPS)[None, :]).astype(jnp.float32)
    start_rows = tokens + jnp.dot(one_hot, group_table, precision=EXACT)[:, None, :]
    per_batch = math.gcd(SEQS, max(1, 4096 // LEN))
    shaped = start_rows.reshape(SEQS // per_batch, per_batch, LEN, D)
    length_rows = lengths.reshape(SEQS // per_batch, per_batch)

    def layer_step(batch_pair):
        return jax.checkpoint(layer_block)(batch_pair[0], batch_pair[1], params)
    return lax.map(layer_step, (shaped, length_rows)).reshape(SEQS, LEN, D)

def reference(tokens, group_ids, lengths, cotangent, group_table, first_gain, first_shift, qkv_weight, query_value_bias, out_weight, out_bias, second_gain, second_shift, up_weight, up_bias, down_weight, down_bias):
    floats = [weight_arg.astype(jnp.float32) for weight_arg in (group_table, first_gain, first_shift, qkv_weight, query_value_bias, out_weight, out_bias, second_gain, second_shift, up_weight, up_bias, down_weight, down_bias)]

    def forward_of(inputs, table_arg, *params):
        return forward(inputs, group_ids, lengths, table_arg, params)
    result, pull_back = jax.vjp(forward_of, tokens.astype(jnp.float32), *floats)
    gradients = pull_back(cotangent.astype(jnp.float32))
    return (result.astype(jnp.bfloat16), gradients[0].astype(jnp.bfloat16), gradients[1], gradients[2], gradients[3], gradients[4], gradients[5], gradients[6], gradients[7], gradients[8], gradients[9], gradients[10], gradients[11], gradients[12], gradients[13])
```

```python
import functools
import math
import types

import jax
import jax.numpy as jnp
from jax import lax
from jax.experimental import pallas as pl
from jax.experimental.pallas import tpu as pltpu
from jax.sharding import PartitionSpec as P

HEADS = 12
HEAD = 64


EPSILON = 1e-05
NEG_LARGE = -1e30
EXACT = lax.Precision.HIGHEST


VMEM_LIMIT = 64 << 20


BF = jnp.bfloat16
F32 = jnp.float32
MESH = pl.DeviceIdType.MESH
LOG2E = 1.4426950408889634


def dot(a, b):
    return lax.dot_general(a, b, (((1,), (0,)), ((), ())), preferred_element_type=F32)


def dot_nt(a, b):
    return lax.dot_general(a, b, (((1,), (1,)), ((), ())), preferred_element_type=F32)


def dot_tn(a, b):
    return lax.dot_general(a, b, (((0,), (0,)), ((), ())), preferred_element_type=F32)


def flipped(index, bit):
    return index + bit - 2 * bit * lax.rem(index // bit, 2)


class Place:
    def __init__(self):
        self.d = lax.axis_index("dp")
        self.z = lax.axis_index("seq")
        self.c = lax.rem(self.d, 2)
        self.x = lax.rem(self.d // 2, 2)
        self.y = lax.rem(self.d // 4, 2)
        self.zl = lax.rem(self.z, 2)
        self.zh = lax.rem(self.z // 2, 2)
        self.core = (flipped(self.d, 1), self.z)
        self.along_x = (flipped(self.d, 2), self.z)
        self.along_y = (flipped(self.d, 4), self.z)
        self.z_near = (self.d, flipped(self.z, 1))
        self.z_far = (self.d, flipped(self.z, 2))

    def around(self, k):
        return (self.d, lax.rem(self.z + k, 4))


def send(src, dst, sems, index, to):
    copy = pltpu.make_async_remote_copy(
        src_ref=src,
        dst_ref=dst,
        send_sem=sems.at[0, index],
        recv_sem=sems.at[1, index],
        device_id=to,
        device_id_type=MESH,
    )
    return copy


class ReduceScatter:
    def __init__(self, place, g, rc, r1, r2, rz1, rz2, core_sems, sems, parts):
        self.p, self.g, self.rc, self.r1, self.r2 = place, g, rc, r1, r2
        self.rz1, self.rz2, self.core_sems, self.sems, self.parts = rz1, rz2, core_sems, sems, parts

    def core_copy(self, part):
        p = self.p
        if self.parts == "yx":
            ky, kx = part // 2, lax.rem(part, 2)
            src = self.g.at[:, ky, kx, 1 - p.c]
            dst = self.rc.at[:, ky, kx]
        elif self.parts == "z":
            kh, kl = part // 2, lax.rem(part, 2)
            src = self.g.at[:, :, :, 1 - p.c, kh, kl]
            dst = self.rc.at[:, :, :, kh, kl]
        else:
            src = self.g.at[:, :, :, 1 - p.c]
            dst = self.rc
        return send(src, dst, self.core_sems, part, p.core)

    def core_start(self, part):
        self.core_copy(part).start()

    def core_sum(self):
        p = self.p
        for part in range(4 if self.parts else 1):
            self.core_copy(part).wait()

        def add(i, _):
            h, ky, kx = i // 4, lax.rem(i // 2, 2), lax.rem(i, 2)
            self.g[h, ky, kx, p.c] = self.g[h, ky, kx, p.c] + self.rc[h, ky, kx]
            return 0

        lax.fori_loop(0, 8, add, 0)

    def first_copies(self):
        p, g = self.p, self.g
        return (
            send(g.at[0, :, 1 - p.x, p.c], self.r1.at[0], self.sems, 0, p.along_x),
            send(g.at[1, 1 - p.y, :, p.c], self.r1.at[1], self.sems, 1, p.along_y),
        )

    def first_start(self):
        for copy in self.first_copies():
            copy.start()

    def first_sum(self):
        p, g = self.p, self.g
        for copy in self.first_copies():
            copy.wait()
        for i in range(2):
            g[0, i, p.x, p.c] = g[0, i, p.x, p.c] + self.r1[0, i]
            g[1, p.y, i, p.c] = g[1, p.y, i, p.c] + self.r1[1, i]

    def second_copies(self):
        p, g = self.p, self.g
        return (
            send(g.at[0, 1 - p.y, p.x, p.c], self.r2.at[0], self.sems, 2, p.along_y),
            send(g.at[1, p.y, 1 - p.x, p.c], self.r2.at[1], self.sems, 3, p.along_x),
        )

    def second_start(self):
        for copy in self.second_copies():
            copy.start()

    def second_sum(self):
        p, g = self.p, self.g
        for copy in self.second_copies():
            copy.wait()
        for h in range(2):
            g[h, p.y, p.x, p.c] = g[h, p.y, p.x, p.c] + self.r2[h]

    def third_copy(self):
        p, g = self.p, self.g
        return send(g.at[:, p.y, p.x, p.c, :, 1 - p.zl], self.rz1, self.sems, 4, p.z_near)

    def third_start(self):
        self.third_copy().start()

    def third_sum(self):
        p, g = self.p, self.g
        self.third_copy().wait()
        for h in range(2):
            for i in range(2):
                mine = (h, p.y, p.x, p.c, i, p.zl)
                g[mine] = g[mine] + self.rz1[h, i]

    def fourth_copy(self):
        p, g = self.p, self.g
        return send(g.at[:, p.y, p.x, p.c, 1 - p.zh, p.zl], self.rz2, self.sems, 5, p.z_far)

    def fourth_start(self):
        self.fourth_copy().start()

    def fourth_sum(self, out):
        p, g = self.p, self.g
        self.fourth_copy().wait()
        for h in range(2):
            mine = (h, p.y, p.x, p.c, p.zh, p.zl)
            out[h] = g[mine].astype(F32) + self.rz2[h].astype(F32)


def norm_stats(v):
    mean = jnp.mean(v, axis=-1, keepdims=True)
    centred = v - mean
    inverse = lax.rsqrt(jnp.mean(centred * centred, axis=-1, keepdims=True) + EPSILON)
    return mean, inverse


def norm_back(t, gain, n, inverse):
    u = t * gain
    return inverse * (
        u - jnp.mean(u, axis=-1, keepdims=True) - n * jnp.mean(u * n, axis=-1, keepdims=True)
    )


def column_sum(v):
    return jnp.sum(v, axis=0, keepdims=True)


def layer_kernel(names, *refs):
    r = types.SimpleNamespace(**dict(zip(names, refs)))
    p = Place()
    T, D = r.tokens.shape
    U = HEADS // 4
    HF = U * HEAD

    barrier = pltpu.get_barrier_semaphore()
    partners = [p.core, p.along_x, p.along_y] + [p.around(k) for k in (1, 2, 3)]
    for partner in partners:
        pl.semaphore_signal(barrier, inc=1, device_id=partner, device_id_type=MESH)

    pool = r.pool
    load_sems = r.load_sems

    def load(src, dst, index):
        copy = pltpu.make_async_copy(src, dst, load_sems.at[index])
        copy.start()
        return copy

    tokens_load = load(r.tokens, r.tok, 0)
    qkv_loads = [
        load(r.qkv_weight.at[:, pl.ds(i * D, D)], pool.at[1 + i], 1 + i) for i in range(3)
    ]
    cot_load = load(r.cotangent, r.cot, 4)
    out_load = load(r.out_weight, pool.at[0], 5)

    gid = r.group_ids[0]
    length = r.lengths[0]
    table = r.group_table[...]
    group_rows = lax.broadcasted_iota(jnp.int32, table.shape, 0)
    table_row = jnp.sum(jnp.where(group_rows == gid, table, 0.0), axis=0, keepdims=True)
    tokens_load.wait()
    start = r.tok[...].astype(F32) + table_row
    r.start[...] = start
    mean, inverse = norm_stats(start)
    norm_one = ((start - mean) * inverse * r.first_gain[...] + r.first_shift[...]).astype(BF)
    r.norm_oneT[...] = norm_one.T
    mix = r.mix
    qv_bias = r.qv_bias
    for i in range(3):
        qkv_loads[i].wait()
        rows = dot(norm_one, pool[1 + i])
        if i != 1:
            rows = rows + qv_bias[pl.ds(i // 2, 1), :]
        mix[i] = rows.astype(BF).T
    up_loads = [
        load(r.up_weight.at[:, pl.ds(i * D, D)], pool.at[1 + i], 6 + i) for i in range(4)
    ]
    down_loads = [
        load(r.down_weight.at[pl.ds(i * D, D), :], pool.at[5 + i], 10 + i) for i in range(4)
    ]

    pl.semaphore_wait(barrier, len(partners))

    qkv = r.qkv

    def unit_rows(s, u):
        return pl.ds(pl.multiple_of((s * U + u) * HEAD, HEAD), HEAD)

    def qkv_copy(k, u):
        to = p.around(k)
        return send(
            mix.at[:, unit_rows(to[1], u), :], qkv.at[u, p.z], r.qkv_sems, u * 3 + k - 1, to
        )

    for u in range(U):
        for k in (1, 2, 3):
            qkv_copy(k, u).start()
    own_qkv = []
    for u in range(U):
        copy = pltpu.make_async_copy(
            mix.at[:, unit_rows(p.z, u), :], qkv.at[u, p.z], r.own_sems.at[u]
        )
        copy.start()
        own_qkv.append(copy)

    cot_load.wait()
    cot = r.cot[...]
    r.cotT[...] = cot.T

    key_iota = lax.broadcasted_iota(jnp.int32, (T, T), 0)
    query_iota = lax.broadcasted_iota(jnp.int32, (T, T), 1)
    scale2 = HEAD**-0.5 * LOG2E

    def masked(u, i, j):
        scores = dot_tn(qkv[u, j, 1], qkv[u, i, 0]) * scale2
        allowed = key_iota < length - j * T
        if i == j:
            allowed = allowed & (key_iota <= query_iota)
        return jnp.where(allowed, scores, NEG_LARGE)

    attT, outT, out_low, lse = r.attT, r.outT, r.out_low, r.lse

    def att_copy(k, u):
        to = p.around(k)
        return send(
            out_low.at[u, to[1]],
            attT.at[unit_rows(p.z, u), :],
            r.att_sems,
            u * 3 + k - 1,
            to,
        )

    own_att = []
    for u in range(U):
        own_qkv[u].wait()
        for k in (1, 2, 3):
            qkv_copy(k, u).wait()
        for i in range(4):
            blocks = [masked(u, i, j) for j in range(i + 1)]
            top = functools.reduce(
                jnp.maximum, [jnp.max(b, axis=0, keepdims=True) for b in blocks]
            )
            weights = [jnp.exp2(b - top) for b in blocks]
            total = sum(jnp.sum(w, axis=0, keepdims=True) for w in weights)
            acc = sum(dot(qkv[u, j, 2], weights[j].astype(BF)) for j in range(i + 1))
            value = acc * (1.0 / total)
            outT[u, i] = value
            out_low[u, i] = value.astype(BF)
            lse[u, i] = top + jnp.log2(total)
        for k in (1, 2, 3):
            att_copy(k, u).start()
        copy = pltpu.make_async_copy(
            out_low.at[u, p.z], attT.at[unit_rows(p.z, u), :], r.own_sems.at[U + u]
        )
        copy.start()
        own_att.append(copy)
    for u in range(U):
        own_att[u].wait()
        for k in (1, 2, 3):
            att_copy(k, u).wait()

    out_load.wait()
    after = start_of(r) + dot(attT[...].T, pool[0]) + r.out_bias[...]
    r.after[...] = after
    mean, inverse = norm_stats(after)
    norm_two = ((after - mean) * inverse * r.second_gain[...] + r.second_shift[...]).astype(BF)
    r.norm_two[...] = norm_two
    r.norm_twoT[...] = norm_two.T
    r.total[...] = after + r.down_bias[...]
    r.t[...] = jnp.zeros((T, D), F32)
    for copy in up_loads + down_loads:
        copy.wait()

    g_down, g_up, g_out, g_qkv = r.g_down, r.g_up, r.g_out, r.g_qkv

    def scatter(name, parts):
        return ReduceScatter(
            p,
            getattr(r, "g_" + name),
            getattr(r, "rc_" + name),
            getattr(r, "r1_" + name),
            getattr(r, "r2_" + name),
            getattr(r, "rz1_" + name),
            getattr(r, "rz2_" + name),
            getattr(r, "cs_" + name),
            getattr(r, "ss_" + name),
            parts,
        )

    down = scatter("down", "yx")
    up = scatter("up", "z")
    out = scatter("out", "")
    proj = scatter("qkv", "")
    small = r.small
    gelu_c = math.sqrt(2.0 / math.pi)

    def chunk(k, _):
        kh, kl = k // 2, lax.rem(k, 2)
        weight = pool[1 + k]
        weight_down = pool[5 + k]
        hidden = dot(r.norm_two[...], weight) + r.up_bias[pl.ds(k, 1), :]
        act_grad = dot_nt(r.cot[...], weight_down)
        square = hidden * hidden
        th = jnp.tanh(gelu_c * hidden * (1.0 + 0.044715 * square))
        half = 0.5 + 0.5 * th
        act = (hidden * half).astype(BF)
        slope = half + 0.5 * hidden * (1.0 - th * th) * gelu_c * (1.0 + 3 * 0.044715 * square)
        grad = act_grad * slope
        small[pl.ds(24 + k, 1), :] = column_sum(grad)
        low = grad.astype(BF)
        r.total[...] += dot(act, weight_down)
        r.t[...] += dot_nt(low, weight)
        piece = D // 2
        for cc in range(2):
            rows = dot(r.cotT[...], act[:, cc * piece : (cc + 1) * piece]).astype(BF)
            part = D // 4
            for z in range(4):
                for h in range(2):
                    at = z * part + h * (part // 2)
                    g_down[h, kh, kl, cc, z // 2, z % 2] = rows[at : at + part // 2]
        down.core_start(k)
        rows = dot(r.norm_twoT[...], low).astype(BF)
        part = D // 8
        for d in range(8):
            for h in range(2):
                at = d * part + h * (part // 2)
                g_up[h, d // 4, (d // 2) % 2, d % 2, kh, kl] = rows[at : at + part // 2]
        up.core_start(k)
        return 0

    lax.fori_loop(0, 4, chunk, 0)

    qkv_loads = [
        load(r.qkv_weight.at[:, pl.ds(i * D, D)], pool.at[1 + i], 14 + i) for i in range(3)
    ]

    r.result[...] = r.total[...].astype(BF)
    cot = r.cot[...].astype(F32)
    after = r.after[...]
    mean, inverse = norm_stats(after)
    n = (after - mean) * inverse
    t = r.t[...]
    after_grad = cot + norm_back(t, r.second_gain[...], n, inverse)
    r.after_grad[...] = after_grad
    after_low = after_grad.astype(BF)
    doT, dor = r.doT, r.dor
    doT[...] = dot_nt(pool[0], after_low).astype(BF)

    def do_copy(k):
        to = p.around(k)
        rows = pl.ds(pl.multiple_of(to[1] * HF, HF), HF)
        return send(doT.at[rows, :], dor.at[p.z], r.do_sems, k - 1, to)

    for k in (1, 2, 3):
        do_copy(k).start()
    own_do = pltpu.make_async_copy(
        doT.at[pl.ds(pl.multiple_of(p.z * HF, HF), HF), :], dor.at[p.z], r.own_sems.at[2 * U]
    )
    own_do.start()
    small[pl.ds(20, 1), :] = column_sum(after_grad)
    small[pl.ds(21, 1), :] = column_sum(t * n)
    small[pl.ds(22, 1), :] = column_sum(t)
    small[pl.ds(23, 1), :] = column_sum(cot)
    after_lowT = after_low.T
    part = D // 8
    for z in range(4):
        rows = dot_nt(attT[...], after_lowT[z * (D // 4) : (z + 1) * (D // 4)]).astype(BF)
        for d in range(8):
            for h in range(2):
                at = d * part + h * (part // 2)
                g_out[h, d // 4, (d // 2) % 2, d % 2, z // 2, z % 2] = rows[at : at + part // 2]
    out.core_start(0)

    down.core_sum()
    down.first_start()
    up.core_sum()
    up.first_start()
    out.core_sum()
    out.first_start()

    own_do.wait()
    for k in (1, 2, 3):
        do_copy(k).wait()
    mgT = r.mgT

    def back_copy(k, u):
        to = p.around(k)
        return send(
            mix.at[:, unit_rows(to[1], u), :],
            mgT.at[:, unit_rows(p.z, u), :],
            r.back_sems,
            u * 3 + k - 1,
            to,
        )

    own_back = []
    for u in range(U):
        key_grads = [jnp.zeros((HEAD, T), F32) for _ in range(4)]
        value_grads = [jnp.zeros((HEAD, T), F32) for _ in range(4)]
        for i in range(4):
            do_i = dor[i, u * HEAD : (u + 1) * HEAD]
            delta = column_sum(do_i.astype(F32) * outT[u, i])
            lse_i = lse[u, i]
            query_grad = jnp.zeros((HEAD, T), F32)
            for j in range(i + 1):
                probs = jnp.exp2(masked(u, i, j) - lse_i)
                prob_grad = dot_tn(qkv[u, j, 2], do_i)
                score_grad = (probs * (prob_grad - delta)).astype(BF)
                query_grad += dot(qkv[u, j, 1], score_grad)
                key_grads[j] += dot_nt(qkv[u, i, 0], score_grad)
                value_grads[j] += dot_nt(do_i, probs.astype(BF))
            mix[0, (i * U + u) * HEAD : (i * U + u + 1) * HEAD] = (query_grad * HEAD**-0.5).astype(BF)
        for j in range(4):
            rows = slice((j * U + u) * HEAD, (j * U + u + 1) * HEAD)
            mix[1, rows] = (key_grads[j] * HEAD**-0.5).astype(BF)
            mix[2, rows] = value_grads[j].astype(BF)
        for k in (1, 2, 3):
            back_copy(k, u).start()
        copy = pltpu.make_async_copy(
            mix.at[:, unit_rows(p.z, u), :],
            mgT.at[:, unit_rows(p.z, u), :],
            r.own_sems.at[2 * U + 1 + u],
        )
        copy.start()
        own_back.append(copy)
        if u == 1:
            down.first_sum()
            down.second_start()
    up.first_sum()
    up.second_start()
    out.first_sum()
    out.second_start()
    down.second_sum()
    down.third_start()
    up.second_sum()
    up.third_start()
    out.second_sum()
    out.third_start()

    for u in range(U):
        own_back[u].wait()
        for k in (1, 2, 3):
            back_copy(k, u).wait()

    share = 3 * D // 4
    part = D // 8
    for z in range(4):
        a, b = z * share // D, (z + 1) * share // D
        cut = (z + 1) * share - b * D
        pieces = [mgT[a, z * share - a * D : (D if b > a else cut)]]
        if b > a and cut > 0:
            pieces.append(mgT[b, 0:cut])
        pieces = pieces[0] if len(pieces) == 1 else jnp.concatenate(pieces, axis=0)
        rows = dot_nt(r.norm_oneT[...], pieces).astype(BF)
        for d in range(8):
            for h in range(2):
                at = d * part + h * (part // 2)
                g_qkv[h, d // 4, (d // 2) % 2, d % 2, z // 2, z % 2] = rows[at : at + part // 2]
    proj.core_start(0)
    for copy in qkv_loads:
        copy.wait()
    t1 = dot(pool[1], mgT[0]) + dot(pool[2], mgT[1]) + dot(pool[3], mgT[2])
    t1 = t1.T
    start = r.start[...]
    mean, inverse = norm_stats(start)
    n = (start - mean) * inverse
    start_grad = r.after_grad[...] + norm_back(t1, r.first_gain[...], n, inverse)
    r.grad_tokens[...] = start_grad.astype(BF)
    ones = jnp.ones((8, T), BF)
    small[pl.ds(0, 16), :] = jnp.where(group_rows == gid, column_sum(start_grad), 0.0)
    small[pl.ds(16, 1), :] = column_sum(t1 * n)
    small[pl.ds(17, 1), :] = column_sum(t1)
    small[pl.ds(18, 1), :] = dot_nt(ones, mgT[0])[0:1]
    small[pl.ds(19, 1), :] = dot_nt(ones, mgT[2])[0:1]

    small_in, small_sems = r.small_in, r.small_sems
    small_to = [p.core, p.along_x, p.along_y, p.z_near, p.z_far]

    def small_copy(step):
        return send(small, small_in.at[step], small_sems, step, small_to[step])

    def small_sum(step):
        small_copy(step).wait()
        small[...] = small[...] + small_in[step]

    small_copy(0).start()
    proj.core_sum()
    proj.first_start()
    small_sum(0)
    small_copy(1).start()
    down.third_sum()
    down.fourth_start()
    up.third_sum()
    up.fourth_start()
    out.third_sum()
    out.fourth_start()
    small_sum(1)
    small_copy(2).start()
    proj.first_sum()
    proj.second_start()
    small_sum(2)
    small_copy(3).start()
    down.fourth_sum(r.s_down)
    up.fourth_sum(r.s_up)
    out.fourth_sum(r.s_out)
    proj.second_sum()
    proj.third_start()
    small_sum(3)
    small_copy(4).start()
    proj.third_sum()
    proj.fourth_start()
    small_sum(4)
    r.small_out[...] = small[...]
    proj.fourth_sum(r.s_qkv)


def start_of(r):
    return r.start[...]


def outputs_kernel(result, grad_tokens, small, s_qkv, s_out, s_up, s_down, *outs):
    (
        o_result,
        o_tokens,
        o_table,
        o_first_gain,
        o_first_shift,
        o_qkv,
        o_qv_bias,
        o_out,
        o_out_bias,
        o_second_gain,
        o_second_shift,
        o_up,
        o_up_bias,
        o_down,
        o_down_bias,
    ) = outs
    D = small.shape[1]
    o_result[...] = result[...].reshape(o_result.shape)
    o_tokens[...] = grad_tokens[...].reshape(o_tokens.shape)
    o_table[...] = small[0:16]
    o_qv_bias[...] = small[18:20]
    for ref, row in (
        (o_first_gain, 16),
        (o_first_shift, 17),
        (o_out_bias, 20),
        (o_second_gain, 21),
        (o_second_shift, 22),
        (o_down_bias, 23),
    ):
        ref[...] = small[row]
    for k in range(4):
        o_up_bias[pl.ds(k * D, D)] = small[24 + k]
    for ref, value in ((o_qkv, s_qkv), (o_out, s_out), (o_up, s_up)):
        half = value.shape[1]
        for h in range(2):
            ref[h * half : (h + 1) * half] = value[h]
    half = s_down.shape[1]
    o_down[...] = jnp.concatenate([s_down[0], s_down[1]], axis=0).T


def fused(
    tokens,
    group_ids,
    lengths,
    cotangent,
    group_table,
    first_gain,
    first_shift,
    qkv_weight,
    query_value_bias,
    out_weight,
    out_bias,
    second_gain,
    second_shift,
    up_weight,
    up_bias,
    down_weight,
    down_bias,
):
    _, T, D = tokens.shape
    F = up_weight.shape[1]
    U = HEADS // 4
    any_spec = pl.BlockSpec(memory_space=pl.ANY)
    vmem = pl.BlockSpec(memory_space=pltpu.VMEM)
    smem = pl.BlockSpec(memory_space=pltpu.SMEM)
    inputs = dict(
        tokens=(tokens.reshape(T, D), any_spec),
        group_ids=(group_ids, smem),
        lengths=(lengths, smem),
        cotangent=(cotangent.reshape(T, D), any_spec),
        group_table=(group_table, vmem),
        first_gain=(first_gain.reshape(1, D), vmem),
        first_shift=(first_shift.reshape(1, D), vmem),
        qkv_weight=(qkv_weight, any_spec),
        qv_bias=(query_value_bias, vmem),
        out_weight=(out_weight, any_spec),
        out_bias=(out_bias.reshape(1, D), vmem),
        second_gain=(second_gain.reshape(1, D), vmem),
        second_shift=(second_shift.reshape(1, D), vmem),
        up_weight=(up_weight, any_spec),
        up_bias=(up_bias.reshape(4, D), vmem),
        down_weight=(down_weight, any_spec),
        down_bias=(down_bias.reshape(1, D), vmem),
    )
    shares = dict(
        down=(D // 8, F // 8),
        up=(D // 16, F // 4),
        out=(D // 16, D // 4),
        qkv=(D // 16, 3 * D // 4),
    )
    outputs = dict(
        result=((T, D), BF),
        grad_tokens=((T, D), BF),
        small_out=((28, D), F32),
    )
    outputs.update({"s_" + k: ((2,) + shares[k], F32) for k in ("qkv", "out", "up", "down")})
    dma = pltpu.SemaphoreType.DMA
    scratch = dict(
        pool=pltpu.VMEM((9, D, D), BF),
        tok=pltpu.VMEM((T, D), BF),
        cot=pltpu.VMEM((T, D), BF),
        cotT=pltpu.VMEM((D, T), BF),
        start=pltpu.VMEM((T, D), F32),
        norm_oneT=pltpu.VMEM((D, T), BF),
        mix=pltpu.VMEM((3, D, T), BF),
        qkv=pltpu.VMEM((U, 4, 3, HEAD, T), BF),
        outT=pltpu.VMEM((U, 4, HEAD, T), F32),
        out_low=pltpu.VMEM((U, 4, HEAD, T), BF),
        lse=pltpu.VMEM((U, 4, 1, T), F32),
        attT=pltpu.VMEM((D, T), BF),
        after=pltpu.VMEM((T, D), F32),
        norm_two=pltpu.VMEM((T, D), BF),
        norm_twoT=pltpu.VMEM((D, T), BF),
        total=pltpu.VMEM((T, D), F32),
        t=pltpu.VMEM((T, D), F32),
        after_grad=pltpu.VMEM((T, D), F32),
        doT=pltpu.VMEM((D, T), BF),
        dor=pltpu.VMEM((4, U * HEAD, T), BF),
        mgT=pltpu.VMEM((3, D, T), BF),
        small=pltpu.VMEM((28, D), F32),
        small_in=pltpu.VMEM((5, 28, D), F32),
        load_sems=dma((17,)),
        own_sems=dma((3 * U + 1,)),
        qkv_sems=dma((2, 3 * U)),
        att_sems=dma((2, 3 * U)),
        do_sems=dma((2, 3)),
        back_sems=dma((2, 3 * U)),
        small_sems=dma((2, 5)),
    )
    for name, (rows, columns) in shares.items():
        extra = {
            "g_" + name: pltpu.VMEM((2, 2, 2, 2, 2, 2, rows, columns), BF),
            "rc_" + name: pltpu.VMEM((2, 2, 2, 2, 2, rows, columns), BF),
            "r1_" + name: pltpu.VMEM((2, 2, 2, 2, rows, columns), BF),
            "r2_" + name: pltpu.VMEM((2, 2, 2, rows, columns), BF),
            "rz1_" + name: pltpu.VMEM((2, 2, rows, columns), BF),
            "rz2_" + name: pltpu.VMEM((2, rows, columns), BF),
            "cs_" + name: dma((2, 4)),
            "ss_" + name: dma((2, 6)),
        }
        scratch.update(extra)
    names = list(inputs) + list(outputs) + list(scratch)
    done = pl.pallas_call(
        functools.partial(layer_kernel, names),
        name="layer",
        out_shape=[jax.ShapeDtypeStruct(*o) for o in outputs.values()],
        in_specs=[i[1] for i in inputs.values()],
        out_specs=[vmem] * len(outputs),
        scratch_shapes=list(scratch.values()),
        compiler_params=pltpu.CompilerParams(
            collective_id=0, has_side_effects=True, vmem_limit_bytes=VMEM_LIMIT
        ),
    )(*[i[0] for i in inputs.values()])
    shape = jax.ShapeDtypeStruct
    return pl.pallas_call(
        outputs_kernel,
        name="outputs",
        out_shape=[
            shape((1, T, D), BF),
            shape((1, T, D), BF),
            shape((16, D), F32),
            shape((D,), F32),
            shape((D,), F32),
            shape((D // 8, 3 * D // 4), F32),
            shape((2, D), F32),
            shape((D // 8, D // 4), F32),
            shape((D,), F32),
            shape((D,), F32),
            shape((D,), F32),
            shape((D // 8, F // 4), F32),
            shape((F,), F32),
            shape((F // 8, D // 4), F32),
            shape((D,), F32),
        ],
        in_specs=[vmem] * len(done),
        out_specs=[vmem] * 15,
    )(*done)


def shifted(array, axis, by):
    devices = lax.axis_size(axis)
    pairs = [(i, i + by) for i in range(devices) if 0 <= i + by < devices]
    return lax.ppermute(array, axis, pairs)


def as_sent(array):
    return jax.tree.map(lambda a: a.astype(jnp.bfloat16) if a.dtype == jnp.float32 else a, array)


def shifted_2(block, axis, distance):
    devices = range(lax.axis_size(axis))
    route = [((i - distance) % len(devices), i) for i in devices]
    return lax.ppermute(block, axis, route)


def layer_norm(inputs, norm_gain, norm_shift):
    average = jnp.mean(inputs, -1, keepdims=True)
    centred = inputs - average
    inverse = lax.rsqrt(jnp.mean(centred * centred, -1, keepdims=True) + EPSILON)
    return centred * inverse * norm_gain + norm_shift


def tanh_gelu(inputs):
    return jax.nn.gelu(inputs, approximate=True)


def keep_same(state_value):
    return state_value


def scores_of(queries, key_piece, key_start, query_start, lengths):
    sequences, block_len = (queries.shape[0], queries.shape[1])
    key_heads = key_piece.reshape(sequences, key_piece.shape[1], HEADS, HEAD)
    raw_scores = jnp.einsum(
        "gqhe,gkhe->ghqk", queries, key_heads, preferred_element_type=jnp.float32
    ) * HEAD ** (-0.5)
    key_pos = key_start + jnp.arange(key_piece.shape[1])
    query_pos = query_start + jnp.arange(block_len)
    allowed = (query_pos[:, None] >= key_pos[None, :])[None] & (
        key_pos[None, None, :] < lengths[:, None, None]
    )
    return (raw_scores, allowed[:, None])


def plain(
    tokens,
    group_ids,
    lengths,
    cotangent,
    group_table,
    first_gain,
    first_shift,
    qkv_weight,
    query_value_bias,
    out_weight,
    out_bias,
    second_gain,
    second_shift,
    up_weight,
    up_bias,
    down_weight,
    down_bias,
):
    sequences, block_len, features = tokens.shape
    token_rows = sequences * block_len
    seq_count = lax.axis_size("seq")
    seq_index = lax.axis_index("seq")
    query_start = seq_index * block_len
    score_scale = HEAD ** (-0.5)
    one_hot = (group_ids[:, None] == jnp.arange(group_table.shape[0])[None, :]).astype(jnp.float32)
    table_rows = jnp.dot(one_hot, group_table, precision=EXACT)
    start_rows = (tokens.astype(jnp.float32) + table_rows[:, None, :]).reshape(token_rows, features)
    norm_one, pull_one = jax.vjp(layer_norm, start_rows, first_gain, first_shift)
    norm_one_low = norm_one.astype(jnp.bfloat16)
    full_bias = jnp.concatenate(
        [query_value_bias[0], jnp.zeros((features,), jnp.float32), query_value_bias[1]]
    )
    mixed_rows = (
        jnp.dot(norm_one_low, qkv_weight, preferred_element_type=jnp.float32) + full_bias
    ).astype(jnp.bfloat16)
    mixed_rows = mixed_rows.reshape(sequences, block_len, 3 * features)
    queries = mixed_rows[:, :, :features].reshape(sequences, block_len, HEADS, HEAD)
    key_rows = mixed_rows[:, :, features : 2 * features]
    values = mixed_rows[:, :, 2 * features :]
    pieces = []
    current = (key_rows, values)
    for cycle_step in range(seq_count):
        if cycle_step > 0:
            current = shifted((current[0], current[1]), "seq", 1)
        anchor = (seq_index - cycle_step) % seq_count
        pieces.append((current[0], current[1], anchor * block_len, cycle_step <= seq_index))
    shape_rows = (sequences, HEADS, block_len)
    row_max = jnp.full(shape_rows, NEG_LARGE, jnp.float32)
    row_sum = jnp.zeros(shape_rows, jnp.float32)
    stored = []
    for key_piece, value_piece, key_start, active in pieces:

        def visit_block(state_pair, key_piece=key_piece, key_start=key_start):
            raw_scores, allowed = scores_of(queries, key_piece, key_start, query_start, lengths)
            masked_scores = jnp.where(allowed, raw_scores, NEG_LARGE)
            new_max = jnp.maximum(state_pair[0], jnp.max(masked_scores, -1))
            weights = jnp.where(allowed, jnp.exp(masked_scores - new_max[..., None]), 0.0)
            return (
                new_max,
                state_pair[1] * jnp.exp(state_pair[0] - new_max) + jnp.sum(weights, -1),
                masked_scores,
            )

        def pass_block(state_pair):
            return (
                state_pair[0],
                state_pair[1],
                jnp.full(shape_rows + (block_len,), NEG_LARGE, jnp.float32),
            )

        row_max, row_sum, masked_scores = lax.cond(
            active, visit_block, pass_block, (row_max, row_sum)
        )
        stored.append(masked_scores)
    log_sum = row_max + jnp.log(row_sum)
    attended = jnp.zeros((sequences, block_len, HEADS, HEAD), jnp.float32)
    for piece_data, masked_scores in zip(pieces, stored):

        def attend_block(total_out, value_piece=piece_data[1], masked_scores=masked_scores):
            probs = jnp.exp(masked_scores - log_sum[..., None]).astype(jnp.bfloat16)
            value_heads = value_piece.reshape(sequences, block_len, HEADS, HEAD)
            return total_out + jnp.einsum(
                "ghqk,gkhe->gqhe", probs, value_heads, preferred_element_type=jnp.float32
            )

        attended = lax.cond(piece_data[3], attend_block, keep_same, attended)
    attended_low = attended.reshape(token_rows, features).astype(jnp.bfloat16)
    after_attn = (
        start_rows
        + jnp.dot(attended_low, out_weight, preferred_element_type=jnp.float32)
        + out_bias
    )
    norm_two, pull_two = jax.vjp(layer_norm, after_attn, second_gain, second_shift)
    norm_two_low = norm_two.astype(jnp.bfloat16)
    up_rows = jnp.dot(norm_two_low, up_weight, preferred_element_type=jnp.float32) + up_bias
    activated, pull_gelu = jax.vjp(tanh_gelu, up_rows)
    activated_low = activated.astype(jnp.bfloat16)
    result_rows = (
        after_attn
        + jnp.dot(activated_low, down_weight, preferred_element_type=jnp.float32)
        + down_bias
    )
    result = result_rows.astype(jnp.bfloat16).reshape(tokens.shape)
    outer_low = cotangent.reshape(token_rows, features)
    outer_grad = outer_low.astype(jnp.float32)
    grad_down_weight = jnp.dot(activated_low.T, outer_low, preferred_element_type=jnp.float32)
    grad_down_bias = jnp.sum(outer_grad, 0)
    up_grad = pull_gelu(jnp.dot(outer_low, down_weight.T, preferred_element_type=jnp.float32))[0]
    grad_up_bias = jnp.sum(up_grad, 0)
    up_low = up_grad.astype(jnp.bfloat16)
    grad_up_weight = jnp.dot(norm_two_low.T, up_low, preferred_element_type=jnp.float32)
    part_after, grad_second_gain, grad_second_shift = pull_two(
        jnp.dot(up_low, up_weight.T, preferred_element_type=jnp.float32)
    )
    after_grad = outer_grad + part_after
    grad_out_bias = jnp.sum(after_grad, 0)
    after_low = after_grad.astype(jnp.bfloat16)
    grad_out_weight = jnp.dot(attended_low.T, after_low, preferred_element_type=jnp.float32)
    out_grad = jnp.dot(after_low, out_weight.T, preferred_element_type=jnp.float32).astype(
        jnp.bfloat16
    )
    out_grad = out_grad.reshape(sequences, block_len, HEADS, HEAD)
    delta = jnp.transpose(jnp.sum(out_grad.astype(jnp.float32) * attended, -1), (0, 2, 1))

    def back_block(query_grad, key_piece, value_piece, key_start):
        raw_scores, allowed = scores_of(queries, key_piece, key_start, query_start, lengths)
        probs = jnp.where(allowed, jnp.exp(raw_scores - log_sum[..., None]), 0.0)
        value_heads = value_piece.reshape(sequences, block_len, HEADS, HEAD)
        key_heads = key_piece.reshape(sequences, block_len, HEADS, HEAD)
        prob_grad = jnp.einsum(
            "gqhe,gkhe->ghqk", out_grad, value_heads, preferred_element_type=jnp.float32
        )
        score_grad = (probs * (prob_grad - delta[..., None])).astype(jnp.bfloat16)
        query_grad = (
            query_grad
            + jnp.einsum(
                "ghqk,gkhe->gqhe", score_grad, key_heads, preferred_element_type=jnp.float32
            )
            * score_scale
        )
        key_add = (
            jnp.einsum("ghqk,gqhe->gkhe", score_grad, queries, preferred_element_type=jnp.float32)
            * score_scale
        )
        value_add = jnp.einsum(
            "ghqk,gqhe->gkhe",
            probs.astype(jnp.bfloat16),
            out_grad,
            preferred_element_type=jnp.float32,
        )
        return (
            query_grad,
            key_add.reshape(sequences, block_len, features),
            value_add.reshape(sequences, block_len, features),
        )

    empty_rows = jnp.zeros((sequences, block_len, features), jnp.float32)

    def skip_back(query_grad):
        return (query_grad, empty_rows, empty_rows)

    query_grad = jnp.zeros((sequences, block_len, HEADS, HEAD), jnp.float32)
    carried = (empty_rows, empty_rows)
    for cycle_step in range(seq_count):
        piece_data = pieces[cycle_step]

        def visit_back(state_grad, piece_data=piece_data):
            return back_block(state_grad, piece_data[0], piece_data[1], piece_data[2])

        query_grad, key_add, value_add = lax.cond(piece_data[3], visit_back, skip_back, query_grad)
        carried = shifted_2(
            (as_sent(carried[0] + key_add), as_sent(carried[1] + value_add)), "seq", 1
        )
    key_grad, value_grad = carried
    query_flat = query_grad.reshape(token_rows, features)
    key_flat = key_grad.reshape(token_rows, features)
    value_flat = value_grad.reshape(token_rows, features)
    grad_query_value_bias = jnp.stack([jnp.sum(query_flat, 0), jnp.sum(value_flat, 0)])
    mixed_grad = jnp.concatenate([query_flat, key_flat, value_flat], -1).astype(jnp.bfloat16)
    grad_qkv_weight = jnp.dot(norm_one_low.T, mixed_grad, preferred_element_type=jnp.float32)
    part_start, grad_first_gain, grad_first_shift = pull_one(
        jnp.dot(mixed_grad, qkv_weight.T, preferred_element_type=jnp.float32)
    )
    start_grad = after_grad + part_start
    grad_tokens = start_grad.astype(jnp.bfloat16).reshape(tokens.shape)
    grad_group_table = jnp.dot(
        one_hot.T, jnp.sum(start_grad.reshape(sequences, block_len, features), 1), precision=EXACT
    )
    small_sums = lax.psum(
        (
            grad_group_table,
            grad_first_gain,
            grad_first_shift,
            grad_query_value_bias,
            grad_out_bias,
            grad_second_gain,
            grad_second_shift,
            grad_up_bias,
            grad_down_bias,
        ),
        ("dp", "seq"),
    )
    matrices = (grad_qkv_weight, grad_out_weight, grad_up_weight, grad_down_weight)
    shares = (
        lax.psum_scatter(
            matrices[0].astype(jnp.bfloat16), "seq", scatter_dimension=1, tiled=True
        ).astype(jnp.float32),
        lax.psum_scatter(
            matrices[1].astype(jnp.bfloat16), "seq", scatter_dimension=1, tiled=True
        ).astype(jnp.float32),
        lax.psum_scatter(
            matrices[2].astype(jnp.bfloat16), "seq", scatter_dimension=1, tiled=True
        ).astype(jnp.float32),
        lax.psum_scatter(
            matrices[3].astype(jnp.bfloat16), "seq", scatter_dimension=1, tiled=True
        ).astype(jnp.float32),
    )
    shares = (
        lax.psum_scatter(
            shares[0].astype(jnp.bfloat16), "dp", scatter_dimension=0, tiled=True
        ).astype(jnp.float32),
        lax.psum_scatter(
            shares[1].astype(jnp.bfloat16), "dp", scatter_dimension=0, tiled=True
        ).astype(jnp.float32),
        lax.psum_scatter(
            shares[2].astype(jnp.bfloat16), "dp", scatter_dimension=0, tiled=True
        ).astype(jnp.float32),
        lax.psum_scatter(
            shares[3].astype(jnp.bfloat16), "dp", scatter_dimension=0, tiled=True
        ).astype(jnp.float32),
    )
    return (
        result,
        grad_tokens,
        small_sums[0],
        small_sums[1],
        small_sums[2],
        shares[0],
        small_sums[3],
        shares[1],
        small_sums[4],
        small_sums[5],
        small_sums[6],
        shares[2],
        small_sums[7],
        shares[3],
        small_sums[8],
    )


def solution(mesh):
    in_specs = (
        P("dp", "seq", None),
        P("dp"),
        P("dp"),
        P("dp", "seq", None),
        P(),
        P(),
        P(),
        P(),
        P(),
        P(),
        P(),
        P(),
        P(),
        P(),
        P(),
        P(),
        P(),
    )
    out_specs = (
        P("dp", "seq", None),
        P("dp", "seq", None),
        P(),
        P(),
        P(),
        P("dp", "seq"),
        P(),
        P("dp", "seq"),
        P(),
        P(),
        P(),
        P("dp", "seq"),
        P(),
        P("dp", "seq"),
        P(),
    )
    def shards(*arrays):
        sizes = (mesh.shape["dp"], mesh.shape["seq"]) + arrays[0].shape
        return (fused if sizes == (8, 4, 1, 256, 768) else plain)(*arrays)

    return jax.shard_map(shards, mesh=mesh, in_specs=in_specs, out_specs=out_specs, check_vma=False)
```

```python
import functools
import math
import types

import jax
import jax.numpy as jnp
from jax import lax
from jax.experimental import pallas as pl
from jax.experimental.pallas import tpu as pltpu
from jax.sharding import PartitionSpec as P

HEADS = 12
HEAD = 64


EPSILON = 1e-05
NEG_LARGE = -1e30
EXACT = lax.Precision.HIGHEST


VMEM_LIMIT = 64 << 20
GROUP = 6


BF = jnp.bfloat16
F32 = jnp.float32
MESH = pl.DeviceIdType.MESH
LOG2E = 1.4426950408889634


def dot(a, b):
    return lax.dot_general(a, b, (((1,), (0,)), ((), ())), preferred_element_type=F32)


def dot_nt(a, b):
    return lax.dot_general(a, b, (((1,), (1,)), ((), ())), preferred_element_type=F32)


def dot_tn(a, b):
    return lax.dot_general(a, b, (((0,), (0,)), ((), ())), preferred_element_type=F32)


def flipped(index, bit):
    return index + bit - 2 * bit * lax.rem(index // bit, 2)


class Place:
    def __init__(self):
        self.d = lax.axis_index("dp")
        self.z = lax.axis_index("seq")
        self.c = lax.rem(self.d, 2)
        self.x = lax.rem(self.d // 2, 2)
        self.y = lax.rem(self.d // 4, 2)
        self.zl = lax.rem(self.z, 2)
        self.zh = lax.rem(self.z // 2, 2)
        self.core = (flipped(self.d, 1), self.z)
        self.along_x = (flipped(self.d, 2), self.z)
        self.along_y = (flipped(self.d, 4), self.z)
        self.z_near = (self.d, flipped(self.z, 1))
        self.z_far = (self.d, flipped(self.z, 2))
        self.z_mirror = (self.d, 3 - self.z)

    def along_z(self, k):
        return (self.d, self.z + k)


def send(src, dst, sems, index, to):
    copy = pltpu.make_async_remote_copy(
        src_ref=src,
        dst_ref=dst,
        send_sem=sems.at[0, index],
        recv_sem=sems.at[1, index],
        device_id=to,
        device_id_type=MESH,
    )
    return copy


class ReduceScatter:
    def __init__(self, place, g, rc, r1, r2, rz1, rz2, core_sems, sems, parts):
        self.p, self.g, self.rc, self.r1, self.r2 = place, g, rc, r1, r2
        self.rz1, self.rz2, self.core_sems, self.sems, self.parts = rz1, rz2, core_sems, sems, parts
        self.count = 4 if parts else 1

    def core_copy(self, k):
        p = self.p
        kh, kl = k // 2, lax.rem(k, 2)
        if self.parts == "yx":
            src, dst = self.g.at[:, kh, kl, 1 - p.c], self.rc.at[:, kh, kl]
        elif self.parts == "z":
            src, dst = self.g.at[:, :, :, 1 - p.c, kh, kl], self.rc.at[:, :, :, kh, kl]
        else:
            src, dst = self.g.at[:, :, :, 1 - p.c], self.rc
        return send(src, dst, self.core_sems, k, p.core)

    def core_start(self, k):
        self.core_copy(k).start()

    def core_sum(self, k):
        p, g, rc = self.p, self.g, self.rc
        kh, kl = k // 2, lax.rem(k, 2)
        self.core_copy(k).wait()
        if self.parts == "yx":
            for h in range(2):
                g[h, kh, kl, p.c] = g[h, kh, kl, p.c] + rc[h, kh, kl]
            return

        def add(i, _):
            h, y, x = i // 4, lax.rem(i // 2, 2), lax.rem(i, 2)
            if self.parts == "z":
                g[h, y, x, p.c, kh, kl] = g[h, y, x, p.c, kh, kl] + rc[h, y, x, kh, kl]
            else:
                g[h, y, x, p.c] = g[h, y, x, p.c] + rc[h, y, x]
            return 0

        lax.fori_loop(0, 8, add, 0)

    def first_x(self, k):
        p, g, r1 = self.p, self.g, self.r1
        kh, kl = k // 2, lax.rem(k, 2)
        if self.parts == "yx":
            return send(g.at[0, kh, 1 - p.x, p.c], r1.at[0, kh], self.sems, kh, p.along_x)
        if self.parts == "z":
            return send(
                g.at[0, :, 1 - p.x, p.c, kh, kl], r1.at[0, :, kh, kl], self.sems, k, p.along_x
            )
        return send(g.at[0, :, 1 - p.x, p.c], r1.at[0], self.sems, 0, p.along_x)

    def first_y(self, k):
        p, g, r1 = self.p, self.g, self.r1
        kh, kl = k // 2, lax.rem(k, 2)
        if self.parts == "yx":
            return send(g.at[1, 1 - p.y, kl, p.c], r1.at[1, kl], self.sems, 4 + kl, p.along_y)
        if self.parts == "z":
            return send(
                g.at[1, 1 - p.y, :, p.c, kh, kl], r1.at[1, :, kh, kl], self.sems, 4 + k, p.along_y
            )
        return send(g.at[1, 1 - p.y, :, p.c], r1.at[1], self.sems, 4, p.along_y)

    def first_start(self, k):
        p = self.p
        if self.parts == "yx":
            pl.when(lax.rem(k, 2) != p.x)(lambda: self.first_x(k).start())
            pl.when(k // 2 != p.y)(lambda: self.first_y(k).start())
        else:
            self.first_x(k).start()
            self.first_y(k).start()

    def first_sum(self):
        p, g = self.p, self.g
        if self.parts == "yx":
            for i in range(2):
                self.first_x(2 * i).wait()
                self.first_y(i).wait()
        else:
            for k in range(self.count):
                self.first_x(k).wait()
                self.first_y(k).wait()
        for i in range(2):
            g[0, i, p.x, p.c] = g[0, i, p.x, p.c] + self.r1[0, i]
            g[1, p.y, i, p.c] = g[1, p.y, i, p.c] + self.r1[1, i]

    def second_copies(self):
        p, g = self.p, self.g
        return (
            send(g.at[0, 1 - p.y, p.x, p.c], self.r2.at[0], self.sems, 8, p.along_y),
            send(g.at[1, p.y, 1 - p.x, p.c], self.r2.at[1], self.sems, 9, p.along_x),
        )

    def second_start(self):
        for copy in self.second_copies():
            copy.start()

    def second_sum(self):
        p, g = self.p, self.g
        for copy in self.second_copies():
            copy.wait()
        for h in range(2):
            g[h, p.y, p.x, p.c] = g[h, p.y, p.x, p.c] + self.r2[h]

    def third_copy(self):
        p, g = self.p, self.g
        return send(g.at[:, p.y, p.x, p.c, :, 1 - p.zl], self.rz1, self.sems, 10, p.z_near)

    def third_start(self):
        self.third_copy().start()

    def third_sum(self):
        p, g = self.p, self.g
        self.third_copy().wait()
        for h in range(2):
            for i in range(2):
                mine = (h, p.y, p.x, p.c, i, p.zl)
                g[mine] = g[mine] + self.rz1[h, i]

    def fourth_copy(self):
        p, g = self.p, self.g
        return send(g.at[:, p.y, p.x, p.c, 1 - p.zh, p.zl], self.rz2, self.sems, 11, p.z_far)

    def fourth_start(self):
        self.fourth_copy().start()

    def fourth_sum(self, out):
        p, g = self.p, self.g
        self.fourth_copy().wait()
        for h in range(2):
            mine = (h, p.y, p.x, p.c, p.zh, p.zl)
            out[h] = g[mine].astype(F32) + self.rz2[h].astype(F32)


def norm_stats(v):
    mean = jnp.mean(v, axis=-1, keepdims=True)
    centred = v - mean
    inverse = lax.rsqrt(jnp.mean(centred * centred, axis=-1, keepdims=True) + EPSILON)
    return mean, inverse


def norm_back(t, gain, n, inverse):
    u = t * gain
    return inverse * (
        u - jnp.mean(u, axis=-1, keepdims=True) - n * jnp.mean(u * n, axis=-1, keepdims=True)
    )


def column_sum(v):
    return jnp.sum(v, axis=0, keepdims=True)


def layer_kernel(names, *refs):
    r = types.SimpleNamespace(**dict(zip(names, refs)))
    p = Place()
    T, D = r.tokens.shape

    barrier = pltpu.get_barrier_semaphore()
    partners = (p.core, p.along_x, p.along_y, p.z_near, p.z_far, p.z_mirror)
    for partner in partners:
        pl.semaphore_signal(barrier, inc=1, device_id=partner, device_id_type=MESH)

    pool = r.pool

    def load(src, dst, index):
        return pltpu.make_async_copy(src, dst, r.load_sems.at[index])

    def slot_of(k):
        return jnp.where(k == 2, 1, 4 + 2 * lax.rem(k, 3))

    def up_load(k):
        src = r.up_weight.at[:, pl.ds(pl.multiple_of(k * D, D), D)]
        return load(src, pool.at[slot_of(k)], 6 + k)

    def down_load(k):
        src = r.down_weight.at[pl.ds(pl.multiple_of(k * D, D), D), :]
        return load(src, pool.at[slot_of(k) + 1], 10 + k)

    tokens_load = load(r.tokens, r.tok, 0)
    tokens_load.start()
    qkv_loads = [
        load(r.qkv_weight.at[:, pl.ds(i * D, D)], pool.at[1 + i], 1 + i) for i in range(3)
    ]
    for i in (1, 2, 0):
        qkv_loads[i].start()
    cot_load = load(r.cotangent, r.cot, 4)
    out_load = load(r.out_weight, pool.at[0], 5)
    for copy in (cot_load, out_load, up_load(0), down_load(0), up_load(1), down_load(1)):
        copy.start()

    gid = r.group_ids[0]
    length = r.lengths[0]
    table = r.group_table[...]
    group_rows = lax.broadcasted_iota(jnp.int32, table.shape, 0)
    table_row = jnp.sum(jnp.where(group_rows == gid, table, 0.0), axis=0, keepdims=True)
    tokens_load.wait()
    start = r.tok[...].astype(F32) + table_row
    mean, inverse = norm_stats(start)
    nx, nxT = r.nx, r.nxT
    nx[0] = ((start - mean) * inverse * row_of(r.first_gain) + row_of(r.first_shift)).astype(BF)

    pl.semaphore_wait(barrier, len(partners))

    def nx_copy(s):
        return send(nx.at[s], nx.at[s + 1], r.nx_sems, s, p.along_z(1))

    def nx_wait(s):
        return send(nx.at[s - 1], nx.at[s], r.nx_sems, s - 1, p.along_z(-1)).wait_recv()

    kv, qT, outT, top, mass = r.kv, r.qT, r.outT, r.top, r.mass
    key_iota = lax.broadcasted_iota(jnp.int32, (T, T), 0)
    query_iota = lax.broadcasted_iota(jnp.int32, (T, T), 1)
    scale2 = HEAD**-0.5 * LOG2E

    def head_rows(h):
        return pl.ds(pl.multiple_of(h * HEAD, HEAD), HEAD)

    def masked(s, rows):
        scores = dot_tn(kv[s, 0, rows], qT[rows]) * scale2
        allowed = key_iota < length - (p.z - s) * T
        if s == 0:
            allowed = allowed & (key_iota <= query_iota)
        return jnp.where(allowed, scores, NEG_LARGE)

    def attend(s):
        def some_heads(g, _):
            heads = [g * GROUP + i for i in range(GROUP)]
            places = [head_rows(h) for h in heads]
            scores = [masked(s, rows) for rows in places]
            highest = [jnp.max(v, axis=0, keepdims=True) for v in scores]
            if s > 0:
                highest = [jnp.maximum(v, top[h]) for v, h in zip(highest, heads)]
                fade = [jnp.exp2(top[h] - v) for v, h in zip(highest, heads)]
            weights = [jnp.exp2(v - m) for v, m in zip(scores, highest)]
            total = [column_sum(v) for v in weights]
            value = [dot(kv[s, 1, rows], v.astype(BF)) for v, rows in zip(weights, places)]
            for i, (h, rows) in enumerate(zip(heads, places)):
                if s > 0:
                    total[i] = total[i] + mass[h] * fade[i]
                    value[i] = value[i] + outT[rows] * fade[i]
                top[h] = highest[i]
                mass[h] = total[i]
                outT[rows] = value[i]
            return 0

        lax.fori_loop(0, HEADS // GROUP, some_heads, 0)

    def forward_step(s):
        if s > 0:
            nx_wait(s)
        if s < 3:
            pl.when(p.z < 3)(lambda: nx_copy(s).start())
        block = nx[s]
        nxT[:, s * T : (s + 1) * T] = block.T
        if s == 0:
            qkv_loads[1].wait()
        kv[s, 0] = dot(block, pool[2]).astype(BF).T
        if s == 0:
            qkv_loads[2].wait()
        kv[s, 1] = (dot(block, pool[3]) + r.qv_bias[1:2]).astype(BF).T
        if s == 0:
            qkv_loads[0].wait()
            qT[...] = (dot(block, pool[1]) + r.qv_bias[0:1]).astype(BF).T
        attend(s)

    forward_step(0)
    cot_load.wait()
    r.cotT[...] = r.cot[...].T
    for k in range(4):
        r.up_rows[k : k + 1] = r.up_bias[k * D : (k + 1) * D].reshape(1, D)
    for s in (1, 2, 3):
        pl.when(p.z >= s)(functools.partial(forward_step, s))
    up_load(2).start()
    down_load(2).start()

    def finish(h, _):
        rows = head_rows(h)
        value = outT[rows] * (1.0 / mass[h])
        outT[rows] = value
        r.attT[rows] = value.astype(BF)
        top[h] = top[h] + jnp.log2(mass[h])
        return 0

    lax.fori_loop(0, HEADS, finish, 0, unroll=True)
    attT = r.attT

    out_load.wait()
    after = r.tok[...].astype(F32) + table_row + dot(attT[...].T, pool[0]) + row_of(r.out_bias)
    r.after[...] = after
    mean, inverse = norm_stats(after)
    norm_two = ((after - mean) * inverse * row_of(r.second_gain) + row_of(r.second_shift)).astype(BF)
    r.norm_two[...] = norm_two
    r.norm_twoT[...] = norm_two.T
    r.total[...] = after + row_of(r.down_bias)
    r.t[...] = jnp.zeros((T, D), F32)

    g_down, g_up, g_out, g_qkv = r.g_down, r.g_up, r.g_out, r.g_qkv

    def scatter(name, parts):
        return ReduceScatter(
            p,
            getattr(r, "g_" + name),
            getattr(r, "rc_" + name),
            getattr(r, "r1_" + name),
            getattr(r, "r2_" + name),
            getattr(r, "rz1_" + name),
            getattr(r, "rz2_" + name),
            getattr(r, "cs_" + name),
            getattr(r, "ss_" + name),
            parts,
        )

    down = scatter("down", "yx")
    up = scatter("up", "z")
    out = scatter("out", "")
    proj = scatter("qkv", "")
    small = r.small
    gelu_c = math.sqrt(2.0 / math.pi)

    def pass_on(k):
        down.core_sum(k)
        down.first_start(k)
        up.core_sum(k)
        up.first_start(k)

    def chunk(k, _):
        kh, kl = k // 2, lax.rem(k, 2)
        up_load(k).wait()
        down_load(k).wait()
        weight = pool[slot_of(k)]
        weight_down = pool[slot_of(k) + 1]
        hidden = dot(r.norm_two[...], weight) + r.up_rows[pl.ds(k, 1), :]
        act_grad = dot_nt(r.cot[...], weight_down)
        square = hidden * hidden
        th = jnp.tanh(gelu_c * hidden * (1.0 + 0.044715 * square))
        half = 0.5 + 0.5 * th
        act = (hidden * half).astype(BF)
        slope = half + 0.5 * hidden * (1.0 - th * th) * gelu_c * (1.0 + 3 * 0.044715 * square)
        grad = act_grad * slope
        small[pl.ds(24 + k, 1), :] = column_sum(grad)
        low = grad.astype(BF)
        piece = D // 2
        for cc in range(2):
            rows = dot(r.cotT[...], act[:, cc * piece : (cc + 1) * piece]).astype(BF)
            part = D // 4
            for z in range(4):
                for h in range(2):
                    at = z * part + h * (part // 2)
                    g_down[h, kh, kl, cc, z // 2, z % 2] = rows[at : at + part // 2]
        down.core_start(k)
        rows = dot(r.norm_twoT[...], low).astype(BF)
        part = D // 8
        for d in range(8):
            for h in range(2):
                at = d * part + h * (part // 2)
                g_up[h, d // 4, (d // 2) % 2, d % 2, kh, kl] = rows[at : at + part // 2]
        up.core_start(k)
        r.total[...] += dot(act, weight_down)
        r.t[...] += dot_nt(low, weight)

        def last_load():
            up_load(3).start()
            down_load(3).start()

        pl.when(k == 0)(last_load)
        pl.when(k > 0)(lambda: pass_on(k - 1))
        return 0

    lax.fori_loop(0, 4, chunk, 0)
    pass_on(3)

    qkv_loads = [
        load(r.qkv_weight.at[:, pl.ds(i * D, D)], pool.at[1 + i], 14 + i) for i in range(3)
    ]
    for copy in qkv_loads:
        copy.start()

    nx[3] = r.total[...].astype(BF)
    result_store = pltpu.make_async_copy(nx.at[3], r.result, r.load_sems.at[17])
    result_store.start()
    cot = r.cot[...].astype(F32)
    after = r.after[...]
    mean, inverse = norm_stats(after)
    n = (after - mean) * inverse
    t = r.t[...]
    after_grad = cot + norm_back(t, row_of(r.second_gain), n, inverse)
    r.after[...] = after_grad
    after_low = after_grad.astype(BF)
    doT = r.doT
    doT[...] = dot_nt(pool[0], after_low).astype(BF)
    small[pl.ds(20, 1), :] = column_sum(after_grad)
    small[pl.ds(21, 1), :] = column_sum(t * n)
    small[pl.ds(22, 1), :] = column_sum(t)
    small[pl.ds(23, 1), :] = column_sum(cot)
    after_lowT = after_low.T
    part = D // 8
    for z in range(4):
        rows = dot_nt(attT[...], after_lowT[z * (D // 4) : (z + 1) * (D // 4)]).astype(BF)
        for d in range(8):
            for h in range(2):
                at = d * part + h * (part // 2)
                g_out[h, d // 4, (d // 2) % 2, d % 2, z // 2, z % 2] = rows[at : at + part // 2]
    out.core_start(0)

    delta = r.delta
    for h in range(HEADS):
        rows = slice(h * HEAD, (h + 1) * HEAD)
        delta[h] = column_sum(doT[rows].astype(F32) * outT[rows])
    outT[...] = jnp.zeros((D, T), F32)
    mg = r.mg

    def attend_back(s):
        lanes = slice(s * T, (s + 1) * T)

        def some_heads(g, _):
            heads = [g * GROUP + i for i in range(GROUP)]
            places = [head_rows(h) for h in heads]
            scores = [masked(s, rows) for rows in places]
            prob_grad = [dot_tn(kv[s, 1, rows], doT[rows]) for rows in places]
            probs = [jnp.exp2(v - top[h]) for v, h in zip(scores, heads)]
            score_grad = [
                (v * (w - delta[h])).astype(BF) for v, w, h in zip(probs, prob_grad, heads)
            ]
            probs = [v.astype(BF) for v in probs]
            query_add = [dot(kv[s, 0, rows], v) for v, rows in zip(score_grad, places)]
            key_add = [dot_nt(qT[rows], v) for v, rows in zip(score_grad, places)]
            value_add = [dot_nt(doT[rows], v) for v, rows in zip(probs, places)]
            for i, rows in enumerate(places):
                outT[rows] = outT[rows] + query_add[i]
                mg[0, rows, lanes] = (key_add[i] * HEAD**-0.5).astype(BF)
                mg[1, rows, lanes] = value_add[i].astype(BF)
            return 0

        lax.fori_loop(0, HEADS // GROUP, some_heads, 0)

    def t1_of(s):
        lanes = slice(s * T, (s + 1) * T)
        return dot(pool[2], mg[0, :, lanes]) + dot(pool[3], mg[1, :, lanes])

    def t1_copy(s):
        return send(kv.at[s, 0], r.t1_in.at[s - 1], r.t1_sems, s - 1, p.along_z(-1))

    def t1_wait(s):
        send(kv.at[s + 1, 0], r.t1_in.at[s], r.t1_sems, s, p.along_z(1)).wait_recv()

    def back_step(s):
        attend_back(s)
        kv[s, 0] = t1_of(s).astype(BF)
        pl.when(p.z == 3)(lambda: t1_copy(s).start())

    def no_step(s):
        lanes = slice(s * T, (s + 1) * T)
        nxT[:, lanes] = jnp.zeros((D, T), BF)
        for i in range(2):
            mg[i, :, lanes] = jnp.zeros((D, T), BF)

    for copy in qkv_loads:
        copy.wait()
    for s in (3, 2, 1):
        pl.when(p.z >= s)(functools.partial(back_step, s))
        pl.when(p.z < s)(functools.partial(no_step, s))
        if s == 3:
            out.core_sum(0)
            out.first_start(0)
    attend_back(0)

    query_grad = outT[...] * HEAD**-0.5
    query_low = query_grad.astype(BF)
    share = 3 * D // 4
    part = D // 8
    for z in range(4):
        columns = []
        for i in range(3):
            low_at, high_at = max(z * share, i * D) - i * D, min((z + 1) * share, (i + 1) * D) - i * D
            if low_at >= high_at:
                continue
            if i == 0:
                columns.append(dot_nt(nxT[:, 0:T], query_low[low_at:high_at]))
            else:
                columns.append(dot_nt(nxT[...], mg[i - 1, low_at:high_at]))
        rows = (columns[0] if len(columns) == 1 else jnp.concatenate(columns, axis=1)).astype(BF)
        for d in range(8):
            for h in range(2):
                at = d * part + h * (part // 2)
                g_qkv[h, d // 4, (d // 2) % 2, d % 2, z // 2, z % 2] = rows[at : at + part // 2]
    proj.core_start(0)
    t1 = t1_of(0) + dot(pool[1], query_low)
    r.outT[...] = t1
    ones = jnp.ones((8, 4 * T), BF)
    small[pl.ds(18, 1), :] = dot_nt(ones[:, 0:T], query_low)[0:1]
    small[pl.ds(19, 1), :] = dot_nt(ones, mg[1])[0:1]

    down.first_sum()
    down.second_start()
    proj.core_sum(0)
    proj.first_start(0)

    def t1_pass(s):
        t1_wait(s)
        kv[s, 0] = kv[s, 0] + r.t1_in[s]
        t1_copy(s).start()

    pl.when(p.z == 2)(lambda: t1_pass(2))
    up.first_sum()
    up.second_start()
    out.first_sum()
    out.second_start()
    pl.when((p.z >= 1) & (p.z < 3))(lambda: t1_pass(1))
    down.second_sum()
    down.third_start()
    up.second_sum()
    up.third_start()

    def t1_last():
        t1_wait(0)
        outT[...] = outT[...] + r.t1_in[0].astype(F32)

    pl.when(p.z < 3)(t1_last)
    t1 = outT[...].T
    start = r.tok[...].astype(F32) + table_row
    mean, inverse = norm_stats(start)
    n = (start - mean) * inverse
    start_grad = r.after[...] + norm_back(t1, row_of(r.first_gain), n, inverse)
    r.norm_two[...] = start_grad.astype(BF)
    tokens_store = pltpu.make_async_copy(r.norm_two, r.grad_tokens, r.load_sems.at[18])
    tokens_store.start()
    small[pl.ds(0, 16), :] = jnp.where(group_rows == gid, column_sum(start_grad), 0.0)
    small[pl.ds(16, 1), :] = column_sum(t1 * n)
    small[pl.ds(17, 1), :] = column_sum(t1)

    small_in, small_sems = r.small_in, r.small_sems
    small_to = [p.core, p.along_x, p.along_y, p.z_near, p.z_far]

    def small_copy(step):
        return send(small, small_in.at[step], small_sems, step, small_to[step])

    def small_sum(step):
        small_copy(step).wait()
        small[...] = small[...] + small_in[step]

    small_copy(0).start()
    out.second_sum()
    out.third_start()
    down.third_sum()
    down.fourth_start()
    small_sum(0)
    small_copy(1).start()
    proj.first_sum()
    proj.second_start()
    up.third_sum()
    up.fourth_start()
    small_sum(1)
    small_copy(2).start()
    out.third_sum()
    out.fourth_start()
    small_sum(2)
    small_copy(3).start()
    proj.second_sum()
    proj.third_start()
    small_sum(3)
    small_copy(4).start()
    down.fourth_sum(r.s_down)
    up.fourth_sum(r.s_up)
    out.fourth_sum(r.s_out)
    proj.third_sum()
    proj.fourth_start()
    small_sum(4)
    r.small_out[...] = small[...]
    for s in (0, 1, 2):
        pl.when((p.z < 3) & (p.z >= s))(lambda s=s: nx_copy(s).wait_send())
    for s in (1, 2, 3):
        pl.when(p.z >= s)(lambda s=s: t1_copy(s).wait_send())
    result_store.wait()
    tokens_store.wait()
    proj.fourth_sum(r.s_qkv)


def row_of(ref):
    return ref[...].reshape(1, ref.shape[0])


def outputs_kernel(result, grad_tokens, small, s_qkv, s_out, s_up, s_down, *outs):
    (
        o_result,
        o_tokens,
        o_table,
        o_first_gain,
        o_first_shift,
        o_qkv,
        o_qv_bias,
        o_out,
        o_out_bias,
        o_second_gain,
        o_second_shift,
        o_up,
        o_up_bias,
        o_down,
        o_down_bias,
    ) = outs
    D = small.shape[1]
    o_result[...] = result[...].reshape(o_result.shape)
    o_tokens[...] = grad_tokens[...].reshape(o_tokens.shape)
    o_table[...] = small[0:16]
    o_qv_bias[...] = small[18:20]
    for ref, row in (
        (o_first_gain, 16),
        (o_first_shift, 17),
        (o_out_bias, 20),
        (o_second_gain, 21),
        (o_second_shift, 22),
        (o_down_bias, 23),
    ):
        ref[...] = small[row]
    for k in range(4):
        o_up_bias[pl.ds(k * D, D)] = small[24 + k]
    for ref, value in ((o_qkv, s_qkv), (o_out, s_out), (o_up, s_up), (o_down, s_down)):
        half = value.shape[1]
        for h in range(2):
            ref[h * half : (h + 1) * half] = value[h]


def fused(
    tokens,
    group_ids,
    lengths,
    cotangent,
    group_table,
    first_gain,
    first_shift,
    qkv_weight,
    query_value_bias,
    out_weight,
    out_bias,
    second_gain,
    second_shift,
    up_weight,
    up_bias,
    down_weight,
    down_bias,
):
    _, T, D = tokens.shape
    F = up_weight.shape[1]
    any_spec = pl.BlockSpec(memory_space=pl.ANY)
    vmem = pl.BlockSpec(memory_space=pltpu.VMEM)
    smem = pl.BlockSpec(memory_space=pltpu.SMEM)
    inputs = dict(
        tokens=(tokens.reshape(T, D), any_spec),
        group_ids=(group_ids, smem),
        lengths=(lengths, smem),
        cotangent=(cotangent.reshape(T, D), any_spec),
        group_table=(group_table, vmem),
        first_gain=(first_gain, vmem),
        first_shift=(first_shift, vmem),
        qkv_weight=(qkv_weight, any_spec),
        qv_bias=(query_value_bias, vmem),
        out_weight=(out_weight, any_spec),
        out_bias=(out_bias, vmem),
        second_gain=(second_gain, vmem),
        second_shift=(second_shift, vmem),
        up_weight=(up_weight, any_spec),
        up_bias=(up_bias, vmem),
        down_weight=(down_weight, any_spec),
        down_bias=(down_bias, vmem),
    )
    shares = dict(
        down=(D // 8, F // 8),
        up=(D // 16, F // 4),
        out=(D // 16, D // 4),
        qkv=(D // 16, 3 * D // 4),
    )
    outputs = dict(
        result=((T, D), BF),
        grad_tokens=((T, D), BF),
        small_out=((28, D), F32),
    )
    outputs.update({"s_" + k: ((2,) + shares[k], F32) for k in ("qkv", "out", "up", "down")})
    dma = pltpu.SemaphoreType.DMA
    scratch = dict(
        pool=pltpu.VMEM((8, D, D), BF),
        tok=pltpu.VMEM((T, D), BF),
        cot=pltpu.VMEM((T, D), BF),
        cotT=pltpu.VMEM((D, T), BF),
        nx=pltpu.VMEM((4, T, D), BF),
        nxT=pltpu.VMEM((D, 4 * T), BF),
        qT=pltpu.VMEM((D, T), BF),
        kv=pltpu.VMEM((4, 2, D, T), BF),
        outT=pltpu.VMEM((D, T), F32),
        top=pltpu.VMEM((HEADS, 1, T), F32),
        mass=pltpu.VMEM((HEADS, 1, T), F32),
        delta=pltpu.VMEM((HEADS, 1, T), F32),
        attT=pltpu.VMEM((D, T), BF),
        after=pltpu.VMEM((T, D), F32),
        norm_two=pltpu.VMEM((T, D), BF),
        norm_twoT=pltpu.VMEM((D, T), BF),
        total=pltpu.VMEM((T, D), F32),
        t=pltpu.VMEM((T, D), F32),
        doT=pltpu.VMEM((D, T), BF),
        mg=pltpu.VMEM((2, D, 4 * T), BF),
        t1_in=pltpu.VMEM((3, D, T), BF),
        up_rows=pltpu.VMEM((4, D), F32),
        small=pltpu.VMEM((28, D), F32),
        small_in=pltpu.VMEM((5, 28, D), F32),
        load_sems=dma((19,)),
        nx_sems=dma((2, 3)),
        t1_sems=dma((2, 3)),
        small_sems=dma((2, 5)),
    )
    for name, (rows, columns) in shares.items():
        extra = {
            "g_" + name: pltpu.VMEM((2, 2, 2, 2, 2, 2, rows, columns), BF),
            "rc_" + name: pltpu.VMEM((2, 2, 2, 2, 2, rows, columns), BF),
            "r1_" + name: pltpu.VMEM((2, 2, 2, 2, rows, columns), BF),
            "r2_" + name: pltpu.VMEM((2, 2, 2, rows, columns), BF),
            "rz1_" + name: pltpu.VMEM((2, 2, rows, columns), BF),
            "rz2_" + name: pltpu.VMEM((2, rows, columns), BF),
            "cs_" + name: dma((2, 4)),
            "ss_" + name: dma((2, 12)),
        }
        scratch.update(extra)
    names = list(inputs) + list(outputs) + list(scratch)
    done = pl.pallas_call(
        functools.partial(layer_kernel, names),
        name="layer",
        out_shape=[jax.ShapeDtypeStruct(*o) for o in outputs.values()],
        in_specs=[i[1] for i in inputs.values()],
        out_specs=[any_spec] * 2 + [vmem] * (len(outputs) - 2),
        scratch_shapes=list(scratch.values()),
        compiler_params=pltpu.CompilerParams(
            collective_id=0, has_side_effects=True, vmem_limit_bytes=VMEM_LIMIT
        ),
    )(*[i[0] for i in inputs.values()])
    shape = jax.ShapeDtypeStruct
    outs = pl.pallas_call(
        outputs_kernel,
        name="outputs",
        out_shape=[
            shape((1, T, D), BF),
            shape((1, T, D), BF),
            shape((16, D), F32),
            shape((D,), F32),
            shape((D,), F32),
            shape((D // 8, 3 * D // 4), F32),
            shape((2, D), F32),
            shape((D // 8, D // 4), F32),
            shape((D,), F32),
            shape((D,), F32),
            shape((D,), F32),
            shape((D // 8, F // 4), F32),
            shape((F,), F32),
            shape((D // 4, F // 8), F32),
            shape((D,), F32),
        ],
        in_specs=[vmem] * len(done),
        out_specs=[vmem] * 15,
    )(*done)
    return (*outs[:13], outs[13].T, outs[14])


def shifted(array, axis, by):
    devices = lax.axis_size(axis)
    pairs = [(i, i + by) for i in range(devices) if 0 <= i + by < devices]
    return lax.ppermute(array, axis, pairs)


def as_sent(array):
    return jax.tree.map(lambda a: a.astype(jnp.bfloat16) if a.dtype == jnp.float32 else a, array)


def shifted_2(block, axis, distance):
    devices = range(lax.axis_size(axis))
    route = [((i - distance) % len(devices), i) for i in devices]
    return lax.ppermute(block, axis, route)


def layer_norm(inputs, norm_gain, norm_shift):
    average = jnp.mean(inputs, -1, keepdims=True)
    centred = inputs - average
    inverse = lax.rsqrt(jnp.mean(centred * centred, -1, keepdims=True) + EPSILON)
    return centred * inverse * norm_gain + norm_shift


def tanh_gelu(inputs):
    return jax.nn.gelu(inputs, approximate=True)


def keep_same(state_value):
    return state_value


def scores_of(queries, key_piece, key_start, query_start, lengths):
    sequences, block_len = (queries.shape[0], queries.shape[1])
    key_heads = key_piece.reshape(sequences, key_piece.shape[1], HEADS, HEAD)
    raw_scores = jnp.einsum(
        "gqhe,gkhe->ghqk", queries, key_heads, preferred_element_type=jnp.float32
    ) * HEAD ** (-0.5)
    key_pos = key_start + jnp.arange(key_piece.shape[1])
    query_pos = query_start + jnp.arange(block_len)
    allowed = (query_pos[:, None] >= key_pos[None, :])[None] & (
        key_pos[None, None, :] < lengths[:, None, None]
    )
    return (raw_scores, allowed[:, None])


def plain(
    tokens,
    group_ids,
    lengths,
    cotangent,
    group_table,
    first_gain,
    first_shift,
    qkv_weight,
    query_value_bias,
    out_weight,
    out_bias,
    second_gain,
    second_shift,
    up_weight,
    up_bias,
    down_weight,
    down_bias,
):
    sequences, block_len, features = tokens.shape
    token_rows = sequences * block_len
    seq_count = lax.axis_size("seq")
    seq_index = lax.axis_index("seq")
    query_start = seq_index * block_len
    score_scale = HEAD ** (-0.5)
    one_hot = (group_ids[:, None] == jnp.arange(group_table.shape[0])[None, :]).astype(jnp.float32)
    table_rows = jnp.dot(one_hot, group_table, precision=EXACT)
    start_rows = (tokens.astype(jnp.float32) + table_rows[:, None, :]).reshape(token_rows, features)
    norm_one, pull_one = jax.vjp(layer_norm, start_rows, first_gain, first_shift)
    norm_one_low = norm_one.astype(jnp.bfloat16)
    full_bias = jnp.concatenate(
        [query_value_bias[0], jnp.zeros((features,), jnp.float32), query_value_bias[1]]
    )
    mixed_rows = (
        jnp.dot(norm_one_low, qkv_weight, preferred_element_type=jnp.float32) + full_bias
    ).astype(jnp.bfloat16)
    mixed_rows = mixed_rows.reshape(sequences, block_len, 3 * features)
    queries = mixed_rows[:, :, :features].reshape(sequences, block_len, HEADS, HEAD)
    key_rows = mixed_rows[:, :, features : 2 * features]
    values = mixed_rows[:, :, 2 * features :]
    pieces = []
    current = (key_rows, values)
    for cycle_step in range(seq_count):
        if cycle_step > 0:
            current = shifted((current[0], current[1]), "seq", 1)
        anchor = (seq_index - cycle_step) % seq_count
        pieces.append((current[0], current[1], anchor * block_len, cycle_step <= seq_index))
    shape_rows = (sequences, HEADS, block_len)
    row_max = jnp.full(shape_rows, NEG_LARGE, jnp.float32)
    row_sum = jnp.zeros(shape_rows, jnp.float32)
    stored = []
    for key_piece, value_piece, key_start, active in pieces:

        def visit_block(state_pair, key_piece=key_piece, key_start=key_start):
            raw_scores, allowed = scores_of(queries, key_piece, key_start, query_start, lengths)
            masked_scores = jnp.where(allowed, raw_scores, NEG_LARGE)
            new_max = jnp.maximum(state_pair[0], jnp.max(masked_scores, -1))
            weights = jnp.where(allowed, jnp.exp(masked_scores - new_max[..., None]), 0.0)
            return (
                new_max,
                state_pair[1] * jnp.exp(state_pair[0] - new_max) + jnp.sum(weights, -1),
                masked_scores,
            )

        def pass_block(state_pair):
            return (
                state_pair[0],
                state_pair[1],
                jnp.full(shape_rows + (block_len,), NEG_LARGE, jnp.float32),
            )

        row_max, row_sum, masked_scores = lax.cond(
            active, visit_block, pass_block, (row_max, row_sum)
        )
        stored.append(masked_scores)
    log_sum = row_max + jnp.log(row_sum)
    attended = jnp.zeros((sequences, block_len, HEADS, HEAD), jnp.float32)
    for piece_data, masked_scores in zip(pieces, stored):

        def attend_block(total_out, value_piece=piece_data[1], masked_scores=masked_scores):
            probs = jnp.exp(masked_scores - log_sum[..., None]).astype(jnp.bfloat16)
            value_heads = value_piece.reshape(sequences, block_len, HEADS, HEAD)
            return total_out + jnp.einsum(
                "ghqk,gkhe->gqhe", probs, value_heads, preferred_element_type=jnp.float32
            )

        attended = lax.cond(piece_data[3], attend_block, keep_same, attended)
    attended_low = attended.reshape(token_rows, features).astype(jnp.bfloat16)
    after_attn = (
        start_rows
        + jnp.dot(attended_low, out_weight, preferred_element_type=jnp.float32)
        + out_bias
    )
    norm_two, pull_two = jax.vjp(layer_norm, after_attn, second_gain, second_shift)
    norm_two_low = norm_two.astype(jnp.bfloat16)
    up_rows = jnp.dot(norm_two_low, up_weight, preferred_element_type=jnp.float32) + up_bias
    activated, pull_gelu = jax.vjp(tanh_gelu, up_rows)
    activated_low = activated.astype(jnp.bfloat16)
    result_rows = (
        after_attn
        + jnp.dot(activated_low, down_weight, preferred_element_type=jnp.float32)
        + down_bias
    )
    result = result_rows.astype(jnp.bfloat16).reshape(tokens.shape)
    outer_low = cotangent.reshape(token_rows, features)
    outer_grad = outer_low.astype(jnp.float32)
    grad_down_weight = jnp.dot(activated_low.T, outer_low, preferred_element_type=jnp.float32)
    grad_down_bias = jnp.sum(outer_grad, 0)
    up_grad = pull_gelu(jnp.dot(outer_low, down_weight.T, preferred_element_type=jnp.float32))[0]
    grad_up_bias = jnp.sum(up_grad, 0)
    up_low = up_grad.astype(jnp.bfloat16)
    grad_up_weight = jnp.dot(norm_two_low.T, up_low, preferred_element_type=jnp.float32)
    part_after, grad_second_gain, grad_second_shift = pull_two(
        jnp.dot(up_low, up_weight.T, preferred_element_type=jnp.float32)
    )
    after_grad = outer_grad + part_after
    grad_out_bias = jnp.sum(after_grad, 0)
    after_low = after_grad.astype(jnp.bfloat16)
    grad_out_weight = jnp.dot(attended_low.T, after_low, preferred_element_type=jnp.float32)
    out_grad = jnp.dot(after_low, out_weight.T, preferred_element_type=jnp.float32).astype(
        jnp.bfloat16
    )
    out_grad = out_grad.reshape(sequences, block_len, HEADS, HEAD)
    delta = jnp.transpose(jnp.sum(out_grad.astype(jnp.float32) * attended, -1), (0, 2, 1))

    def back_block(query_grad, key_piece, value_piece, key_start):
        raw_scores, allowed = scores_of(queries, key_piece, key_start, query_start, lengths)
        probs = jnp.where(allowed, jnp.exp(raw_scores - log_sum[..., None]), 0.0)
        value_heads = value_piece.reshape(sequences, block_len, HEADS, HEAD)
        key_heads = key_piece.reshape(sequences, block_len, HEADS, HEAD)
        prob_grad = jnp.einsum(
            "gqhe,gkhe->ghqk", out_grad, value_heads, preferred_element_type=jnp.float32
        )
        score_grad = (probs * (prob_grad - delta[..., None])).astype(jnp.bfloat16)
        query_grad = (
            query_grad
            + jnp.einsum(
                "ghqk,gkhe->gqhe", score_grad, key_heads, preferred_element_type=jnp.float32
            )
            * score_scale
        )
        key_add = (
            jnp.einsum("ghqk,gqhe->gkhe", score_grad, queries, preferred_element_type=jnp.float32)
            * score_scale
        )
        value_add = jnp.einsum(
            "ghqk,gqhe->gkhe",
            probs.astype(jnp.bfloat16),
            out_grad,
            preferred_element_type=jnp.float32,
        )
        return (
            query_grad,
            key_add.reshape(sequences, block_len, features),
            value_add.reshape(sequences, block_len, features),
        )

    empty_rows = jnp.zeros((sequences, block_len, features), jnp.float32)

    def skip_back(query_grad):
        return (query_grad, empty_rows, empty_rows)

    query_grad = jnp.zeros((sequences, block_len, HEADS, HEAD), jnp.float32)
    carried = (empty_rows, empty_rows)
    for cycle_step in range(seq_count):
        piece_data = pieces[cycle_step]

        def visit_back(state_grad, piece_data=piece_data):
            return back_block(state_grad, piece_data[0], piece_data[1], piece_data[2])

        query_grad, key_add, value_add = lax.cond(piece_data[3], visit_back, skip_back, query_grad)
        carried = shifted_2(
            (as_sent(carried[0] + key_add), as_sent(carried[1] + value_add)), "seq", 1
        )
    key_grad, value_grad = carried
    query_flat = query_grad.reshape(token_rows, features)
    key_flat = key_grad.reshape(token_rows, features)
    value_flat = value_grad.reshape(token_rows, features)
    grad_query_value_bias = jnp.stack([jnp.sum(query_flat, 0), jnp.sum(value_flat, 0)])
    mixed_grad = jnp.concatenate([query_flat, key_flat, value_flat], -1).astype(jnp.bfloat16)
    grad_qkv_weight = jnp.dot(norm_one_low.T, mixed_grad, preferred_element_type=jnp.float32)
    part_start, grad_first_gain, grad_first_shift = pull_one(
        jnp.dot(mixed_grad, qkv_weight.T, preferred_element_type=jnp.float32)
    )
    start_grad = after_grad + part_start
    grad_tokens = start_grad.astype(jnp.bfloat16).reshape(tokens.shape)
    grad_group_table = jnp.dot(
        one_hot.T, jnp.sum(start_grad.reshape(sequences, block_len, features), 1), precision=EXACT
    )
    small_sums = lax.psum(
        (
            grad_group_table,
            grad_first_gain,
            grad_first_shift,
            grad_query_value_bias,
            grad_out_bias,
            grad_second_gain,
            grad_second_shift,
            grad_up_bias,
            grad_down_bias,
        ),
        ("dp", "seq"),
    )
    matrices = (grad_qkv_weight, grad_out_weight, grad_up_weight, grad_down_weight)
    shares = (
        lax.psum_scatter(
            matrices[0].astype(jnp.bfloat16), "seq", scatter_dimension=1, tiled=True
        ).astype(jnp.float32),
        lax.psum_scatter(
            matrices[1].astype(jnp.bfloat16), "seq", scatter_dimension=1, tiled=True
        ).astype(jnp.float32),
        lax.psum_scatter(
            matrices[2].astype(jnp.bfloat16), "seq", scatter_dimension=1, tiled=True
        ).astype(jnp.float32),
        lax.psum_scatter(
            matrices[3].astype(jnp.bfloat16), "seq", scatter_dimension=1, tiled=True
        ).astype(jnp.float32),
    )
    shares = (
        lax.psum_scatter(
            shares[0].astype(jnp.bfloat16), "dp", scatter_dimension=0, tiled=True
        ).astype(jnp.float32),
        lax.psum_scatter(
            shares[1].astype(jnp.bfloat16), "dp", scatter_dimension=0, tiled=True
        ).astype(jnp.float32),
        lax.psum_scatter(
            shares[2].astype(jnp.bfloat16), "dp", scatter_dimension=0, tiled=True
        ).astype(jnp.float32),
        lax.psum_scatter(
            shares[3].astype(jnp.bfloat16), "dp", scatter_dimension=0, tiled=True
        ).astype(jnp.float32),
    )
    return (
        result,
        grad_tokens,
        small_sums[0],
        small_sums[1],
        small_sums[2],
        shares[0],
        small_sums[3],
        shares[1],
        small_sums[4],
        small_sums[5],
        small_sums[6],
        shares[2],
        small_sums[7],
        shares[3],
        small_sums[8],
    )


def solution(mesh):
    in_specs = (
        P("dp", "seq", None),
        P("dp"),
        P("dp"),
        P("dp", "seq", None),
        P(),
        P(),
        P(),
        P(),
        P(),
        P(),
        P(),
        P(),
        P(),
        P(),
        P(),
        P(),
        P(),
    )
    out_specs = (
        P("dp", "seq", None),
        P("dp", "seq", None),
        P(),
        P(),
        P(),
        P("dp", "seq"),
        P(),
        P("dp", "seq"),
        P(),
        P(),
        P(),
        P("dp", "seq"),
        P(),
        P("dp", "seq"),
        P(),
    )
    def shards(*arrays):
        sizes = (mesh.shape["dp"], mesh.shape["seq"]) + arrays[0].shape
        return (fused if sizes == (8, 4, 1, 256, 768) else plain)(*arrays)

    return jax.shard_map(shards, mesh=mesh, in_specs=in_specs, out_specs=out_specs, check_vma=False)
```

```python
import functools
import math
import types

import jax
import jax.numpy as jnp
from jax import lax
from jax.experimental import pallas as pl
from jax.experimental.pallas import tpu as pltpu
from jax.sharding import PartitionSpec as P

HEADS = 12
HEAD = 64


EPSILON = 1e-05
NEG_LARGE = -1e30
EXACT = lax.Precision.HIGHEST


VMEM_LIMIT = 64 << 20
GROUP = 6


BF = jnp.bfloat16
F32 = jnp.float32
MESH = pl.DeviceIdType.MESH
LOG2E = 1.4426950408889634


def dot(a, b):
    return lax.dot_general(a, b, (((1,), (0,)), ((), ())), preferred_element_type=F32)


def dot_nt(a, b):
    return lax.dot_general(a, b, (((1,), (1,)), ((), ())), preferred_element_type=F32)


def dot_tn(a, b):
    return lax.dot_general(a, b, (((0,), (0,)), ((), ())), preferred_element_type=F32)


def flipped(index, bit):
    return index + bit - 2 * bit * lax.rem(index // bit, 2)


class Place:
    def __init__(self):
        self.d = lax.axis_index("dp")
        self.z = lax.axis_index("seq")
        self.c = lax.rem(self.d, 2)
        self.x = lax.rem(self.d // 2, 2)
        self.y = lax.rem(self.d // 4, 2)
        self.zl = lax.rem(self.z, 2)
        self.zh = lax.rem(self.z // 2, 2)
        self.core = (flipped(self.d, 1), self.z)
        self.along_x = (flipped(self.d, 2), self.z)
        self.along_y = (flipped(self.d, 4), self.z)
        self.z_near = (self.d, flipped(self.z, 1))
        self.z_far = (self.d, flipped(self.z, 2))
        self.z_mirror = (self.d, 3 - self.z)
        self.diagonal = (flipped(flipped(self.d, 2), 4), self.z)

    def along_z(self, k):
        return (self.d, self.z + k)


def send(src, dst, sems, index, to):
    copy = pltpu.make_async_remote_copy(
        src_ref=src,
        dst_ref=dst,
        send_sem=sems.at[0, index],
        recv_sem=sems.at[1, index],
        device_id=to,
        device_id_type=MESH,
    )
    return copy


class ReduceScatter:
    def __init__(
        self, place, g, rc, r1, r2, rz1, rz2, core_sems, sems, parts, out, zb=None, columns=None
    ):
        self.p, self.g, self.rc, self.r1, self.r2 = place, g, rc, r1, r2
        self.rz1, self.rz2, self.core_sems, self.sems, self.parts = rz1, rz2, core_sems, sems, parts
        self.count = 4 if parts else 1
        self.out, self.columns = out, columns
        self.zb = g.at[:, place.y, place.x, place.c] if zb is None else zb

    def core_copy(self, k):
        p = self.p
        kh, kl = k // 2, lax.rem(k, 2)
        if self.parts == "yx":
            src, dst = self.g.at[:, kh, kl, 1 - p.c], self.rc.at[:, kh, kl]
        elif self.parts == "z":
            src, dst = self.g.at[:, :, :, 1 - p.c, kh, kl], self.rc.at[:, :, :, kh, kl]
        else:
            src, dst = self.g.at[:, :, :, 1 - p.c], self.rc
        return send(src, dst, self.core_sems, k, p.core)

    def core_start(self, k):
        self.core_copy(k).start()

    def core_sum(self, k):
        p, g, rc = self.p, self.g, self.rc
        kh, kl = k // 2, lax.rem(k, 2)
        self.core_copy(k).wait()
        if self.parts == "yx":
            for h in range(2):
                g[h, kh, kl, p.c] = g[h, kh, kl, p.c] + rc[h, kh, kl]
            return

        def add(i, _):
            h, y, x = i // 4, lax.rem(i // 2, 2), lax.rem(i, 2)
            if self.parts == "z":
                g[h, y, x, p.c, kh, kl] = g[h, y, x, p.c, kh, kl] + rc[h, y, x, kh, kl]
            else:
                g[h, y, x, p.c] = g[h, y, x, p.c] + rc[h, y, x]
            return 0

        lax.fori_loop(0, 8, add, 0)

    def first_x(self, k):
        p, g, r1 = self.p, self.g, self.r1
        kh, kl = k // 2, lax.rem(k, 2)
        if self.parts == "yx":
            return send(g.at[0, kh, 1 - p.x, p.c], r1.at[0, kh], self.sems, kh, p.along_x)
        if self.parts == "z":
            return send(
                g.at[0, :, 1 - p.x, p.c, kh, kl], r1.at[0, :, kh, kl], self.sems, k, p.along_x
            )
        return send(g.at[0, :, 1 - p.x, p.c], r1.at[0], self.sems, 0, p.along_x)

    def first_y(self, k):
        p, g, r1 = self.p, self.g, self.r1
        kh, kl = k // 2, lax.rem(k, 2)
        if self.parts == "yx":
            return send(g.at[1, 1 - p.y, kl, p.c], r1.at[1, kl], self.sems, 4 + kl, p.along_y)
        if self.parts == "z":
            return send(
                g.at[1, 1 - p.y, :, p.c, kh, kl], r1.at[1, :, kh, kl], self.sems, 4 + k, p.along_y
            )
        return send(g.at[1, 1 - p.y, :, p.c], r1.at[1], self.sems, 4, p.along_y)

    def first_start(self, k):
        p = self.p
        if self.parts == "yx":
            pl.when(lax.rem(k, 2) != p.x)(lambda: self.first_x(k).start())
            pl.when(k // 2 != p.y)(lambda: self.first_y(k).start())
        else:
            self.first_x(k).start()
            self.first_y(k).start()

    def first_sum(self):
        p, g = self.p, self.g
        if self.parts == "yx":
            for i in range(2):
                self.first_x(2 * i).wait()
                self.first_y(i).wait()
        else:
            for k in range(self.count):
                self.first_x(k).wait()
                self.first_y(k).wait()
        for i in range(2):
            g[0, i, p.x, p.c] = g[0, i, p.x, p.c] + self.r1[0, i]
            g[1, p.y, i, p.c] = g[1, p.y, i, p.c] + self.r1[1, i]

    def second_copies(self):
        p, g = self.p, self.g
        return (
            send(g.at[0, 1 - p.y, p.x, p.c], self.r2.at[0], self.sems, 8, p.along_y),
            send(g.at[1, p.y, 1 - p.x, p.c], self.r2.at[1], self.sems, 9, p.along_x),
        )

    def second_start(self):
        for copy in self.second_copies():
            copy.start()

    def second_sum(self):
        p, g = self.p, self.g
        for copy in self.second_copies():
            copy.wait()
        for h in range(2):
            total = g[h, p.y, p.x, p.c] + self.r2[h]
            if self.columns is None:
                g[h, p.y, p.x, p.c] = total
            else:
                for z, (first, last) in enumerate(self.columns):
                    self.zb[h, z // 2, z % 2] = total[:, first:last]

    def third_copy(self):
        p = self.p
        return send(self.zb.at[:, :, 1 - p.zl], self.rz1, self.sems, 10, p.z_near)

    def third_start(self):
        self.third_copy().start()

    def third_sum(self):
        p, zb = self.p, self.zb
        self.third_copy().wait()
        for h in range(2):
            for i in range(2):
                zb[h, i, p.zl] = zb[h, i, p.zl] + self.rz1[h, i]

    def fourth_copy(self):
        p = self.p
        return send(self.zb.at[:, 1 - p.zh, p.zl], self.rz2, self.sems, 11, p.z_far)

    def fourth_start(self):
        self.fourth_copy().start()

    def fourth_sum(self):
        p, zb = self.p, self.zb
        self.fourth_copy().wait()
        for h in range(2):
            self.out[h] = zb[h, p.zh, p.zl].astype(F32) + self.rz2[h].astype(F32)

    def advance(self, step):
        if step == 0:
            self.core_sum(0)
            self.first_start(0)
        elif step == 1:
            self.first_sum()
            self.second_start()
        elif step == 2:
            self.second_sum()
            self.third_start()
        elif step == 3:
            self.third_sum()
            self.fourth_start()
        else:
            self.fourth_sum()


class SmallSum:
    def __init__(self, place, zin, cin, xin, sems, out, spread):
        self.p, self.zin, self.cin, self.xin, self.sems = place, zin, cin, xin, sems
        self.out, self.spread = out, spread
        self.corner = place.d // 2

    def z_copies(self):
        p, mine = self.p, self.zin.at[self.p.z]
        peers = (p.z_near, p.z_far, p.z_mirror)
        return [send(mine, mine, self.sems, i, to) for i, to in enumerate(peers)]

    def core_copy(self):
        return send(self.cin.at[0], self.cin.at[1], self.sems, 3, self.p.core)

    def xy_copies(self):
        p, mine = self.p, self.xin.at[self.corner]
        peers = (p.along_x, p.along_y, p.diagonal)
        return [send(mine, mine, self.sems, 4 + i, to) for i, to in enumerate(peers)]

    def advance(self, step):
        cin, zin, xin = self.cin, self.zin, self.xin
        if step == 0:
            for copy in self.z_copies():
                copy.start()
        elif step == 1:
            for copy in self.z_copies():
                copy.wait()
            cin[0] = self.spread(zin[0] + zin[1] + zin[2] + zin[3])
            self.core_copy().start()
        elif step == 2:
            self.core_copy().wait()
            xin[self.corner] = cin[0] + cin[1]
            for copy in self.xy_copies():
                copy.start()
        else:
            for copy in self.xy_copies():
                copy.wait()
            self.out[...] = xin[0] + xin[1] + xin[2] + xin[3]


def norm_stats(v):
    mean = jnp.mean(v, axis=-1, keepdims=True)
    centred = v - mean
    inverse = lax.rsqrt(jnp.mean(centred * centred, axis=-1, keepdims=True) + EPSILON)
    return mean, inverse


def norm_back(t, gain, n, inverse):
    u = t * gain
    return inverse * (
        u - jnp.mean(u, axis=-1, keepdims=True) - n * jnp.mean(u * n, axis=-1, keepdims=True)
    )


def column_sum(v):
    return jnp.sum(v, axis=0, keepdims=True)


def layer_kernel(names, *refs):
    r = types.SimpleNamespace(**dict(zip(names, refs)))
    p = Place()
    T, D = r.tokens.shape

    barrier = pltpu.get_barrier_semaphore()
    partners = (p.core, p.along_x, p.along_y, p.diagonal, p.z_near, p.z_far, p.z_mirror)
    for partner in partners:
        pl.semaphore_signal(barrier, inc=1, device_id=partner, device_id_type=MESH)

    pool = r.pool

    def load(src, dst, index):
        return pltpu.make_async_copy(src, dst, r.load_sems.at[index])

    def chunk_of(i):
        flip_y, flip_x = 1 - lax.rem(i, 2), 1 - i // 2
        return 2 * (p.y + flip_y - 2 * flip_y * p.y) + p.x + flip_x - 2 * flip_x * p.x

    def up_load(i):
        src = r.up_weight.at[:, pl.ds(pl.multiple_of(chunk_of(i) * D, D), D)]
        return load(src, pool.at[1 + i], 6 + i)

    def down_load(i):
        src = r.down_weight.at[pl.ds(pl.multiple_of(chunk_of(i) * D, D), D), :]
        return load(src, pool.at[4 + i], 10 + i)

    tokens_load = load(r.tokens, r.tok, 0)
    tokens_load.start()
    qkv_loads = [
        load(r.qkv_weight.at[:, pl.ds(i * D, D)], pool.at[1 + i], 1 + i) for i in range(3)
    ]
    for i in (1, 2, 0):
        qkv_loads[i].start()
    cot_load = load(r.cotangent, r.cot, 4)
    out_load = load(r.out_weight, pool.at[0], 5)
    for copy in [cot_load] + [down_load(i) for i in range(4)] + [out_load]:
        copy.start()

    gid = r.group_ids[0]
    length = r.lengths[0]
    table = r.group_table[...]
    group_rows = lax.broadcasted_iota(jnp.int32, table.shape, 0)
    table_row = jnp.sum(jnp.where(group_rows == gid, table, 0.0), axis=0, keepdims=True)
    tokens_load.wait()
    start = r.tok[...].astype(F32) + table_row
    mean, inverse = norm_stats(start)
    nx, nxT = r.nx, r.nxT
    nx[0] = ((start - mean) * inverse * row_of(r.first_gain) + row_of(r.first_shift)).astype(BF)

    pl.semaphore_wait(barrier, len(partners))

    def nx_copy(s):
        return send(nx.at[s], nx.at[s + 1], r.nx_sems, s, p.along_z(1))

    def nx_wait(s):
        return send(nx.at[s - 1], nx.at[s], r.nx_sems, s - 1, p.along_z(-1)).wait_recv()

    kv, qT, outT, stat, mass = r.kv, r.qT, r.outT, r.stat, r.mass
    qin, doin, stat_in = r.qin, r.doin, r.stat_in
    key_iota = lax.broadcasted_iota(jnp.int32, (T, T), 0)
    query_iota = lax.broadcasted_iota(jnp.int32, (T, T), 1)
    scale2 = HEAD**-0.5 * LOG2E

    def q_copy(t):
        src = qT if t == 0 else qin.at[t - 1]
        return send(src, qin.at[t], r.q_sems, t, p.along_z(-1))

    def q_wait(t):
        send(qT, qin.at[t], r.q_sems, t, p.along_z(1)).wait_recv()

    def q_pass(t):
        q_wait(t)
        q_copy(t + 1).start()

    def head_rows(h):
        return pl.ds(pl.multiple_of(h * HEAD, HEAD), HEAD)

    def masked(scores, block, causal):
        allowed = key_iota < length - block * T
        if causal:
            allowed = allowed & (key_iota <= query_iota)
        return jnp.where(allowed, scores * scale2, NEG_LARGE)

    def attend(s, own):
        def some_heads(g, _):
            heads = [g * GROUP + i for i in range(GROUP)]
            places = [head_rows(h) for h in heads]
            scores = [masked(dot_tn(kv[s, 0, rows], qT[rows]), p.z - s, own) for rows in places]
            highest = [jnp.max(v, axis=0, keepdims=True) for v in scores]
            if not own:
                highest = [jnp.maximum(v, stat[pl.ds(h, 1)]) for v, h in zip(highest, heads)]
                fade = [jnp.exp2(stat[pl.ds(h, 1)] - v) for v, h in zip(highest, heads)]
            weights = [jnp.exp2(v - m) for v, m in zip(scores, highest)]
            total = [column_sum(v) for v in weights]
            value = [dot(kv[s, 1, rows], v.astype(BF)) for v, rows in zip(weights, places)]
            for i, (h, rows) in enumerate(zip(heads, places)):
                if not own:
                    total[i] = total[i] + mass[pl.ds(h, 1)] * fade[i]
                    value[i] = value[i] + outT[rows] * fade[i]
                stat[pl.ds(h, 1)] = highest[i]
                mass[pl.ds(h, 1)] = total[i]
                outT[rows] = value[i]
            return 0

        lax.fori_loop(0, HEADS // GROUP, some_heads, 0)

    def project(s):
        block = nx[s]
        kv[s, 0] = dot(block, pool[2]).astype(BF).T
        kv[s, 1] = (dot(block, pool[3]) + r.qv_bias[1:2]).astype(BF).T

    pl.when(p.z < 3)(lambda: nx_copy(0).start())
    nxT[...] = nx[0].T
    for copy in qkv_loads:
        copy.wait()
    qT[...] = (dot(nx[0], pool[1]) + r.qv_bias[0:1]).astype(BF).T
    pl.when(p.z >= 1)(lambda: q_copy(0).start())
    project(0)
    attend(0, True)
    cot_load.wait()
    r.cotT[...] = r.cot[...].T
    for k in range(4):
        r.up_rows[k : k + 1] = r.up_bias[k * D : (k + 1) * D].reshape(1, D)

    def act_grad(i):
        down_load(i).wait()
        r.act_grad[lax.rem(i, 2)] = dot_nt(r.cot[...], pool[4 + i])

    lax.fori_loop(0, 2, lambda i, _: (act_grad(i), 0)[1], 0)

    def earlier_block(s, _):
        nx_wait(s)
        pl.when((s < 3) & (p.z < 3))(lambda: nx_copy(s).start())
        project(s)
        attend(s, False)
        pl.when((s == 1) & (p.z < 3))(functools.partial(q_pass, 0))
        return 0

    lax.fori_loop(1, p.z + 1, earlier_block, 0)
    for i in (0, 1, 2):
        up_load(i).start()

    def finish(h, _):
        rows = head_rows(h)
        value = outT[rows] * (1.0 / mass[pl.ds(h, 1)])
        outT[rows] = value
        r.attT[rows] = value.astype(BF)
        return 0

    lax.fori_loop(0, HEADS, finish, 0, unroll=True)
    stat[0:HEADS] = stat[0:HEADS] + jnp.log2(mass[...])
    attT = r.attT

    out_load.wait()
    after = r.tok[...].astype(F32) + table_row + dot(attT[...].T, pool[0]) + row_of(r.out_bias)
    r.after[...] = after
    mean, inverse = norm_stats(after)
    norm_two = ((after - mean) * inverse * row_of(r.second_gain) + row_of(r.second_shift)).astype(BF)
    r.norm_two[...] = norm_two
    r.norm_twoT[...] = norm_two.T
    r.total[...] = after + row_of(r.down_bias)
    r.t[...] = jnp.zeros((T, D), F32)

    g_down, g_up, g_out = r.g_down, r.g_up, r.g_out

    def scatter(name, parts, out, columns=None):
        return ReduceScatter(
            p,
            getattr(r, "g_" + name),
            getattr(r, "rc_" + name),
            getattr(r, "r1_" + name),
            getattr(r, "r2_" + name),
            getattr(r, "rz1_" + name),
            getattr(r, "rz2_" + name),
            getattr(r, "cs_" + name),
            getattr(r, "ss_" + name),
            parts,
            out,
            getattr(r, "zb_" + name, None),
            columns,
        )

    narrow, width = D // 4, D // 2
    down = scatter("down", "yx", r.s_down)
    up = scatter("up", "z", r.s_up)
    out = scatter("out", "", r.s_out, [(z * narrow, (z + 1) * narrow) for z in range(4)])
    queries, keys, values = [(i * width, (i + 1) * width) for i in range(3)]
    projs = [
        scatter("p0", "", r.fin.at[0], (queries, keys, values, values)),
        scatter("p1", "", r.fin.at[1], (queries, queries, keys, values)),
    ]

    def spread(rows):
        table_grad = jnp.where(group_rows == gid, rows[0:1], 0.0)
        return jnp.concatenate([table_grad, rows[1:5]], axis=0)

    early = SmallSum(
        p, r.early_z, r.early_c, r.early_x, r.early_sems, r.early_out, lambda rows: rows
    )
    late = SmallSum(p, r.late_z, r.late_c, r.late_x, r.late_sems, r.late_out, spread)
    small = r.early_z.at[p.z]
    gelu_c = math.sqrt(2.0 / math.pi)

    def pass_on(k):
        down.core_sum(k)
        down.first_start(k)
        up.core_sum(k)
        up.first_start(k)

    def chunk(i, _):
        k = chunk_of(i)
        kh, kl = k // 2, lax.rem(k, 2)
        up_load(i).wait()
        pl.when(i >= 2)(lambda: act_grad(i))
        weight = pool[1 + i]
        weight_down = pool[4 + i]
        hidden = dot(r.norm_two[...], weight) + r.up_rows[pl.ds(k, 1), :]
        square = hidden * hidden
        th = jnp.tanh(gelu_c * hidden * (1.0 + 0.044715 * square))
        half = 0.5 + 0.5 * th
        act = (hidden * half).astype(BF)
        slope = half + 0.5 * hidden * (1.0 - th * th) * gelu_c * (1.0 + 3 * 0.044715 * square)
        grad = r.act_grad[lax.rem(i, 2)] * slope
        small[pl.ds(4 + k, 1), :] = column_sum(grad)
        low = grad.astype(BF)
        piece = D // 2
        for cc in range(2):
            rows = dot(r.cotT[...], act[:, cc * piece : (cc + 1) * piece]).astype(BF)
            part = D // 4
            for z in range(4):
                for h in range(2):
                    at = z * part + h * (part // 2)
                    g_down[h, kh, kl, cc, z // 2, z % 2] = rows[at : at + part // 2]
        down.core_start(k)
        part = D // 8
        for y in range(2):
            rows = dot(r.norm_twoT[y * 4 * part : (y + 1) * 4 * part], low).astype(BF)
            for d in range(4):
                for h in range(2):
                    at = d * part + h * (part // 2)
                    g_up[h, y, d // 2, d % 2, kh, kl] = rows[at : at + part // 2]
        up.core_start(k)
        pl.when(i > 0)(lambda: pass_on(chunk_of(i - 1)))
        r.total[...] += dot(act, weight_down)
        r.t[...] += dot_nt(low, weight)
        pl.when(i == 0)(lambda: up_load(3).start())
        return 0

    lax.fori_loop(0, 4, chunk, 0)
    pass_on(chunk_of(3))
    pl.when(p.z == 1)(functools.partial(q_pass, 1))

    qkv_loads = [
        load(r.qkv_weight.at[:, pl.ds(i * D, D)], pool.at[1 + i], 14 + i) for i in range(3)
    ]
    for copy in qkv_loads:
        copy.start()

    nx[3] = r.total[...].astype(BF)
    result_store = pltpu.make_async_copy(nx.at[3], r.result, r.load_sems.at[17])
    result_store.start()
    cot = r.cot[...].astype(F32)
    after = r.after[...]
    mean, inverse = norm_stats(after)
    n = (after - mean) * inverse
    t = r.t[...]
    after_grad = cot + norm_back(t, row_of(r.second_gain), n, inverse)
    r.after[...] = after_grad
    after_low = after_grad.astype(BF)
    doT = r.doT
    doT[...] = dot_nt(pool[0], after_low).astype(BF)
    for h in range(HEADS):
        rows = slice(h * HEAD, (h + 1) * HEAD)
        stat[HEADS + h : HEADS + h + 1] = column_sum(doT[rows].astype(F32) * outT[rows])
    def group_rows_of(group):
        return pl.ds(pl.multiple_of(group * width, width), width)

    def do_copy(t, group):
        rows = group_rows_of(group)
        src = doT.at[rows] if isinstance(t, int) and t == 0 else doin.at[t - 1, rows]
        return send(src, doin.at[t, rows], r.do_sems, 2 * t + group, p.along_z(-1))

    def stat_copy(t):
        src = stat if isinstance(t, int) and t == 0 else stat_in.at[t - 1]
        return send(src, stat_in.at[t], r.stat_sems, t, p.along_z(-1))

    def do_send(t, group):
        pl.when(group == 0)(lambda: stat_copy(t).start())
        do_copy(t, group).start()

    def stat_wait(t):
        send(stat, stat_in.at[t], r.stat_sems, t, p.along_z(1)).wait_recv()

    def do_wait(t, group):
        rows = group_rows_of(group)
        send(doT.at[rows], doin.at[t, rows], r.do_sems, 2 * t + group, p.along_z(1)).wait_recv()
        pl.when(group == 0)(lambda: stat_wait(t))

    for group in range(2):
        pl.when(p.z >= 1)(functools.partial(do_send, 0, group))
    small[pl.ds(0, 1), :] = column_sum(after_grad)
    small[pl.ds(1, 1), :] = column_sum(t * n)
    small[pl.ds(2, 1), :] = column_sum(t)
    small[pl.ds(3, 1), :] = column_sum(cot)
    rows = dot(attT[...], after_low).astype(BF)
    part = D // 8
    for d in range(8):
        for h in range(2):
            at = d * part + h * (part // 2)
            g_out[h, d // 4, (d // 2) % 2, d % 2] = rows[at : at + part // 2]
    out.core_start(0)

    outT[...] = jnp.zeros((D, T), F32)
    key_grad, value_grad = r.key_grad, r.value_grad
    mixed = (kv.at[1, 0], kv.at[1, 1], kv.at[2, 0])

    def grads_of(s, group, queries, out_grads, sums, causal, for_queries, for_keys):
        heads = [group * GROUP + i for i in range(GROUP)]
        places = [head_rows(h) for h in heads]
        scores = [dot_tn(kv[s, 0, rows], queries[rows]) for rows in places]
        prob_grad = [dot_tn(kv[s, 1, rows], out_grads[rows]) for rows in places]
        scores = [masked(v, p.z - s, causal) for v in scores]
        probs = [jnp.exp2(v - sums[pl.ds(h, 1)]) for v, h in zip(scores, heads)]
        score_grad = [
            (v * (w - sums[pl.ds(HEADS + h, 1)])).astype(BF)
            for v, w, h in zip(probs, prob_grad, heads)
        ]
        if for_queries:
            query_add = [dot(kv[s, 0, rows], v) for v, rows in zip(score_grad, places)]
        if for_keys:
            probs = [v.astype(BF) for v in probs]
            key_add = [dot_nt(queries[rows], v) for v, rows in zip(score_grad, places)]
            value_add = [dot_nt(out_grads[rows], v) for v, rows in zip(probs, places)]
        for i, rows in enumerate(places):
            if for_queries:
                outT[rows] = outT[rows] + query_add[i]
            if for_keys and for_queries:
                key_grad[rows] = key_add[i]
                value_grad[rows] = value_add[i]
            elif for_keys:
                key_grad[rows] = key_grad[rows] + key_add[i]
                value_grad[rows] = value_grad[rows] + value_add[i]

    def query_step(i, _):
        grads_of(p.z - i // 2, lax.rem(i, 2), qT, doT, stat, False, True, False)
        return 0

    def own_step(group, _):
        grads_of(0, group, qT, doT, stat, True, True, True)
        return 0

    def key_step(t, group):
        pl.when((p.z == 0) & (group == 0))(lambda: q_wait(t))
        do_wait(t, group)
        pl.when(p.z >= 1)(lambda: do_send(t + 1, group))
        grads_of(0, group, qin.at[t], doin.at[t], stat_in.at[t], False, False, True)

    def proj_grad(group):
        rows = slice(group * width, (group + 1) * width)
        mixed[0][rows] = (outT[rows] * HEAD**-0.5).astype(BF)
        mixed[1][rows] = (key_grad[rows] * HEAD**-0.5).astype(BF)
        mixed[2][rows] = value_grad[rows].astype(BF)
        target = (r.g_p0, r.g_p1)[group]
        part = D // 8
        for i in range(3):
            piece = dot_nt(nxT[...], mixed[i][rows]).astype(BF)
            for d in range(8):
                for h in range(2):
                    at = d * part + h * (part // 2)
                    target[h, d // 4, (d // 2) % 2, d % 2, :, i * width : (i + 1) * width] = piece[
                        at : at + part // 2
                    ]
        projs[group].core_start(0)

    def norm_back_one():
        outT[...] = sum(dot(pool[1 + i], mixed[i][...]) for i in range(3))
        ones = jnp.ones((8, T), BF)
        rows = r.late_z.at[p.z]
        rows[pl.ds(3, 1), :] = dot_nt(ones, mixed[0][...])[0:1]
        rows[pl.ds(4, 1), :] = dot_nt(ones, mixed[2][...])[0:1]
        t1 = outT[...].T
        start = r.tok[...].astype(F32) + table_row
        mean, inverse = norm_stats(start)
        n = (start - mean) * inverse
        start_grad = r.after[...] + norm_back(t1, row_of(r.first_gain), n, inverse)
        r.norm_two[...] = start_grad.astype(BF)
        tokens_store.start()
        rows[pl.ds(0, 1), :] = column_sum(start_grad)
        rows[pl.ds(1, 1), :] = column_sum(t1 * n)
        rows[pl.ds(2, 1), :] = column_sum(t1)
        late.advance(0)

    tokens_store = pltpu.make_async_copy(r.norm_two, r.grad_tokens, r.load_sems.at[18])

    for copy in qkv_loads:
        copy.wait()
    lax.fori_loop(0, 2 * p.z, query_step, 0)
    lax.fori_loop(0, 2, own_step, 0)
    step = functools.partial

    ahead = (
        (
            (0, step(early.advance, 0)),
            (3, step(down.advance, 1)),
            (3, step(down.advance, 2)),
            (3, step(up.advance, 1)),
            (5, step(proj_grad, 0)),
        ),
        (
            (0, step(down.advance, 1)),
            (3, step(proj_grad, 0)),
        ),
        (
        ),
        (
        ),
    )
    rest = (
        ((), step(proj_grad, 1)),
        ((0, 1), step(down.advance, 1)),
        ((0, 1), step(proj_grad, 0)),
        ((0,), step(up.advance, 1)),
        ((), step(projs[0].advance, 0)),
        ((0,), step(early.advance, 0)),
        ((), norm_back_one),
        ((0,), step(down.advance, 2)),
        ((), step(projs[1].advance, 0)),
        ((), step(up.advance, 2)),
        ((), step(down.advance, 3)),
        ((), step(projs[0].advance, 1)),
        ((), step(projs[1].advance, 1)),
        ((), step(up.advance, 3)),
        ((), step(projs[0].advance, 2)),
        ((), step(out.advance, 0)),
        ((), step(projs[1].advance, 2)),
        ((), step(out.advance, 1)),
        ((), step(down.advance, 4)),
        ((), step(projs[0].advance, 3)),
        ((), step(early.advance, 1)),
        ((), step(late.advance, 1)),
        ((), step(out.advance, 2)),
        ((), step(late.advance, 2)),
        ((), step(projs[1].advance, 3)),
        ((), step(early.advance, 2)),
        ((), step(out.advance, 3)),
        ((), step(up.advance, 4)),
        ((), step(projs[1].advance, 4)),
        ((), step(late.advance, 3)),
        ((), step(projs[0].advance, 4)),
        ((), step(early.advance, 3)),
        ((), step(out.advance, 4)),
    )

    def half_round(i, _):
        for z in range(3):
            for at, one in ahead[z]:
                pl.when((p.z == z) & (i == at))(one)
        pl.when(p.z + i // 2 < 3)(lambda: key_step(i // 2, lax.rem(i, 2)))
        return 0

    for _, one in ahead[3]:
        pl.when(p.z == 3)(one)
    lax.fori_loop(0, 7, half_round, 0)
    for done, one in rest:
        if len(done) == 0:
            one()
        else:
            planes = [z for z in range(4) if z not in done]
            if planes:
                pl.when(functools.reduce(jnp.logical_or, [p.z == z for z in planes]))(one)
    for s in (0, 1, 2):
        pl.when((p.z < 3) & (p.z >= s))(lambda s=s: nx_copy(s).wait_send())
    def sent(t):
        q_copy(t).wait_send()
        stat_copy(t).wait_send()
        do_copy(t, 0).wait_send()
        do_copy(t, 1).wait_send()

    for t in range(3):
        pl.when((p.z >= 1) & (p.z + t <= 3))(functools.partial(sent, t))
    result_store.wait()
    tokens_store.wait()
    fin = r.fin
    layouts = (
        ((0, 0, width), (1, 0, narrow)),
        ((1, narrow, width), (0, 0, width)),
        ((1, 0, width), (0, 0, narrow)),
        ((0, narrow, width), (1, 0, width)),
    )

    def lay_out(order):
        for h in range(2):
            r.s_qkv[h] = jnp.concatenate([fin[g, h, :, a:b] for g, a, b in order], axis=1)

    for z in range(4):
        pl.when(p.z == z)(functools.partial(lay_out, layouts[z]))


def row_of(ref):
    return ref[...].reshape(1, ref.shape[0])


def outputs_kernel(result, grad_tokens, early, late, s_qkv, s_out, s_up, s_down, *outs):
    (
        o_result,
        o_tokens,
        o_table,
        o_first_gain,
        o_first_shift,
        o_qkv,
        o_qv_bias,
        o_out,
        o_out_bias,
        o_second_gain,
        o_second_shift,
        o_up,
        o_up_bias,
        o_down,
        o_down_bias,
    ) = outs
    D = early.shape[1]
    o_result[...] = result[...].reshape(o_result.shape)
    o_tokens[...] = grad_tokens[...].reshape(o_tokens.shape)
    o_table[...] = late[0:16]
    o_first_gain[...] = late[16]
    o_first_shift[...] = late[17]
    o_out_bias[...] = early[0]
    o_second_gain[...] = early[1]
    o_second_shift[...] = early[2]
    o_down_bias[...] = early[3]
    for k in range(4):
        o_up_bias[pl.ds(k * D, D)] = early[4 + k]
    o_qv_bias[...] = late[18:20]
    for ref, value in ((o_qkv, s_qkv), (o_out, s_out), (o_up, s_up), (o_down, s_down)):
        half = value.shape[1]
        for h in range(2):
            ref[h * half : (h + 1) * half] = value[h]


def fused(
    tokens,
    group_ids,
    lengths,
    cotangent,
    group_table,
    first_gain,
    first_shift,
    qkv_weight,
    query_value_bias,
    out_weight,
    out_bias,
    second_gain,
    second_shift,
    up_weight,
    up_bias,
    down_weight,
    down_bias,
):
    _, T, D = tokens.shape
    F = up_weight.shape[1]
    any_spec = pl.BlockSpec(memory_space=pl.ANY)
    vmem = pl.BlockSpec(memory_space=pltpu.VMEM)
    smem = pl.BlockSpec(memory_space=pltpu.SMEM)
    inputs = dict(
        tokens=(tokens.reshape(T, D), any_spec),
        group_ids=(group_ids, smem),
        lengths=(lengths, smem),
        cotangent=(cotangent.reshape(T, D), any_spec),
        group_table=(group_table, vmem),
        first_gain=(first_gain, vmem),
        first_shift=(first_shift, vmem),
        qkv_weight=(qkv_weight, any_spec),
        qv_bias=(query_value_bias, vmem),
        out_weight=(out_weight, any_spec),
        out_bias=(out_bias, vmem),
        second_gain=(second_gain, vmem),
        second_shift=(second_shift, vmem),
        up_weight=(up_weight, any_spec),
        up_bias=(up_bias, vmem),
        down_weight=(down_weight, any_spec),
        down_bias=(down_bias, vmem),
    )
    shares = dict(
        down=(D // 8, F // 8),
        up=(D // 16, F // 4),
        out=(D // 16, D // 4),
        qkv=(D // 16, 3 * D // 4),
    )
    outputs = dict(
        result=((T, D), BF),
        grad_tokens=((T, D), BF),
        early_out=((8, D), F32),
        late_out=((20, D), F32),
    )
    outputs.update({"s_" + k: ((2,) + shares[k], F32) for k in ("qkv", "out", "up", "down")})
    dma = pltpu.SemaphoreType.DMA
    scratch = dict(
        pool=pltpu.VMEM((8, D, D), BF),
        tok=pltpu.VMEM((T, D), BF),
        cot=pltpu.VMEM((T, D), BF),
        cotT=pltpu.VMEM((D, T), BF),
        nx=pltpu.VMEM((4, T, D), BF),
        nxT=pltpu.VMEM((D, T), BF),
        qT=pltpu.VMEM((D, T), BF),
        kv=pltpu.VMEM((4, 2, D, T), BF),
        outT=pltpu.VMEM((D, T), F32),
        stat=pltpu.VMEM((2 * HEADS, T), F32),
        mass=pltpu.VMEM((HEADS, T), F32),
        qin=pltpu.VMEM((3, D, T), BF),
        doin=pltpu.VMEM((3, D, T), BF),
        stat_in=pltpu.VMEM((3, 2 * HEADS, T), F32),
        key_grad=pltpu.VMEM((D, T), F32),
        value_grad=pltpu.VMEM((D, T), F32),
        attT=pltpu.VMEM((D, T), BF),
        after=pltpu.VMEM((T, D), F32),
        norm_two=pltpu.VMEM((T, D), BF),
        norm_twoT=pltpu.VMEM((D, T), BF),
        act_grad=pltpu.VMEM((2, T, D), F32),
        total=pltpu.VMEM((T, D), F32),
        t=pltpu.VMEM((T, D), F32),
        doT=pltpu.VMEM((D, T), BF),
        up_rows=pltpu.VMEM((4, D), F32),
        early_z=pltpu.VMEM((4, 8, D), F32),
        early_c=pltpu.VMEM((2, 8, D), F32),
        early_x=pltpu.VMEM((4, 8, D), F32),
        late_z=pltpu.VMEM((4, 5, D), F32),
        late_c=pltpu.VMEM((2, 20, D), F32),
        late_x=pltpu.VMEM((4, 20, D), F32),
        fin=pltpu.VMEM((2, 2, D // 16, D // 2), F32),
        load_sems=dma((19,)),
        nx_sems=dma((2, 3)),
        q_sems=dma((2, 3)),
        do_sems=dma((2, 6)),
        stat_sems=dma((2, 3)),
        early_sems=dma((2, 7)),
        late_sems=dma((2, 7)),
    )
    places = dict(
        down=(2, 2, D // 8, F // 8),
        up=(2, 2, D // 16, F // 4),
        out=(D // 16, D),
        p0=(D // 16, 3 * D // 2),
        p1=(D // 16, 3 * D // 2),
    )
    columns_of = dict(shares, p0=(D // 16, D // 2), p1=(D // 16, D // 2))
    for name, place in places.items():
        rows, columns = columns_of[name]
        extra = {
            "g_" + name: pltpu.VMEM((2, 2, 2, 2) + place, BF),
            "rc_" + name: pltpu.VMEM((2, 2, 2) + place, BF),
            "r1_" + name: pltpu.VMEM((2, 2) + place, BF),
            "r2_" + name: pltpu.VMEM((2,) + place, BF),
            "rz1_" + name: pltpu.VMEM((2, 2, rows, columns), BF),
            "rz2_" + name: pltpu.VMEM((2, rows, columns), BF),
            "cs_" + name: dma((2, 4)),
            "ss_" + name: dma((2, 12)),
        }
        if len(place) == 2:
            extra["zb_" + name] = pltpu.VMEM((2, 2, 2, rows, columns), BF)
        scratch.update(extra)
    names = list(inputs) + list(outputs) + list(scratch)
    done = pl.pallas_call(
        functools.partial(layer_kernel, names),
        name="layer",
        out_shape=[jax.ShapeDtypeStruct(*o) for o in outputs.values()],
        in_specs=[i[1] for i in inputs.values()],
        out_specs=[any_spec] * 2 + [vmem] * (len(outputs) - 2),
        scratch_shapes=list(scratch.values()),
        compiler_params=pltpu.CompilerParams(
            collective_id=0, has_side_effects=True, vmem_limit_bytes=VMEM_LIMIT
        ),
    )(*[i[0] for i in inputs.values()])
    shape = jax.ShapeDtypeStruct
    outs = pl.pallas_call(
        outputs_kernel,
        name="outputs",
        out_shape=[
            shape((1, T, D), BF),
            shape((1, T, D), BF),
            shape((16, D), F32),
            shape((D,), F32),
            shape((D,), F32),
            shape((D // 8, 3 * D // 4), F32),
            shape((2, D), F32),
            shape((D // 8, D // 4), F32),
            shape((D,), F32),
            shape((D,), F32),
            shape((D,), F32),
            shape((D // 8, F // 4), F32),
            shape((F,), F32),
            shape((D // 4, F // 8), F32),
            shape((D,), F32),
        ],
        in_specs=[vmem] * len(done),
        out_specs=[vmem] * 15,
    )(*done)
    return (*outs[:13], outs[13].T, outs[14])


def shifted(array, axis, by):
    devices = lax.axis_size(axis)
    pairs = [(i, i + by) for i in range(devices) if 0 <= i + by < devices]
    return lax.ppermute(array, axis, pairs)


def as_sent(array):
    return jax.tree.map(lambda a: a.astype(jnp.bfloat16) if a.dtype == jnp.float32 else a, array)


def shifted_2(block, axis, distance):
    devices = range(lax.axis_size(axis))
    route = [((i - distance) % len(devices), i) for i in devices]
    return lax.ppermute(block, axis, route)


def layer_norm(inputs, norm_gain, norm_shift):
    average = jnp.mean(inputs, -1, keepdims=True)
    centred = inputs - average
    inverse = lax.rsqrt(jnp.mean(centred * centred, -1, keepdims=True) + EPSILON)
    return centred * inverse * norm_gain + norm_shift


def tanh_gelu(inputs):
    return jax.nn.gelu(inputs, approximate=True)


def keep_same(state_value):
    return state_value


def scores_of(queries, key_piece, key_start, query_start, lengths):
    sequences, block_len = (queries.shape[0], queries.shape[1])
    key_heads = key_piece.reshape(sequences, key_piece.shape[1], HEADS, HEAD)
    raw_scores = jnp.einsum(
        "gqhe,gkhe->ghqk", queries, key_heads, preferred_element_type=jnp.float32
    ) * HEAD ** (-0.5)
    key_pos = key_start + jnp.arange(key_piece.shape[1])
    query_pos = query_start + jnp.arange(block_len)
    allowed = (query_pos[:, None] >= key_pos[None, :])[None] & (
        key_pos[None, None, :] < lengths[:, None, None]
    )
    return (raw_scores, allowed[:, None])


def plain(
    tokens,
    group_ids,
    lengths,
    cotangent,
    group_table,
    first_gain,
    first_shift,
    qkv_weight,
    query_value_bias,
    out_weight,
    out_bias,
    second_gain,
    second_shift,
    up_weight,
    up_bias,
    down_weight,
    down_bias,
):
    sequences, block_len, features = tokens.shape
    token_rows = sequences * block_len
    seq_count = lax.axis_size("seq")
    seq_index = lax.axis_index("seq")
    query_start = seq_index * block_len
    score_scale = HEAD ** (-0.5)
    one_hot = (group_ids[:, None] == jnp.arange(group_table.shape[0])[None, :]).astype(jnp.float32)
    table_rows = jnp.dot(one_hot, group_table, precision=EXACT)
    start_rows = (tokens.astype(jnp.float32) + table_rows[:, None, :]).reshape(token_rows, features)
    norm_one, pull_one = jax.vjp(layer_norm, start_rows, first_gain, first_shift)
    norm_one_low = norm_one.astype(jnp.bfloat16)
    full_bias = jnp.concatenate(
        [query_value_bias[0], jnp.zeros((features,), jnp.float32), query_value_bias[1]]
    )
    mixed_rows = (
        jnp.dot(norm_one_low, qkv_weight, preferred_element_type=jnp.float32) + full_bias
    ).astype(jnp.bfloat16)
    mixed_rows = mixed_rows.reshape(sequences, block_len, 3 * features)
    queries = mixed_rows[:, :, :features].reshape(sequences, block_len, HEADS, HEAD)
    key_rows = mixed_rows[:, :, features : 2 * features]
    values = mixed_rows[:, :, 2 * features :]
    pieces = []
    current = (key_rows, values)
    for cycle_step in range(seq_count):
        if cycle_step > 0:
            current = shifted((current[0], current[1]), "seq", 1)
        anchor = (seq_index - cycle_step) % seq_count
        pieces.append((current[0], current[1], anchor * block_len, cycle_step <= seq_index))
    shape_rows = (sequences, HEADS, block_len)
    row_max = jnp.full(shape_rows, NEG_LARGE, jnp.float32)
    row_sum = jnp.zeros(shape_rows, jnp.float32)
    stored = []
    for key_piece, value_piece, key_start, active in pieces:

        def visit_block(state_pair, key_piece=key_piece, key_start=key_start):
            raw_scores, allowed = scores_of(queries, key_piece, key_start, query_start, lengths)
            masked_scores = jnp.where(allowed, raw_scores, NEG_LARGE)
            new_max = jnp.maximum(state_pair[0], jnp.max(masked_scores, -1))
            weights = jnp.where(allowed, jnp.exp(masked_scores - new_max[..., None]), 0.0)
            return (
                new_max,
                state_pair[1] * jnp.exp(state_pair[0] - new_max) + jnp.sum(weights, -1),
                masked_scores,
            )

        def pass_block(state_pair):
            return (
                state_pair[0],
                state_pair[1],
                jnp.full(shape_rows + (block_len,), NEG_LARGE, jnp.float32),
            )

        row_max, row_sum, masked_scores = lax.cond(
            active, visit_block, pass_block, (row_max, row_sum)
        )
        stored.append(masked_scores)
    log_sum = row_max + jnp.log(row_sum)
    attended = jnp.zeros((sequences, block_len, HEADS, HEAD), jnp.float32)
    for piece_data, masked_scores in zip(pieces, stored):

        def attend_block(total_out, value_piece=piece_data[1], masked_scores=masked_scores):
            probs = jnp.exp(masked_scores - log_sum[..., None]).astype(jnp.bfloat16)
            value_heads = value_piece.reshape(sequences, block_len, HEADS, HEAD)
            return total_out + jnp.einsum(
                "ghqk,gkhe->gqhe", probs, value_heads, preferred_element_type=jnp.float32
            )

        attended = lax.cond(piece_data[3], attend_block, keep_same, attended)
    attended_low = attended.reshape(token_rows, features).astype(jnp.bfloat16)
    after_attn = (
        start_rows
        + jnp.dot(attended_low, out_weight, preferred_element_type=jnp.float32)
        + out_bias
    )
    norm_two, pull_two = jax.vjp(layer_norm, after_attn, second_gain, second_shift)
    norm_two_low = norm_two.astype(jnp.bfloat16)
    up_rows = jnp.dot(norm_two_low, up_weight, preferred_element_type=jnp.float32) + up_bias
    activated, pull_gelu = jax.vjp(tanh_gelu, up_rows)
    activated_low = activated.astype(jnp.bfloat16)
    result_rows = (
        after_attn
        + jnp.dot(activated_low, down_weight, preferred_element_type=jnp.float32)
        + down_bias
    )
    result = result_rows.astype(jnp.bfloat16).reshape(tokens.shape)
    outer_low = cotangent.reshape(token_rows, features)
    outer_grad = outer_low.astype(jnp.float32)
    grad_down_weight = jnp.dot(activated_low.T, outer_low, preferred_element_type=jnp.float32)
    grad_down_bias = jnp.sum(outer_grad, 0)
    up_grad = pull_gelu(jnp.dot(outer_low, down_weight.T, preferred_element_type=jnp.float32))[0]
    grad_up_bias = jnp.sum(up_grad, 0)
    up_low = up_grad.astype(jnp.bfloat16)
    grad_up_weight = jnp.dot(norm_two_low.T, up_low, preferred_element_type=jnp.float32)
    part_after, grad_second_gain, grad_second_shift = pull_two(
        jnp.dot(up_low, up_weight.T, preferred_element_type=jnp.float32)
    )
    after_grad = outer_grad + part_after
    grad_out_bias = jnp.sum(after_grad, 0)
    after_low = after_grad.astype(jnp.bfloat16)
    grad_out_weight = jnp.dot(attended_low.T, after_low, preferred_element_type=jnp.float32)
    out_grad = jnp.dot(after_low, out_weight.T, preferred_element_type=jnp.float32).astype(
        jnp.bfloat16
    )
    out_grad = out_grad.reshape(sequences, block_len, HEADS, HEAD)
    delta = jnp.transpose(jnp.sum(out_grad.astype(jnp.float32) * attended, -1), (0, 2, 1))

    def back_block(query_grad, key_piece, value_piece, key_start):
        raw_scores, allowed = scores_of(queries, key_piece, key_start, query_start, lengths)
        probs = jnp.where(allowed, jnp.exp(raw_scores - log_sum[..., None]), 0.0)
        value_heads = value_piece.reshape(sequences, block_len, HEADS, HEAD)
        key_heads = key_piece.reshape(sequences, block_len, HEADS, HEAD)
        prob_grad = jnp.einsum(
            "gqhe,gkhe->ghqk", out_grad, value_heads, preferred_element_type=jnp.float32
        )
        score_grad = (probs * (prob_grad - delta[..., None])).astype(jnp.bfloat16)
        query_grad = (
            query_grad
            + jnp.einsum(
                "ghqk,gkhe->gqhe", score_grad, key_heads, preferred_element_type=jnp.float32
            )
            * score_scale
        )
        key_add = (
            jnp.einsum("ghqk,gqhe->gkhe", score_grad, queries, preferred_element_type=jnp.float32)
            * score_scale
        )
        value_add = jnp.einsum(
            "ghqk,gqhe->gkhe",
            probs.astype(jnp.bfloat16),
            out_grad,
            preferred_element_type=jnp.float32,
        )
        return (
            query_grad,
            key_add.reshape(sequences, block_len, features),
            value_add.reshape(sequences, block_len, features),
        )

    empty_rows = jnp.zeros((sequences, block_len, features), jnp.float32)

    def skip_back(query_grad):
        return (query_grad, empty_rows, empty_rows)

    query_grad = jnp.zeros((sequences, block_len, HEADS, HEAD), jnp.float32)
    carried = (empty_rows, empty_rows)
    for cycle_step in range(seq_count):
        piece_data = pieces[cycle_step]

        def visit_back(state_grad, piece_data=piece_data):
            return back_block(state_grad, piece_data[0], piece_data[1], piece_data[2])

        query_grad, key_add, value_add = lax.cond(piece_data[3], visit_back, skip_back, query_grad)
        carried = shifted_2(
            (as_sent(carried[0] + key_add), as_sent(carried[1] + value_add)), "seq", 1
        )
    key_grad, value_grad = carried
    query_flat = query_grad.reshape(token_rows, features)
    key_flat = key_grad.reshape(token_rows, features)
    value_flat = value_grad.reshape(token_rows, features)
    grad_query_value_bias = jnp.stack([jnp.sum(query_flat, 0), jnp.sum(value_flat, 0)])
    mixed_grad = jnp.concatenate([query_flat, key_flat, value_flat], -1).astype(jnp.bfloat16)
    grad_qkv_weight = jnp.dot(norm_one_low.T, mixed_grad, preferred_element_type=jnp.float32)
    part_start, grad_first_gain, grad_first_shift = pull_one(
        jnp.dot(mixed_grad, qkv_weight.T, preferred_element_type=jnp.float32)
    )
    start_grad = after_grad + part_start
    grad_tokens = start_grad.astype(jnp.bfloat16).reshape(tokens.shape)
    grad_group_table = jnp.dot(
        one_hot.T, jnp.sum(start_grad.reshape(sequences, block_len, features), 1), precision=EXACT
    )
    small_sums = lax.psum(
        (
            grad_group_table,
            grad_first_gain,
            grad_first_shift,
            grad_query_value_bias,
            grad_out_bias,
            grad_second_gain,
            grad_second_shift,
            grad_up_bias,
            grad_down_bias,
        ),
        ("dp", "seq"),
    )
    matrices = (grad_qkv_weight, grad_out_weight, grad_up_weight, grad_down_weight)
    shares = (
        lax.psum_scatter(
            matrices[0].astype(jnp.bfloat16), "seq", scatter_dimension=1, tiled=True
        ).astype(jnp.float32),
        lax.psum_scatter(
            matrices[1].astype(jnp.bfloat16), "seq", scatter_dimension=1, tiled=True
        ).astype(jnp.float32),
        lax.psum_scatter(
            matrices[2].astype(jnp.bfloat16), "seq", scatter_dimension=1, tiled=True
        ).astype(jnp.float32),
        lax.psum_scatter(
            matrices[3].astype(jnp.bfloat16), "seq", scatter_dimension=1, tiled=True
        ).astype(jnp.float32),
    )
    shares = (
        lax.psum_scatter(
            shares[0].astype(jnp.bfloat16), "dp", scatter_dimension=0, tiled=True
        ).astype(jnp.float32),
        lax.psum_scatter(
            shares[1].astype(jnp.bfloat16), "dp", scatter_dimension=0, tiled=True
        ).astype(jnp.float32),
        lax.psum_scatter(
            shares[2].astype(jnp.bfloat16), "dp", scatter_dimension=0, tiled=True
        ).astype(jnp.float32),
        lax.psum_scatter(
            shares[3].astype(jnp.bfloat16), "dp", scatter_dimension=0, tiled=True
        ).astype(jnp.float32),
    )
    return (
        result,
        grad_tokens,
        small_sums[0],
        small_sums[1],
        small_sums[2],
        shares[0],
        small_sums[3],
        shares[1],
        small_sums[4],
        small_sums[5],
        small_sums[6],
        shares[2],
        small_sums[7],
        shares[3],
        small_sums[8],
    )


def solution(mesh):
    in_specs = (
        P("dp", "seq", None),
        P("dp"),
        P("dp"),
        P("dp", "seq", None),
        P(),
        P(),
        P(),
        P(),
        P(),
        P(),
        P(),
        P(),
        P(),
        P(),
        P(),
        P(),
        P(),
    )
    out_specs = (
        P("dp", "seq", None),
        P("dp", "seq", None),
        P(),
        P(),
        P(),
        P("dp", "seq"),
        P(),
        P("dp", "seq"),
        P(),
        P(),
        P(),
        P("dp", "seq"),
        P(),
        P("dp", "seq"),
        P(),
    )
    def shards(*arrays):
        sizes = (mesh.shape["dp"], mesh.shape["seq"]) + arrays[0].shape
        return (fused if sizes == (8, 4, 1, 256, 768) else plain)(*arrays)

    return jax.shard_map(shards, mesh=mesh, in_specs=in_specs, out_specs=out_specs, check_vma=False)
```

```python
import functools
import math
import types

import jax
import jax.numpy as jnp
from jax import lax
from jax.experimental import pallas as pl
from jax.experimental.pallas import tpu as pltpu
from jax.sharding import PartitionSpec as P

HEADS = 12
HEAD = 64


EPSILON = 1e-05
NEG_LARGE = -1e30
EXACT = lax.Precision.HIGHEST


VMEM_LIMIT = 64 << 20
GROUP = 6


BF = jnp.bfloat16
VECTORS = (
    "group_table",
    "first_gain",
    "first_shift",
    "qv_bias",
    "out_bias",
    "second_gain",
    "second_shift",
    "up_bias",
    "down_bias",
)
F32 = jnp.float32
MESH = pl.DeviceIdType.MESH
LOG2E = 1.4426950408889634


def dot(a, b):
    return lax.dot_general(a, b, (((1,), (0,)), ((), ())), preferred_element_type=F32)


def dot_nt(a, b):
    return lax.dot_general(a, b, (((1,), (1,)), ((), ())), preferred_element_type=F32)


def dot_tn(a, b):
    return lax.dot_general(a, b, (((0,), (0,)), ((), ())), preferred_element_type=F32)


def flipped(index, bit):
    return index + bit - 2 * bit * lax.rem(index // bit, 2)


class Place:
    def __init__(self):
        self.d = lax.axis_index("dp")
        self.z = lax.axis_index("seq")
        self.c = lax.rem(self.d, 2)
        self.x = lax.rem(self.d // 2, 2)
        self.y = lax.rem(self.d // 4, 2)
        self.zl = lax.rem(self.z, 2)
        self.zh = lax.rem(self.z // 2, 2)
        self.core = (flipped(self.d, 1), self.z)
        self.along_x = (flipped(self.d, 2), self.z)
        self.along_y = (flipped(self.d, 4), self.z)
        self.z_near = (self.d, flipped(self.z, 1))
        self.z_far = (self.d, flipped(self.z, 2))
        self.z_mirror = (self.d, 3 - self.z)
        self.diagonal = (flipped(flipped(self.d, 2), 4), self.z)

    def along_z(self, k):
        return (self.d, self.z + k)


def send(src, dst, sems, index, to):
    copy = pltpu.make_async_remote_copy(
        src_ref=src,
        dst_ref=dst,
        send_sem=sems.at[0, index],
        recv_sem=sems.at[1, index],
        device_id=to,
        device_id_type=MESH,
    )
    return copy


class ReduceScatter:
    def __init__(
        self, place, g, rc, r1, r2, rz1, rz2, core_sems, sems, parts, out, zb=None, columns=None
    ):
        self.p, self.g, self.rc, self.r1, self.r2 = place, g, rc, r1, r2
        self.rz1, self.rz2, self.core_sems, self.sems, self.parts = rz1, rz2, core_sems, sems, parts
        self.count = 4 if parts else 1
        self.out, self.columns = out, columns
        self.zb = g.at[:, place.y, place.x, place.c] if zb is None else zb

    def core_copy(self, k):
        p = self.p
        kh, kl = k // 2, lax.rem(k, 2)
        if self.parts == "yx":
            src, dst = self.g.at[:, kh, kl, 1 - p.c], self.rc.at[:, kh, kl]
        elif self.parts == "z":
            src, dst = self.g.at[:, :, :, 1 - p.c, kh, kl], self.rc.at[:, :, :, kh, kl]
        else:
            src, dst = self.g.at[:, :, :, 1 - p.c], self.rc
        return send(src, dst, self.core_sems, k, p.core)

    def core_start(self, k):
        self.core_copy(k).start()

    def core_sum(self, k):
        p, g, rc = self.p, self.g, self.rc
        kh, kl = k // 2, lax.rem(k, 2)
        self.core_copy(k).wait()
        if self.parts == "yx":
            for h in range(2):
                g[h, kh, kl, p.c] = g[h, kh, kl, p.c] + rc[h, kh, kl]
            return

        def add(i, _):
            h, y, x = i // 4, lax.rem(i // 2, 2), lax.rem(i, 2)
            if self.parts == "z":
                g[h, y, x, p.c, kh, kl] = g[h, y, x, p.c, kh, kl] + rc[h, y, x, kh, kl]
            else:
                g[h, y, x, p.c] = g[h, y, x, p.c] + rc[h, y, x]
            return 0

        lax.fori_loop(0, 8, add, 0)

    def first_x(self, k):
        p, g, r1 = self.p, self.g, self.r1
        kh, kl = k // 2, lax.rem(k, 2)
        if self.parts == "yx":
            return send(g.at[0, kh, 1 - p.x, p.c], r1.at[0, kh], self.sems, kh, p.along_x)
        if self.parts == "z":
            return send(
                g.at[0, :, 1 - p.x, p.c, kh, kl], r1.at[0, :, kh, kl], self.sems, k, p.along_x
            )
        return send(g.at[0, :, 1 - p.x, p.c], r1.at[0], self.sems, 0, p.along_x)

    def first_y(self, k):
        p, g, r1 = self.p, self.g, self.r1
        kh, kl = k // 2, lax.rem(k, 2)
        if self.parts == "yx":
            return send(g.at[1, 1 - p.y, kl, p.c], r1.at[1, kl], self.sems, 4 + kl, p.along_y)
        if self.parts == "z":
            return send(
                g.at[1, 1 - p.y, :, p.c, kh, kl], r1.at[1, :, kh, kl], self.sems, 4 + k, p.along_y
            )
        return send(g.at[1, 1 - p.y, :, p.c], r1.at[1], self.sems, 4, p.along_y)

    def first_start(self, k):
        p = self.p
        if self.parts == "yx":
            pl.when(lax.rem(k, 2) != p.x)(lambda: self.first_x(k).start())
            pl.when(k // 2 != p.y)(lambda: self.first_y(k).start())
        else:
            self.first_x(k).start()
            self.first_y(k).start()

    def first_sum(self):
        p, g = self.p, self.g
        if self.parts == "yx":
            for i in range(2):
                self.first_x(2 * i).wait()
                self.first_y(i).wait()
        else:
            for k in range(self.count):
                self.first_x(k).wait()
                self.first_y(k).wait()
        for i in range(2):
            g[0, i, p.x, p.c] = g[0, i, p.x, p.c] + self.r1[0, i]
            g[1, p.y, i, p.c] = g[1, p.y, i, p.c] + self.r1[1, i]

    def second_copies(self):
        p, g = self.p, self.g
        return (
            send(g.at[0, 1 - p.y, p.x, p.c], self.r2.at[0], self.sems, 8, p.along_y),
            send(g.at[1, p.y, 1 - p.x, p.c], self.r2.at[1], self.sems, 9, p.along_x),
        )

    def second_start(self):
        for copy in self.second_copies():
            copy.start()

    def second_sum(self):
        p, g = self.p, self.g
        for copy in self.second_copies():
            copy.wait()
        for h in range(2):
            total = g[h, p.y, p.x, p.c] + self.r2[h]
            if self.columns is None:
                g[h, p.y, p.x, p.c] = total
            else:
                for z, (first, last) in enumerate(self.columns):
                    self.zb[h, z // 2, z % 2] = total[:, first:last]

    def third_copy(self):
        p = self.p
        return send(self.zb.at[:, :, 1 - p.zl], self.rz1, self.sems, 10, p.z_near)

    def third_start(self):
        self.third_copy().start()

    def third_sum(self):
        p, zb = self.p, self.zb
        self.third_copy().wait()
        for h in range(2):
            for i in range(2):
                zb[h, i, p.zl] = zb[h, i, p.zl] + self.rz1[h, i]

    def fourth_copy(self):
        p = self.p
        return send(self.zb.at[:, 1 - p.zh, p.zl], self.rz2, self.sems, 11, p.z_far)

    def fourth_start(self):
        self.fourth_copy().start()

    def fourth_sum(self):
        p, zb = self.p, self.zb
        self.fourth_copy().wait()
        for h in range(2):
            total = zb[h, p.zh, p.zl].astype(F32) + self.rz2[h].astype(F32)
            if callable(self.out):
                self.out(h, total)
            else:
                self.out[h] = total

    def advance(self, step):
        if step == 0:
            self.core_sum(0)
            self.first_start(0)
        elif step == 1:
            self.first_sum()
            self.second_start()
        elif step == 2:
            self.second_sum()
            self.third_start()
        elif step == 3:
            self.third_sum()
            self.fourth_start()
        else:
            self.fourth_sum()


class SmallSum:
    def __init__(self, place, zin, cin, xin, sems, out, spread):
        self.p, self.zin, self.cin, self.xin, self.sems = place, zin, cin, xin, sems
        self.out, self.spread = out, spread
        self.corner = place.d // 2

    def z_copies(self):
        p, mine = self.p, self.zin.at[self.p.z]
        peers = (p.z_near, p.z_far, p.z_mirror)
        return [send(mine, mine, self.sems, i, to) for i, to in enumerate(peers)]

    def core_copy(self):
        return send(self.cin.at[0], self.cin.at[1], self.sems, 3, self.p.core)

    def xy_copies(self):
        p, mine = self.p, self.xin.at[self.corner]
        peers = (p.along_x, p.along_y, p.diagonal)
        return [send(mine, mine, self.sems, 4 + i, to) for i, to in enumerate(peers)]

    def advance(self, step):
        cin, zin, xin = self.cin, self.zin, self.xin
        if step == 0:
            for copy in self.z_copies():
                copy.start()
        elif step == 1:
            for copy in self.z_copies():
                copy.wait()
            cin[0] = self.spread(zin[0] + zin[1] + zin[2] + zin[3])
            self.core_copy().start()
        elif step == 2:
            self.core_copy().wait()
            xin[self.corner] = cin[0] + cin[1]
            for copy in self.xy_copies():
                copy.start()
        else:
            for copy in self.xy_copies():
                copy.wait()
            self.out[...] = xin[0] + xin[1] + xin[2] + xin[3]


def norm_stats(v):
    mean = jnp.mean(v, axis=-1, keepdims=True)
    centred = v - mean
    inverse = lax.rsqrt(jnp.mean(centred * centred, axis=-1, keepdims=True) + EPSILON)
    return mean, inverse


def norm_back(t, gain, n, inverse):
    u = t * gain
    return inverse * (
        u - jnp.mean(u, axis=-1, keepdims=True) - n * jnp.mean(u * n, axis=-1, keepdims=True)
    )


def column_sum(v):
    return jnp.sum(v, axis=0, keepdims=True)


def layer_kernel(names, *refs):
    r = types.SimpleNamespace(**dict(zip(names, refs)))
    p = Place()
    T, D = r.tokens.shape

    barrier = pltpu.get_barrier_semaphore()
    partners = (p.core, p.along_x, p.along_y, p.diagonal, p.z_near, p.z_far, p.z_mirror)
    for partner in partners:
        pl.semaphore_signal(barrier, inc=1, device_id=partner, device_id_type=MESH)

    pool = r.pool

    def load(src, dst, index):
        return pltpu.make_async_copy(src, dst, r.load_sems.at[index])

    def chunk_of(i):
        flip_y, flip_x = 1 - lax.rem(i, 2), 1 - i // 2
        return 2 * (p.y + flip_y - 2 * flip_y * p.y) + p.x + flip_x - 2 * flip_x * p.x

    def up_load(i):
        src = r.up_weight.at[:, pl.ds(pl.multiple_of(chunk_of(i) * D, D), D)]
        return load(src, pool.at[1 + i], 6 + i)

    def down_load(i):
        src = r.down_weight.at[pl.ds(pl.multiple_of(chunk_of(i) * D, D), D), :]
        return load(src, pool.at[4 + i], 10 + i)

    tokens_load = load(r.tokens, r.tok, 0)
    tokens_load.start()
    vectors = [
        load(getattr(r, name), getattr(r, "v_" + name), 20 + i) for i, name in enumerate(VECTORS)
    ]
    for copy in vectors:
        copy.start()
    qkv_loads = [
        load(r.qkv_weight.at[:, pl.ds(i * D, D)], pool.at[1 + i], 1 + i) for i in range(3)
    ]
    for i in (1, 2, 0):
        qkv_loads[i].start()
    cot_load = load(r.cotangent, r.cot, 4)
    out_load = load(r.out_weight, pool.at[0], 5)
    for copy in [cot_load] + [down_load(i) for i in range(4)] + [out_load]:
        copy.start()

    gid = r.group_ids[0]
    length = r.lengths[0]
    for copy in vectors:
        copy.wait()
    table = r.v_group_table[...]
    group_rows = lax.broadcasted_iota(jnp.int32, table.shape, 0)
    table_row = jnp.sum(jnp.where(group_rows == gid, table, 0.0), axis=0, keepdims=True)
    tokens_load.wait()
    start = r.tok[...].astype(F32) + table_row
    mean, inverse = norm_stats(start)
    nx, nxT = r.nx, r.nxT
    r.norm_two[...] = ((start - mean) * inverse * row_of(r.v_first_gain) + row_of(r.v_first_shift)).astype(BF)

    pl.semaphore_wait(barrier, len(partners))

    def nx_copy(s, half):
        rows = pl.ds(half * (T // 2), T // 2)
        own = isinstance(s, int) and s == 0
        src = r.norm_two.at[rows] if own else nx.at[s - 1, rows]
        return send(src, nx.at[s, rows], r.nx_sems, 2 * s + half, p.along_z(1))

    def nx_pass(s, half):
        rows = pl.ds(half * (T // 2), T // 2)
        here = nx.at[s - 1, rows]
        send(here, here, r.nx_sems, 2 * (s - 1) + half, p.along_z(-1)).wait_recv()
        pl.when((s < 3) & (p.z < 3))(lambda: nx_copy(s, half).start())

    kv, qT, outT, stat, mass = r.kv, r.qT, r.outT, r.stat, r.mass
    qin, doin, stat_in = r.qin, r.doin, r.stat_in
    key_iota = lax.broadcasted_iota(jnp.int32, (T, T), 0)
    query_iota = lax.broadcasted_iota(jnp.int32, (T, T), 1)
    scale2 = HEAD**-0.5 * LOG2E

    def q_copy(t):
        src = qT if t == 0 else qin.at[t - 1]
        return send(src, qin.at[t], r.q_sems, t, p.along_z(-1))

    def q_wait(t):
        send(qT, qin.at[t], r.q_sems, t, p.along_z(1)).wait_recv()

    def q_pass(t):
        q_wait(t)
        q_copy(t + 1).start()

    def head_rows(h):
        return pl.ds(pl.multiple_of(h * HEAD, HEAD), HEAD)

    def masked(scores, block, causal):
        allowed = key_iota < length - block * T
        if causal:
            allowed = allowed & (key_iota <= query_iota)
        return jnp.where(allowed, scores * scale2, NEG_LARGE)

    def attend(s, own):
        def some_heads(g, _):
            heads = [g * GROUP + i for i in range(GROUP)]
            places = [head_rows(h) for h in heads]
            scores = [masked(dot_tn(kv[s, 0, rows], qT[rows]), p.z - s, own) for rows in places]
            highest = [jnp.max(v, axis=0, keepdims=True) for v in scores]
            if not own:
                highest = [jnp.maximum(v, stat[pl.ds(h, 1)]) for v, h in zip(highest, heads)]
                fade = [jnp.exp2(stat[pl.ds(h, 1)] - v) for v, h in zip(highest, heads)]
            weights = [jnp.exp2(v - m) for v, m in zip(scores, highest)]
            total = [column_sum(v) for v in weights]
            value = [dot(kv[s, 1, rows], v.astype(BF)) for v, rows in zip(weights, places)]
            for i, (h, rows) in enumerate(zip(heads, places)):
                if not own:
                    total[i] = total[i] + mass[pl.ds(h, 1)] * fade[i]
                    value[i] = value[i] + outT[rows] * fade[i]
                stat[pl.ds(h, 1)] = highest[i]
                mass[pl.ds(h, 1)] = total[i]
                outT[rows] = value[i]
            return 0

        lax.fori_loop(0, HEADS // GROUP, some_heads, 0)

    def project(s, block):
        kv[s, 0] = dot(block, pool[2]).astype(BF).T
        kv[s, 1] = (dot(block, pool[3]) + r.v_qv_bias[1:2]).astype(BF).T

    for half in range(2):
        pl.when(p.z < 3)(functools.partial(lambda half: nx_copy(0, half).start(), half))
    nxT[...] = r.norm_two[...].T
    for copy in qkv_loads:
        copy.wait()
    qT[...] = (dot(r.norm_two[...], pool[1]) + r.v_qv_bias[0:1]).astype(BF).T
    pl.when(p.z >= 1)(lambda: q_copy(0).start())
    project(0, r.norm_two[...])
    attend(0, True)
    cot_load.wait()
    r.cotT[...] = r.cot[...].T
    for k in range(4):
        r.up_rows[k : k + 1] = r.v_up_bias[k * D : (k + 1) * D].reshape(1, D)

    def act_grad(i):
        down_load(i).wait()
        r.act_grad[lax.rem(i, 2)] = dot_nt(r.cot[...], pool[4 + i])

    lax.fori_loop(0, 2, lambda i, _: (act_grad(i), 0)[1], 0)

    def earlier_block(s, _):
        nx_pass(s, 0)
        nx_pass(s, 1)
        project(s, nx[s - 1])
        attend(s, False)
        pl.when((s == 1) & (p.z < 3))(functools.partial(q_pass, 0))
        return 0

    lax.fori_loop(1, p.z + 1, earlier_block, 0)
    for i in (0, 1, 2):
        up_load(i).start()

    def finish(h, _):
        rows = head_rows(h)
        value = outT[rows] * (1.0 / mass[pl.ds(h, 1)])
        outT[rows] = value
        r.attT[rows] = value.astype(BF)
        return 0

    lax.fori_loop(0, HEADS, finish, 0, unroll=True)
    stat[0:HEADS] = stat[0:HEADS] + jnp.log2(mass[...])
    attT = r.attT

    out_load.wait()
    after = r.tok[...].astype(F32) + table_row + dot(attT[...].T, pool[0]) + row_of(r.v_out_bias)
    r.after[...] = after
    mean, inverse = norm_stats(after)
    norm_two = ((after - mean) * inverse * row_of(r.v_second_gain) + row_of(r.v_second_shift)).astype(BF)
    for half in range(2):
        pl.when(p.z < 3)(functools.partial(lambda half: nx_copy(0, half).wait_send(), half))
    r.norm_two[...] = norm_two
    r.norm_twoT[...] = norm_two.T
    r.total[...] = after + row_of(r.v_down_bias)
    r.t[...] = jnp.zeros((T, D), F32)

    g_down, g_up, g_out = r.g_down, r.g_up, r.g_out

    def scatter(name, parts, out, columns=None):
        return ReduceScatter(
            p,
            getattr(r, "g_" + name),
            getattr(r, "rc_" + name),
            getattr(r, "r1_" + name),
            getattr(r, "r2_" + name),
            getattr(r, "rz1_" + name),
            getattr(r, "rz2_" + name),
            getattr(r, "cs_" + name),
            getattr(r, "ss_" + name),
            parts,
            out,
            getattr(r, "zb_" + name, None),
            columns,
        )

    narrow, width = D // 4, D // 2
    down = scatter("down", "yx", r.s_down)
    up = scatter("up", "z", r.s_up)
    out = scatter("out", "", r.s_out, [(z * narrow, (z + 1) * narrow) for z in range(4)])
    queries, keys, values = [(i * width, (i + 1) * width) for i in range(3)]
    projs = [
        scatter("p0", "", lambda h, v: lay_out(0, h, v), (queries, keys, values, values)),
        scatter("p1", "", lambda h, v: lay_out(1, h, v), (queries, queries, keys, values)),
    ]
    layouts = (
        ((0, width, 0), (0, width, narrow), (0, narrow, width), (narrow, width, 0)),
        ((0, narrow, width), (narrow, width, 0), (0, width, 0), (0, width, narrow)),
    )

    def lay_out(chunk, h, value):
        for z, (first, last, at) in enumerate(layouts[chunk]):

            def store(first=first, last=last, at=at):
                r.s_qkv[h, :, at : at + last - first] = value[:, first:last]

            pl.when(p.z == z)(store)


    def spread(rows):
        table_grad = jnp.where(group_rows == gid, rows[0:1], 0.0)
        return jnp.concatenate([table_grad, rows[1:5]], axis=0)

    early = SmallSum(
        p, r.early_z, r.early_c, r.early_x, r.early_sems, r.early_out, lambda rows: rows
    )
    late = SmallSum(p, r.late_z, r.late_c, r.late_x, r.late_sems, r.late_out, spread)
    small = r.early_z.at[p.z]
    gelu_c = math.sqrt(2.0 / math.pi)

    def pass_on(k):
        down.core_sum(k)
        down.first_start(k)
        up.core_sum(k)
        up.first_start(k)

    def chunk(i, _):
        k = chunk_of(i)
        kh, kl = k // 2, lax.rem(k, 2)
        up_load(i).wait()
        pl.when(i >= 2)(lambda: act_grad(i))
        weight = pool[1 + i]
        weight_down = pool[4 + i]
        hidden = dot(r.norm_two[...], weight) + r.up_rows[pl.ds(k, 1), :]
        square = hidden * hidden
        th = jnp.tanh(gelu_c * hidden * (1.0 + 0.044715 * square))
        half = 0.5 + 0.5 * th
        act = (hidden * half).astype(BF)
        slope = half + 0.5 * hidden * (1.0 - th * th) * gelu_c * (1.0 + 3 * 0.044715 * square)
        grad = r.act_grad[lax.rem(i, 2)] * slope
        small[pl.ds(4 + k, 1), :] = column_sum(grad)
        low = grad.astype(BF)
        piece = D // 2
        for cc in range(2):
            rows = dot(r.cotT[...], act[:, cc * piece : (cc + 1) * piece]).astype(BF)
            part = D // 4
            for z in range(4):
                for h in range(2):
                    at = z * part + h * (part // 2)
                    g_down[h, kh, kl, cc, z // 2, z % 2] = rows[at : at + part // 2]
        down.core_start(k)
        part = D // 8
        for y in range(2):
            rows = dot(r.norm_twoT[y * 4 * part : (y + 1) * 4 * part], low).astype(BF)
            for d in range(4):
                for h in range(2):
                    at = d * part + h * (part // 2)
                    g_up[h, y, d // 2, d % 2, kh, kl] = rows[at : at + part // 2]
        up.core_start(k)
        pl.when(i > 0)(lambda: pass_on(chunk_of(i - 1)))
        r.total[...] += dot(act, weight_down)
        r.t[...] += dot_nt(low, weight)
        pl.when(i == 0)(lambda: up_load(3).start())
        return 0

    lax.fori_loop(0, 4, chunk, 0)
    pass_on(chunk_of(3))
    pl.when(p.z == 1)(functools.partial(q_pass, 1))

    qkv_loads = [
        load(r.qkv_weight.at[:, pl.ds(i * D, D)], pool.at[1 + i], 14 + i) for i in range(3)
    ]
    for copy in qkv_loads:
        copy.start()

    nx[2] = r.total[...].astype(BF)
    result_store = pltpu.make_async_copy(nx.at[2], r.result, r.load_sems.at[17])
    result_store.start()
    cot = r.cot[...].astype(F32)
    after = r.after[...]
    mean, inverse = norm_stats(after)
    n = (after - mean) * inverse
    t = r.t[...]
    after_grad = cot + norm_back(t, row_of(r.v_second_gain), n, inverse)
    r.after[...] = after_grad
    after_low = after_grad.astype(BF)
    doT = r.doT
    doT[...] = dot_nt(pool[0], after_low).astype(BF)
    for h in range(HEADS):
        rows = slice(h * HEAD, (h + 1) * HEAD)
        stat[HEADS + h : HEADS + h + 1] = column_sum(doT[rows].astype(F32) * outT[rows])
    def group_rows_of(group):
        return pl.ds(pl.multiple_of(group * width, width), width)

    def do_copy(t, group):
        rows = group_rows_of(group)
        src = doT.at[rows] if isinstance(t, int) and t == 0 else doin.at[t - 1, rows]
        return send(src, doin.at[t, rows], r.do_sems, 2 * t + group, p.along_z(-1))

    def stat_copy(t):
        src = stat if isinstance(t, int) and t == 0 else stat_in.at[t - 1]
        return send(src, stat_in.at[t], r.stat_sems, t, p.along_z(-1))

    def do_send(t, group):
        pl.when(group == 0)(lambda: stat_copy(t).start())
        do_copy(t, group).start()

    def stat_wait(t):
        send(stat, stat_in.at[t], r.stat_sems, t, p.along_z(1)).wait_recv()

    def do_wait(t, group):
        rows = group_rows_of(group)
        send(doT.at[rows], doin.at[t, rows], r.do_sems, 2 * t + group, p.along_z(1)).wait_recv()
        pl.when(group == 0)(lambda: stat_wait(t))

    for group in range(2):
        pl.when(p.z >= 1)(functools.partial(do_send, 0, group))
    small[pl.ds(0, 1), :] = column_sum(after_grad)
    small[pl.ds(1, 1), :] = column_sum(t * n)
    small[pl.ds(2, 1), :] = column_sum(t)
    small[pl.ds(3, 1), :] = column_sum(cot)
    rows = dot(attT[...], after_low).astype(BF)
    part = D // 8
    for d in range(8):
        for h in range(2):
            at = d * part + h * (part // 2)
            g_out[h, d // 4, (d // 2) % 2, d % 2] = rows[at : at + part // 2]
    out.core_start(0)

    outT[...] = jnp.zeros((D, T), F32)
    key_grad, value_grad = r.key_grad, r.value_grad
    mixed = (kv.at[1, 0], kv.at[1, 1], kv.at[2, 0])

    def grads_of(s, group, queries, out_grads, sums, causal, for_queries, for_keys):
        heads = [group * GROUP + i for i in range(GROUP)]
        places = [head_rows(h) for h in heads]
        scores = [dot_tn(kv[s, 0, rows], queries[rows]) for rows in places]
        prob_grad = [dot_tn(kv[s, 1, rows], out_grads[rows]) for rows in places]
        scores = [masked(v, p.z - s, causal) for v in scores]
        probs = [jnp.exp2(v - sums[pl.ds(h, 1)]) for v, h in zip(scores, heads)]
        score_grad = [
            (v * (w - sums[pl.ds(HEADS + h, 1)])).astype(BF)
            for v, w, h in zip(probs, prob_grad, heads)
        ]
        if for_queries:
            query_add = [dot(kv[s, 0, rows], v) for v, rows in zip(score_grad, places)]
        if for_keys:
            probs = [v.astype(BF) for v in probs]
            key_add = [dot_nt(queries[rows], v) for v, rows in zip(score_grad, places)]
            value_add = [dot_nt(out_grads[rows], v) for v, rows in zip(probs, places)]
        for i, rows in enumerate(places):
            if for_queries:
                outT[rows] = outT[rows] + query_add[i]
            if for_keys and for_queries:
                key_grad[rows] = key_add[i]
                value_grad[rows] = value_add[i]
            elif for_keys:
                key_grad[rows] = key_grad[rows] + key_add[i]
                value_grad[rows] = value_grad[rows] + value_add[i]

    def query_step(i, _):
        grads_of(p.z - i // 2, lax.rem(i, 2), qT, doT, stat, False, True, False)
        return 0

    def own_step(group, _):
        grads_of(0, group, qT, doT, stat, True, True, True)
        return 0

    def key_step(t, group):
        pl.when((p.z == 0) & (group == 0))(lambda: q_wait(t))
        do_wait(t, group)
        pl.when(p.z >= 1)(lambda: do_send(t + 1, group))
        grads_of(0, group, qin.at[t], doin.at[t], stat_in.at[t], False, False, True)

    def proj_grad(group):
        rows = slice(group * width, (group + 1) * width)
        mixed[0][rows] = (outT[rows] * HEAD**-0.5).astype(BF)
        mixed[1][rows] = (key_grad[rows] * HEAD**-0.5).astype(BF)
        mixed[2][rows] = value_grad[rows].astype(BF)
        target = (r.g_p0, r.g_p1)[group]
        part = D // 8
        for i in range(3):
            piece = dot_nt(nxT[...], mixed[i][rows]).astype(BF)
            for d in range(8):
                for h in range(2):
                    at = d * part + h * (part // 2)
                    target[h, d // 4, (d // 2) % 2, d % 2, :, i * width : (i + 1) * width] = piece[
                        at : at + part // 2
                    ]
        projs[group].core_start(0)

    def norm_back_one():
        outT[...] = sum(dot(pool[1 + i], mixed[i][...]) for i in range(3))
        ones = jnp.ones((8, T), BF)
        rows = r.late_z.at[p.z]
        rows[pl.ds(3, 1), :] = dot_nt(ones, mixed[0][...])[0:1]
        rows[pl.ds(4, 1), :] = dot_nt(ones, mixed[2][...])[0:1]
        t1 = outT[...].T
        start = r.tok[...].astype(F32) + table_row
        mean, inverse = norm_stats(start)
        n = (start - mean) * inverse
        start_grad = r.after[...] + norm_back(t1, row_of(r.v_first_gain), n, inverse)
        r.norm_two[...] = start_grad.astype(BF)
        tokens_store.start()
        rows[pl.ds(0, 1), :] = column_sum(start_grad)
        rows[pl.ds(1, 1), :] = column_sum(t1 * n)
        rows[pl.ds(2, 1), :] = column_sum(t1)
        late.advance(0)

    tokens_store = pltpu.make_async_copy(r.norm_two, r.grad_tokens, r.load_sems.at[18])

    for copy in qkv_loads:
        copy.wait()
    lax.fori_loop(0, 2 * p.z, query_step, 0)
    lax.fori_loop(0, 2, own_step, 0)
    step = functools.partial

    ahead = (
        (
            (0, step(early.advance, 0)),
            (3, step(down.advance, 1)),
            (3, step(down.advance, 2)),
            (3, step(up.advance, 1)),
            (5, step(proj_grad, 0)),
        ),
        (
            (0, step(down.advance, 1)),
            (3, step(proj_grad, 0)),
        ),
        (
        ),
        (
        ),
    )
    rest = (
        ((), step(proj_grad, 1)),
        ((0, 1), step(down.advance, 1)),
        ((0, 1), step(proj_grad, 0)),
        ((0,), step(up.advance, 1)),
        ((), step(projs[0].advance, 0)),
        ((0,), step(early.advance, 0)),
        ((), norm_back_one),
        ((0,), step(down.advance, 2)),
        ((), step(projs[1].advance, 0)),
        ((), step(up.advance, 2)),
        ((), step(down.advance, 3)),
        ((), step(projs[0].advance, 1)),
        ((), step(projs[1].advance, 1)),
        ((), step(up.advance, 3)),
        ((), step(projs[0].advance, 2)),
        ((), step(out.advance, 0)),
        ((), step(projs[1].advance, 2)),
        ((), step(out.advance, 1)),
        ((), step(down.advance, 4)),
        ((), step(projs[0].advance, 3)),
        ((), step(early.advance, 1)),
        ((), step(late.advance, 1)),
        ((), step(out.advance, 2)),
        ((), step(late.advance, 2)),
        ((), step(projs[1].advance, 3)),
        ((), step(early.advance, 2)),
        ((), step(out.advance, 3)),
        ((), step(up.advance, 4)),
        ((), step(projs[1].advance, 4)),
        ((), step(late.advance, 3)),
        ((), step(projs[0].advance, 4)),
        ((), step(early.advance, 3)),
        ((), step(out.advance, 4)),
    )

    def half_round(i, _):
        for z in range(3):
            for at, one in ahead[z]:
                pl.when((p.z == z) & (i == at))(one)
        pl.when(p.z + i // 2 < 3)(lambda: key_step(i // 2, lax.rem(i, 2)))
        return 0

    for _, one in ahead[3]:
        pl.when(p.z == 3)(one)
    lax.fori_loop(0, 7, half_round, 0)
    for done, one in rest:
        if len(done) == 0:
            one()
        else:
            planes = [z for z in range(4) if z not in done]
            if planes:
                pl.when(functools.reduce(jnp.logical_or, [p.z == z for z in planes]))(one)
    for s in (1, 2):
        for half in range(2):
            pl.when((p.z < 3) & (p.z >= s))(lambda s=s, half=half: nx_copy(s, half).wait_send())
    def sent(t):
        q_copy(t).wait_send()
        stat_copy(t).wait_send()
        do_copy(t, 0).wait_send()
        do_copy(t, 1).wait_send()

    for t in range(3):
        pl.when((p.z >= 1) & (p.z + t <= 3))(functools.partial(sent, t))
    result_store.wait()
    tokens_store.wait()

def row_of(ref):
    return ref[...].reshape(1, ref.shape[0])


def outputs_kernel(result, grad_tokens, early, late, s_qkv, s_out, s_up, s_down, *outs):
    (
        o_result,
        o_tokens,
        o_table,
        o_first_gain,
        o_first_shift,
        o_qkv,
        o_qv_bias,
        o_out,
        o_out_bias,
        o_second_gain,
        o_second_shift,
        o_up,
        o_up_bias,
        o_down,
        o_down_bias,
    ) = outs
    D = early.shape[1]
    o_result[...] = result[...].reshape(o_result.shape)
    o_tokens[...] = grad_tokens[...].reshape(o_tokens.shape)
    o_table[...] = late[0:16]
    o_first_gain[...] = late[16]
    o_first_shift[...] = late[17]
    o_out_bias[...] = early[0]
    o_second_gain[...] = early[1]
    o_second_shift[...] = early[2]
    o_down_bias[...] = early[3]
    for k in range(4):
        o_up_bias[pl.ds(k * D, D)] = early[4 + k]
    o_qv_bias[...] = late[18:20]
    for ref, value in ((o_qkv, s_qkv), (o_out, s_out), (o_up, s_up), (o_down, s_down)):
        half = value.shape[1]
        for h in range(2):
            ref[h * half : (h + 1) * half] = value[h]


def fused(
    tokens,
    group_ids,
    lengths,
    cotangent,
    group_table,
    first_gain,
    first_shift,
    qkv_weight,
    query_value_bias,
    out_weight,
    out_bias,
    second_gain,
    second_shift,
    up_weight,
    up_bias,
    down_weight,
    down_bias,
):
    _, T, D = tokens.shape
    F = up_weight.shape[1]
    any_spec = pl.BlockSpec(memory_space=pl.ANY)
    vmem = pl.BlockSpec(memory_space=pltpu.VMEM)
    smem = pl.BlockSpec(memory_space=pltpu.SMEM)
    inputs = dict(
        tokens=(tokens.reshape(T, D), any_spec),
        group_ids=(group_ids, smem),
        lengths=(lengths, smem),
        cotangent=(cotangent.reshape(T, D), any_spec),
        group_table=(group_table, any_spec),
        first_gain=(first_gain, any_spec),
        first_shift=(first_shift, any_spec),
        qkv_weight=(qkv_weight, any_spec),
        qv_bias=(query_value_bias, any_spec),
        out_weight=(out_weight, any_spec),
        out_bias=(out_bias, any_spec),
        second_gain=(second_gain, any_spec),
        second_shift=(second_shift, any_spec),
        up_weight=(up_weight, any_spec),
        up_bias=(up_bias, any_spec),
        down_weight=(down_weight, any_spec),
        down_bias=(down_bias, any_spec),
    )
    shares = dict(
        down=(D // 8, F // 8),
        up=(D // 16, F // 4),
        out=(D // 16, D // 4),
        qkv=(D // 16, 3 * D // 4),
    )
    outputs = dict(
        result=((T, D), BF),
        grad_tokens=((T, D), BF),
        early_out=((8, D), F32),
        late_out=((20, D), F32),
    )
    outputs.update({"s_" + k: ((2,) + shares[k], F32) for k in ("qkv", "out", "up", "down")})
    dma = pltpu.SemaphoreType.DMA
    scratch = dict(
        pool=pltpu.VMEM((8, D, D), BF),
        v_group_table=pltpu.VMEM(group_table.shape, F32),
        v_first_gain=pltpu.VMEM((D,), F32),
        v_first_shift=pltpu.VMEM((D,), F32),
        v_qv_bias=pltpu.VMEM((2, D), F32),
        v_out_bias=pltpu.VMEM((D,), F32),
        v_second_gain=pltpu.VMEM((D,), F32),
        v_second_shift=pltpu.VMEM((D,), F32),
        v_up_bias=pltpu.VMEM((F,), F32),
        v_down_bias=pltpu.VMEM((D,), F32),
        tok=pltpu.VMEM((T, D), BF),
        cot=pltpu.VMEM((T, D), BF),
        cotT=pltpu.VMEM((D, T), BF),
        nx=pltpu.VMEM((3, T, D), BF),
        nxT=pltpu.VMEM((D, T), BF),
        qT=pltpu.VMEM((D, T), BF),
        kv=pltpu.VMEM((4, 2, D, T), BF),
        outT=pltpu.VMEM((D, T), F32),
        stat=pltpu.VMEM((2 * HEADS, T), F32),
        mass=pltpu.VMEM((HEADS, T), F32),
        qin=pltpu.VMEM((3, D, T), BF),
        doin=pltpu.VMEM((3, D, T), BF),
        stat_in=pltpu.VMEM((3, 2 * HEADS, T), F32),
        key_grad=pltpu.VMEM((D, T), F32),
        value_grad=pltpu.VMEM((D, T), F32),
        attT=pltpu.VMEM((D, T), BF),
        after=pltpu.VMEM((T, D), F32),
        norm_two=pltpu.VMEM((T, D), BF),
        norm_twoT=pltpu.VMEM((D, T), BF),
        act_grad=pltpu.VMEM((2, T, D), F32),
        total=pltpu.VMEM((T, D), F32),
        t=pltpu.VMEM((T, D), F32),
        doT=pltpu.VMEM((D, T), BF),
        up_rows=pltpu.VMEM((4, D), F32),
        early_z=pltpu.VMEM((4, 8, D), F32),
        early_c=pltpu.VMEM((2, 8, D), F32),
        early_x=pltpu.VMEM((4, 8, D), F32),
        late_z=pltpu.VMEM((4, 5, D), F32),
        late_c=pltpu.VMEM((2, 20, D), F32),
        late_x=pltpu.VMEM((4, 20, D), F32),
        load_sems=dma((29,)),
        nx_sems=dma((2, 6)),
        q_sems=dma((2, 3)),
        do_sems=dma((2, 6)),
        stat_sems=dma((2, 3)),
        early_sems=dma((2, 7)),
        late_sems=dma((2, 7)),
    )
    places = dict(
        down=(2, 2, D // 8, F // 8),
        up=(2, 2, D // 16, F // 4),
        out=(D // 16, D),
        p0=(D // 16, 3 * D // 2),
        p1=(D // 16, 3 * D // 2),
    )
    columns_of = dict(shares, p0=(D // 16, D // 2), p1=(D // 16, D // 2))
    for name, place in places.items():
        rows, columns = columns_of[name]
        extra = {
            "g_" + name: pltpu.VMEM((2, 2, 2, 2) + place, BF),
            "rc_" + name: pltpu.VMEM((2, 2, 2) + place, BF),
            "r1_" + name: pltpu.VMEM((2, 2) + place, BF),
            "r2_" + name: pltpu.VMEM((2,) + place, BF),
            "rz1_" + name: pltpu.VMEM((2, 2, rows, columns), BF),
            "rz2_" + name: pltpu.VMEM((2, rows, columns), BF),
            "cs_" + name: dma((2, 4)),
            "ss_" + name: dma((2, 12)),
        }
        if len(place) == 2:
            extra["zb_" + name] = pltpu.VMEM((2, 2, 2, rows, columns), BF)
        scratch.update(extra)
    names = list(inputs) + list(outputs) + list(scratch)
    done = pl.pallas_call(
        functools.partial(layer_kernel, names),
        name="layer",
        out_shape=[jax.ShapeDtypeStruct(*o) for o in outputs.values()],
        in_specs=[i[1] for i in inputs.values()],
        out_specs=[any_spec] * 2 + [vmem] * (len(outputs) - 2),
        scratch_shapes=list(scratch.values()),
        compiler_params=pltpu.CompilerParams(
            collective_id=0, has_side_effects=True, vmem_limit_bytes=VMEM_LIMIT
        ),
    )(*[i[0] for i in inputs.values()])
    shape = jax.ShapeDtypeStruct
    outs = pl.pallas_call(
        outputs_kernel,
        name="outputs",
        out_shape=[
            shape((1, T, D), BF),
            shape((1, T, D), BF),
            shape((16, D), F32),
            shape((D,), F32),
            shape((D,), F32),
            shape((D // 8, 3 * D // 4), F32),
            shape((2, D), F32),
            shape((D // 8, D // 4), F32),
            shape((D,), F32),
            shape((D,), F32),
            shape((D,), F32),
            shape((D // 8, F // 4), F32),
            shape((F,), F32),
            shape((D // 4, F // 8), F32),
            shape((D,), F32),
        ],
        in_specs=[vmem] * len(done),
        out_specs=[vmem] * 15,
    )(*done)
    return (*outs[:13], outs[13].T, outs[14])


def shifted(array, axis, by):
    devices = lax.axis_size(axis)
    pairs = [(i, i + by) for i in range(devices) if 0 <= i + by < devices]
    return lax.ppermute(array, axis, pairs)


def as_sent(array):
    return jax.tree.map(lambda a: a.astype(jnp.bfloat16) if a.dtype == jnp.float32 else a, array)


def shifted_2(block, axis, distance):
    devices = range(lax.axis_size(axis))
    route = [((i - distance) % len(devices), i) for i in devices]
    return lax.ppermute(block, axis, route)


def layer_norm(inputs, norm_gain, norm_shift):
    average = jnp.mean(inputs, -1, keepdims=True)
    centred = inputs - average
    inverse = lax.rsqrt(jnp.mean(centred * centred, -1, keepdims=True) + EPSILON)
    return centred * inverse * norm_gain + norm_shift


def tanh_gelu(inputs):
    return jax.nn.gelu(inputs, approximate=True)


def keep_same(state_value):
    return state_value


def scores_of(queries, key_piece, key_start, query_start, lengths):
    sequences, block_len = (queries.shape[0], queries.shape[1])
    key_heads = key_piece.reshape(sequences, key_piece.shape[1], HEADS, HEAD)
    raw_scores = jnp.einsum(
        "gqhe,gkhe->ghqk", queries, key_heads, preferred_element_type=jnp.float32
    ) * HEAD ** (-0.5)
    key_pos = key_start + jnp.arange(key_piece.shape[1])
    query_pos = query_start + jnp.arange(block_len)
    allowed = (query_pos[:, None] >= key_pos[None, :])[None] & (
        key_pos[None, None, :] < lengths[:, None, None]
    )
    return (raw_scores, allowed[:, None])


def plain(
    tokens,
    group_ids,
    lengths,
    cotangent,
    group_table,
    first_gain,
    first_shift,
    qkv_weight,
    query_value_bias,
    out_weight,
    out_bias,
    second_gain,
    second_shift,
    up_weight,
    up_bias,
    down_weight,
    down_bias,
):
    sequences, block_len, features = tokens.shape
    token_rows = sequences * block_len
    seq_count = lax.axis_size("seq")
    seq_index = lax.axis_index("seq")
    query_start = seq_index * block_len
    score_scale = HEAD ** (-0.5)
    one_hot = (group_ids[:, None] == jnp.arange(group_table.shape[0])[None, :]).astype(jnp.float32)
    table_rows = jnp.dot(one_hot, group_table, precision=EXACT)
    start_rows = (tokens.astype(jnp.float32) + table_rows[:, None, :]).reshape(token_rows, features)
    norm_one, pull_one = jax.vjp(layer_norm, start_rows, first_gain, first_shift)
    norm_one_low = norm_one.astype(jnp.bfloat16)
    full_bias = jnp.concatenate(
        [query_value_bias[0], jnp.zeros((features,), jnp.float32), query_value_bias[1]]
    )
    mixed_rows = (
        jnp.dot(norm_one_low, qkv_weight, preferred_element_type=jnp.float32) + full_bias
    ).astype(jnp.bfloat16)
    mixed_rows = mixed_rows.reshape(sequences, block_len, 3 * features)
    queries = mixed_rows[:, :, :features].reshape(sequences, block_len, HEADS, HEAD)
    key_rows = mixed_rows[:, :, features : 2 * features]
    values = mixed_rows[:, :, 2 * features :]
    pieces = []
    current = (key_rows, values)
    for cycle_step in range(seq_count):
        if cycle_step > 0:
            current = shifted((current[0], current[1]), "seq", 1)
        anchor = (seq_index - cycle_step) % seq_count
        pieces.append((current[0], current[1], anchor * block_len, cycle_step <= seq_index))
    shape_rows = (sequences, HEADS, block_len)
    row_max = jnp.full(shape_rows, NEG_LARGE, jnp.float32)
    row_sum = jnp.zeros(shape_rows, jnp.float32)
    stored = []
    for key_piece, value_piece, key_start, active in pieces:

        def visit_block(state_pair, key_piece=key_piece, key_start=key_start):
            raw_scores, allowed = scores_of(queries, key_piece, key_start, query_start, lengths)
            masked_scores = jnp.where(allowed, raw_scores, NEG_LARGE)
            new_max = jnp.maximum(state_pair[0], jnp.max(masked_scores, -1))
            weights = jnp.where(allowed, jnp.exp(masked_scores - new_max[..., None]), 0.0)
            return (
                new_max,
                state_pair[1] * jnp.exp(state_pair[0] - new_max) + jnp.sum(weights, -1),
                masked_scores,
            )

        def pass_block(state_pair):
            return (
                state_pair[0],
                state_pair[1],
                jnp.full(shape_rows + (block_len,), NEG_LARGE, jnp.float32),
            )

        row_max, row_sum, masked_scores = lax.cond(
            active, visit_block, pass_block, (row_max, row_sum)
        )
        stored.append(masked_scores)
    log_sum = row_max + jnp.log(row_sum)
    attended = jnp.zeros((sequences, block_len, HEADS, HEAD), jnp.float32)
    for piece_data, masked_scores in zip(pieces, stored):

        def attend_block(total_out, value_piece=piece_data[1], masked_scores=masked_scores):
            probs = jnp.exp(masked_scores - log_sum[..., None]).astype(jnp.bfloat16)
            value_heads = value_piece.reshape(sequences, block_len, HEADS, HEAD)
            return total_out + jnp.einsum(
                "ghqk,gkhe->gqhe", probs, value_heads, preferred_element_type=jnp.float32
            )

        attended = lax.cond(piece_data[3], attend_block, keep_same, attended)
    attended_low = attended.reshape(token_rows, features).astype(jnp.bfloat16)
    after_attn = (
        start_rows
        + jnp.dot(attended_low, out_weight, preferred_element_type=jnp.float32)
        + out_bias
    )
    norm_two, pull_two = jax.vjp(layer_norm, after_attn, second_gain, second_shift)
    norm_two_low = norm_two.astype(jnp.bfloat16)
    up_rows = jnp.dot(norm_two_low, up_weight, preferred_element_type=jnp.float32) + up_bias
    activated, pull_gelu = jax.vjp(tanh_gelu, up_rows)
    activated_low = activated.astype(jnp.bfloat16)
    result_rows = (
        after_attn
        + jnp.dot(activated_low, down_weight, preferred_element_type=jnp.float32)
        + down_bias
    )
    result = result_rows.astype(jnp.bfloat16).reshape(tokens.shape)
    outer_low = cotangent.reshape(token_rows, features)
    outer_grad = outer_low.astype(jnp.float32)
    grad_down_weight = jnp.dot(activated_low.T, outer_low, preferred_element_type=jnp.float32)
    grad_down_bias = jnp.sum(outer_grad, 0)
    up_grad = pull_gelu(jnp.dot(outer_low, down_weight.T, preferred_element_type=jnp.float32))[0]
    grad_up_bias = jnp.sum(up_grad, 0)
    up_low = up_grad.astype(jnp.bfloat16)
    grad_up_weight = jnp.dot(norm_two_low.T, up_low, preferred_element_type=jnp.float32)
    part_after, grad_second_gain, grad_second_shift = pull_two(
        jnp.dot(up_low, up_weight.T, preferred_element_type=jnp.float32)
    )
    after_grad = outer_grad + part_after
    grad_out_bias = jnp.sum(after_grad, 0)
    after_low = after_grad.astype(jnp.bfloat16)
    grad_out_weight = jnp.dot(attended_low.T, after_low, preferred_element_type=jnp.float32)
    out_grad = jnp.dot(after_low, out_weight.T, preferred_element_type=jnp.float32).astype(
        jnp.bfloat16
    )
    out_grad = out_grad.reshape(sequences, block_len, HEADS, HEAD)
    delta = jnp.transpose(jnp.sum(out_grad.astype(jnp.float32) * attended, -1), (0, 2, 1))

    def back_block(query_grad, key_piece, value_piece, key_start):
        raw_scores, allowed = scores_of(queries, key_piece, key_start, query_start, lengths)
        probs = jnp.where(allowed, jnp.exp(raw_scores - log_sum[..., None]), 0.0)
        value_heads = value_piece.reshape(sequences, block_len, HEADS, HEAD)
        key_heads = key_piece.reshape(sequences, block_len, HEADS, HEAD)
        prob_grad = jnp.einsum(
            "gqhe,gkhe->ghqk", out_grad, value_heads, preferred_element_type=jnp.float32
        )
        score_grad = (probs * (prob_grad - delta[..., None])).astype(jnp.bfloat16)
        query_grad = (
            query_grad
            + jnp.einsum(
                "ghqk,gkhe->gqhe", score_grad, key_heads, preferred_element_type=jnp.float32
            )
            * score_scale
        )
        key_add = (
            jnp.einsum("ghqk,gqhe->gkhe", score_grad, queries, preferred_element_type=jnp.float32)
            * score_scale
        )
        value_add = jnp.einsum(
            "ghqk,gqhe->gkhe",
            probs.astype(jnp.bfloat16),
            out_grad,
            preferred_element_type=jnp.float32,
        )
        return (
            query_grad,
            key_add.reshape(sequences, block_len, features),
            value_add.reshape(sequences, block_len, features),
        )

    empty_rows = jnp.zeros((sequences, block_len, features), jnp.float32)

    def skip_back(query_grad):
        return (query_grad, empty_rows, empty_rows)

    query_grad = jnp.zeros((sequences, block_len, HEADS, HEAD), jnp.float32)
    carried = (empty_rows, empty_rows)
    for cycle_step in range(seq_count):
        piece_data = pieces[cycle_step]

        def visit_back(state_grad, piece_data=piece_data):
            return back_block(state_grad, piece_data[0], piece_data[1], piece_data[2])

        query_grad, key_add, value_add = lax.cond(piece_data[3], visit_back, skip_back, query_grad)
        carried = shifted_2(
            (as_sent(carried[0] + key_add), as_sent(carried[1] + value_add)), "seq", 1
        )
    key_grad, value_grad = carried
    query_flat = query_grad.reshape(token_rows, features)
    key_flat = key_grad.reshape(token_rows, features)
    value_flat = value_grad.reshape(token_rows, features)
    grad_query_value_bias = jnp.stack([jnp.sum(query_flat, 0), jnp.sum(value_flat, 0)])
    mixed_grad = jnp.concatenate([query_flat, key_flat, value_flat], -1).astype(jnp.bfloat16)
    grad_qkv_weight = jnp.dot(norm_one_low.T, mixed_grad, preferred_element_type=jnp.float32)
    part_start, grad_first_gain, grad_first_shift = pull_one(
        jnp.dot(mixed_grad, qkv_weight.T, preferred_element_type=jnp.float32)
    )
    start_grad = after_grad + part_start
    grad_tokens = start_grad.astype(jnp.bfloat16).reshape(tokens.shape)
    grad_group_table = jnp.dot(
        one_hot.T, jnp.sum(start_grad.reshape(sequences, block_len, features), 1), precision=EXACT
    )
    small_sums = lax.psum(
        (
            grad_group_table,
            grad_first_gain,
            grad_first_shift,
            grad_query_value_bias,
            grad_out_bias,
            grad_second_gain,
            grad_second_shift,
            grad_up_bias,
            grad_down_bias,
        ),
        ("dp", "seq"),
    )
    matrices = (grad_qkv_weight, grad_out_weight, grad_up_weight, grad_down_weight)
    shares = (
        lax.psum_scatter(
            matrices[0].astype(jnp.bfloat16), "seq", scatter_dimension=1, tiled=True
        ).astype(jnp.float32),
        lax.psum_scatter(
            matrices[1].astype(jnp.bfloat16), "seq", scatter_dimension=1, tiled=True
        ).astype(jnp.float32),
        lax.psum_scatter(
            matrices[2].astype(jnp.bfloat16), "seq", scatter_dimension=1, tiled=True
        ).astype(jnp.float32),
        lax.psum_scatter(
            matrices[3].astype(jnp.bfloat16), "seq", scatter_dimension=1, tiled=True
        ).astype(jnp.float32),
    )
    shares = (
        lax.psum_scatter(
            shares[0].astype(jnp.bfloat16), "dp", scatter_dimension=0, tiled=True
        ).astype(jnp.float32),
        lax.psum_scatter(
            shares[1].astype(jnp.bfloat16), "dp", scatter_dimension=0, tiled=True
        ).astype(jnp.float32),
        lax.psum_scatter(
            shares[2].astype(jnp.bfloat16), "dp", scatter_dimension=0, tiled=True
        ).astype(jnp.float32),
        lax.psum_scatter(
            shares[3].astype(jnp.bfloat16), "dp", scatter_dimension=0, tiled=True
        ).astype(jnp.float32),
    )
    return (
        result,
        grad_tokens,
        small_sums[0],
        small_sums[1],
        small_sums[2],
        shares[0],
        small_sums[3],
        shares[1],
        small_sums[4],
        small_sums[5],
        small_sums[6],
        shares[2],
        small_sums[7],
        shares[3],
        small_sums[8],
    )


def solution(mesh):
    in_specs = (
        P("dp", "seq", None),
        P("dp"),
        P("dp"),
        P("dp", "seq", None),
        P(),
        P(),
        P(),
        P(),
        P(),
        P(),
        P(),
        P(),
        P(),
        P(),
        P(),
        P(),
        P(),
    )
    out_specs = (
        P("dp", "seq", None),
        P("dp", "seq", None),
        P(),
        P(),
        P(),
        P("dp", "seq"),
        P(),
        P("dp", "seq"),
        P(),
        P(),
        P(),
        P("dp", "seq"),
        P(),
        P("dp", "seq"),
        P(),
    )
    def shards(*arrays):
        sizes = (mesh.shape["dp"], mesh.shape["seq"]) + arrays[0].shape
        return (fused if sizes == (8, 4, 1, 256, 768) else plain)(*arrays)

    return jax.shard_map(shards, mesh=mesh, in_specs=in_specs, out_specs=out_specs, check_vma=False)
```

```python
import functools
import math
import types

import jax
import jax.numpy as jnp
from jax import lax
from jax.experimental import pallas as pl
from jax.experimental.pallas import tpu as pltpu
from jax.sharding import PartitionSpec as P

HEADS = 12
HEAD = 64


EPSILON = 1e-05
NEG_LARGE = -1e30
EXACT = lax.Precision.HIGHEST


VMEM_LIMIT = 64 << 20
GROUP = 6


BF = jnp.bfloat16
VECTORS = (
    "group_table",
    "first_gain",
    "first_shift",
    "qv_bias",
    "out_bias",
    "second_gain",
    "second_shift",
    "up_bias",
    "down_bias",
)
F32 = jnp.float32
MESH = pl.DeviceIdType.MESH
LOG2E = 1.4426950408889634


def dot(a, b):
    return lax.dot_general(a, b, (((1,), (0,)), ((), ())), preferred_element_type=F32)


def dot_nt(a, b):
    return lax.dot_general(a, b, (((1,), (1,)), ((), ())), preferred_element_type=F32)


def dot_tn(a, b):
    return lax.dot_general(a, b, (((0,), (0,)), ((), ())), preferred_element_type=F32)


def flipped(index, bit):
    return index + bit - 2 * bit * lax.rem(index // bit, 2)


class Place:
    def __init__(self):
        self.d = lax.axis_index("dp")
        self.z = lax.axis_index("seq")
        self.c = lax.rem(self.d, 2)
        self.x = lax.rem(self.d // 2, 2)
        self.y = lax.rem(self.d // 4, 2)
        self.zl = lax.rem(self.z, 2)
        self.zh = lax.rem(self.z // 2, 2)
        self.core = (flipped(self.d, 1), self.z)
        self.along_x = (flipped(self.d, 2), self.z)
        self.along_y = (flipped(self.d, 4), self.z)
        self.z_near = (self.d, flipped(self.z, 1))
        self.z_far = (self.d, flipped(self.z, 2))
        self.z_mirror = (self.d, 3 - self.z)
        self.diagonal = (flipped(flipped(self.d, 2), 4), self.z)

    def along_z(self, k):
        return (self.d, self.z + k)


def send(src, dst, sems, index, to):
    copy = pltpu.make_async_remote_copy(
        src_ref=src,
        dst_ref=dst,
        send_sem=sems.at[0, index],
        recv_sem=sems.at[1, index],
        device_id=to,
        device_id_type=MESH,
    )
    return copy


class ReduceScatter:
    def __init__(
        self, place, g, rc, r1, r2, rz1, rz2, core_sems, sems, parts, out, zb=None, columns=None
    ):
        self.p, self.g, self.rc, self.r1, self.r2 = place, g, rc, r1, r2
        self.rz1, self.rz2, self.core_sems, self.sems, self.parts = rz1, rz2, core_sems, sems, parts
        self.count = 4 if parts else 1
        self.out, self.columns = out, columns
        self.zb = g.at[:, place.y, place.x, place.c] if zb is None else zb

    def core_copy(self, k):
        p = self.p
        kh, kl = k // 2, lax.rem(k, 2)
        if self.parts == "yx":
            src, dst = self.g.at[:, kh, kl, 1 - p.c], self.rc.at[:, kh, kl]
        elif self.parts == "z":
            src, dst = self.g.at[:, :, :, 1 - p.c, kh, kl], self.rc.at[:, :, :, kh, kl]
        else:
            src, dst = self.g.at[:, :, :, 1 - p.c], self.rc
        return send(src, dst, self.core_sems, k, p.core)

    def core_start(self, k):
        self.core_copy(k).start()

    def core_sum(self, k):
        p, g, rc = self.p, self.g, self.rc
        kh, kl = k // 2, lax.rem(k, 2)
        self.core_copy(k).wait()
        if self.parts == "yx":
            for h in range(2):
                g[h, kh, kl, p.c] = g[h, kh, kl, p.c] + rc[h, kh, kl]
            return

        def add(i, _):
            h, y, x = i // 4, lax.rem(i // 2, 2), lax.rem(i, 2)
            if self.parts == "z":
                g[h, y, x, p.c, kh, kl] = g[h, y, x, p.c, kh, kl] + rc[h, y, x, kh, kl]
            else:
                g[h, y, x, p.c] = g[h, y, x, p.c] + rc[h, y, x]
            return 0

        lax.fori_loop(0, 8, add, 0)

    def first_x(self, k):
        p, g, r1 = self.p, self.g, self.r1
        kh, kl = k // 2, lax.rem(k, 2)
        if self.parts == "yx":
            return send(g.at[0, kh, 1 - p.x, p.c], r1.at[0, kh], self.sems, kh, p.along_x)
        if self.parts == "z":
            return send(
                g.at[0, :, 1 - p.x, p.c, kh, kl], r1.at[0, :, kh, kl], self.sems, k, p.along_x
            )
        return send(g.at[0, :, 1 - p.x, p.c], r1.at[0], self.sems, 0, p.along_x)

    def first_y(self, k):
        p, g, r1 = self.p, self.g, self.r1
        kh, kl = k // 2, lax.rem(k, 2)
        if self.parts == "yx":
            return send(g.at[1, 1 - p.y, kl, p.c], r1.at[1, kl], self.sems, 4 + kl, p.along_y)
        if self.parts == "z":
            return send(
                g.at[1, 1 - p.y, :, p.c, kh, kl], r1.at[1, :, kh, kl], self.sems, 4 + k, p.along_y
            )
        return send(g.at[1, 1 - p.y, :, p.c], r1.at[1], self.sems, 4, p.along_y)

    def first_start(self, k):
        p = self.p
        if self.parts == "yx":
            pl.when(lax.rem(k, 2) != p.x)(lambda: self.first_x(k).start())
            pl.when(k // 2 != p.y)(lambda: self.first_y(k).start())
        else:
            self.first_x(k).start()
            self.first_y(k).start()

    def first_sum(self):
        p, g = self.p, self.g
        if self.parts == "yx":
            for i in range(2):
                self.first_x(2 * i).wait()
                self.first_y(i).wait()
        else:
            for k in range(self.count):
                self.first_x(k).wait()
                self.first_y(k).wait()
        for i in range(2):
            g[0, i, p.x, p.c] = g[0, i, p.x, p.c] + self.r1[0, i]
            g[1, p.y, i, p.c] = g[1, p.y, i, p.c] + self.r1[1, i]

    def second_copies(self):
        p, g = self.p, self.g
        return (
            send(g.at[0, 1 - p.y, p.x, p.c], self.r2.at[0], self.sems, 8, p.along_y),
            send(g.at[1, p.y, 1 - p.x, p.c], self.r2.at[1], self.sems, 9, p.along_x),
        )

    def second_start(self):
        for copy in self.second_copies():
            copy.start()

    def second_sum(self):
        p, g = self.p, self.g
        for copy in self.second_copies():
            copy.wait()
        for h in range(2):
            total = g[h, p.y, p.x, p.c] + self.r2[h]
            if self.columns is None:
                g[h, p.y, p.x, p.c] = total
            else:
                for z, (first, last) in enumerate(self.columns):
                    self.zb[h, z // 2, z % 2] = total[:, first:last]

    def third_copy(self):
        p = self.p
        return send(self.zb.at[:, :, 1 - p.zl], self.rz1, self.sems, 10, p.z_near)

    def third_start(self):
        self.third_copy().start()

    def third_sum(self):
        p, zb = self.p, self.zb
        self.third_copy().wait()
        for h in range(2):
            for i in range(2):
                zb[h, i, p.zl] = zb[h, i, p.zl] + self.rz1[h, i]

    def fourth_copy(self):
        p = self.p
        return send(self.zb.at[:, 1 - p.zh, p.zl], self.rz2, self.sems, 11, p.z_far)

    def fourth_start(self):
        self.fourth_copy().start()

    def fourth_sum(self):
        p, zb = self.p, self.zb
        self.fourth_copy().wait()
        for h in range(2):
            total = zb[h, p.zh, p.zl].astype(F32) + self.rz2[h].astype(F32)
            if callable(self.out):
                self.out(h, total)
            else:
                self.out[h] = total

    def advance(self, step):
        if step == 0:
            self.core_sum(0)
            self.first_start(0)
        elif step == 1:
            self.first_sum()
            self.second_start()
        elif step == 2:
            self.second_sum()
            self.third_start()
        elif step == 3:
            self.third_sum()
            self.fourth_start()
        else:
            self.fourth_sum()


class SmallSum:
    def __init__(self, place, zin, cin, xin, sems, out, spread):
        self.p, self.zin, self.cin, self.xin, self.sems = place, zin, cin, xin, sems
        self.out, self.spread = out, spread
        self.corner = place.d // 2

    def z_copies(self):
        p, mine = self.p, self.zin.at[self.p.z]
        peers = (p.z_near, p.z_far, p.z_mirror)
        return [send(mine, mine, self.sems, i, to) for i, to in enumerate(peers)]

    def core_copy(self):
        return send(self.cin.at[0], self.cin.at[1], self.sems, 3, self.p.core)

    def xy_copies(self):
        p, mine = self.p, self.xin.at[self.corner]
        peers = (p.along_x, p.along_y, p.diagonal)
        return [send(mine, mine, self.sems, 4 + i, to) for i, to in enumerate(peers)]

    def advance(self, step):
        cin, zin, xin = self.cin, self.zin, self.xin
        if step == 0:
            for copy in self.z_copies():
                copy.start()
        elif step == 1:
            for copy in self.z_copies():
                copy.wait()
            cin[0] = self.spread(zin[0] + zin[1] + zin[2] + zin[3])
            self.core_copy().start()
        elif step == 2:
            self.core_copy().wait()
            xin[self.corner] = cin[0] + cin[1]
            for copy in self.xy_copies():
                copy.start()
        else:
            for copy in self.xy_copies():
                copy.wait()
            self.out[...] = xin[0] + xin[1] + xin[2] + xin[3]


def norm_stats(v):
    mean = jnp.mean(v, axis=-1, keepdims=True)
    centred = v - mean
    inverse = lax.rsqrt(jnp.mean(centred * centred, axis=-1, keepdims=True) + EPSILON)
    return mean, inverse


def norm_back(t, gain, n, inverse):
    u = t * gain
    return inverse * (
        u - jnp.mean(u, axis=-1, keepdims=True) - n * jnp.mean(u * n, axis=-1, keepdims=True)
    )


def column_sum(v):
    return jnp.sum(v, axis=0, keepdims=True)


def layer_kernel(names, *refs):
    r = types.SimpleNamespace(**dict(zip(names, refs)))
    p = Place()
    T, D = r.tokens.shape

    barrier = pltpu.get_barrier_semaphore()
    partners = (p.core, p.along_x, p.along_y, p.diagonal, p.z_near, p.z_far, p.z_mirror)
    for partner in partners:
        pl.semaphore_signal(barrier, inc=1, device_id=partner, device_id_type=MESH)

    pool = r.pool

    def load(src, dst, index):
        return pltpu.make_async_copy(src, dst, r.load_sems.at[index])

    def chunk_of(i):
        flip_y, flip_x = 1 - lax.rem(i, 2), 1 - i // 2
        return 2 * (p.y + flip_y - 2 * flip_y * p.y) + p.x + flip_x - 2 * flip_x * p.x

    def up_load(i):
        src = r.up_weight.at[:, pl.ds(pl.multiple_of(chunk_of(i) * D, D), D)]
        return load(src, pool.at[1 + i], 6 + i)

    def down_load(i):
        src = r.down_weight.at[pl.ds(pl.multiple_of(chunk_of(i) * D, D), D), :]
        return load(src, pool.at[4 + i], 10 + i)

    tokens_load = load(r.tokens, r.tok, 0)
    tokens_load.start()
    vectors = [
        load(getattr(r, name), getattr(r, "v_" + name), 20 + i) for i, name in enumerate(VECTORS)
    ]
    for copy in vectors:
        copy.start()
    qkv_loads = [
        load(r.qkv_weight.at[:, pl.ds(i * D, D)], pool.at[1 + i], 1 + i) for i in range(3)
    ]
    for i in (1, 2, 0):
        qkv_loads[i].start()
    cot_load = load(r.cotangent, r.cot, 4)
    out_load = load(r.out_weight, pool.at[0], 5)
    for copy in [cot_load] + [down_load(i) for i in range(4)] + [out_load]:
        copy.start()

    gid = r.group_ids[0]
    length = r.lengths[0]
    for copy in vectors:
        copy.wait()
    table = r.v_group_table[...]
    group_rows = lax.broadcasted_iota(jnp.int32, table.shape, 0)
    table_row = jnp.sum(jnp.where(group_rows == gid, table, 0.0), axis=0, keepdims=True)
    tokens_load.wait()
    start = r.tok[...].astype(F32) + table_row
    mean, inverse = norm_stats(start)
    nx, nxT = r.nx, r.nxT
    r.norm_two[...] = ((start - mean) * inverse * row_of(r.v_first_gain) + row_of(r.v_first_shift)).astype(BF)

    pl.semaphore_wait(barrier, len(partners))

    def nx_copy(s, half):
        rows = pl.ds(half * (T // 2), T // 2)
        own = isinstance(s, int) and s == 0
        src = r.norm_two.at[rows] if own else nx.at[s - 1, rows]
        return send(src, nx.at[s, rows], r.nx_sems, 2 * s + half, p.along_z(1))

    def nx_pass(s, half):
        rows = pl.ds(half * (T // 2), T // 2)
        here = nx.at[s - 1, rows]
        send(here, here, r.nx_sems, 2 * (s - 1) + half, p.along_z(-1)).wait_recv()
        pl.when((s < 3) & (p.z < 3))(lambda: nx_copy(s, half).start())

    kv, qT, outT, stat, mass = r.kv, r.qT, r.outT, r.stat, r.mass
    qin, doin, stat_in = r.qin, r.doin, r.stat_in
    key_iota = lax.broadcasted_iota(jnp.int32, (T, T), 0)
    query_iota = lax.broadcasted_iota(jnp.int32, (T, T), 1)
    scale2 = HEAD**-0.5 * LOG2E

    def q_copy(t):
        src = qT if t == 0 else qin.at[t - 1]
        return send(src, qin.at[t], r.q_sems, t, p.along_z(-1))

    def q_wait(t):
        send(qT, qin.at[t], r.q_sems, t, p.along_z(1)).wait_recv()

    def q_pass(t):
        q_wait(t)
        q_copy(t + 1).start()

    def head_rows(h):
        return pl.ds(pl.multiple_of(h * HEAD, HEAD), HEAD)

    def masked(scores, block, causal):
        allowed = key_iota < length - block * T
        if causal:
            allowed = allowed & (key_iota <= query_iota)
        return jnp.where(allowed, scores * scale2, NEG_LARGE)

    def attend(s, own):
        def some_heads(g, _):
            heads = [g * GROUP + i for i in range(GROUP)]
            places = [head_rows(h) for h in heads]
            scores = [masked(dot_tn(kv[s, 0, rows], qT[rows]), p.z - s, own) for rows in places]
            highest = [jnp.max(v, axis=0, keepdims=True) for v in scores]
            if not own:
                highest = [jnp.maximum(v, stat[pl.ds(h, 1)]) for v, h in zip(highest, heads)]
                fade = [jnp.exp2(stat[pl.ds(h, 1)] - v) for v, h in zip(highest, heads)]
            weights = [jnp.exp2(v - m) for v, m in zip(scores, highest)]
            total = [column_sum(v) for v in weights]
            value = [dot(kv[s, 1, rows], v.astype(BF)) for v, rows in zip(weights, places)]
            for i, (h, rows) in enumerate(zip(heads, places)):
                if not own:
                    total[i] = total[i] + mass[pl.ds(h, 1)] * fade[i]
                    value[i] = value[i] + outT[rows] * fade[i]
                stat[pl.ds(h, 1)] = highest[i]
                mass[pl.ds(h, 1)] = total[i]
                outT[rows] = value[i]
            return 0

        lax.fori_loop(0, HEADS // GROUP, some_heads, 0)

    def project(s, block, rows):
        kv[s, 0, :, rows] = dot(block, pool[2]).astype(BF).T
        kv[s, 1, :, rows] = (dot(block, pool[3]) + r.v_qv_bias[1:2]).astype(BF).T

    for half in range(2):
        pl.when(p.z < 3)(functools.partial(lambda half: nx_copy(0, half).start(), half))
    nxT[...] = r.norm_two[...].T
    for copy in qkv_loads:
        copy.wait()
    qT[...] = (dot(r.norm_two[...], pool[1]) + r.v_qv_bias[0:1]).astype(BF).T
    pl.when(p.z >= 1)(lambda: q_copy(0).start())
    project(0, r.norm_two[...], slice(0, T))
    attend(0, True)
    cot_load.wait()
    r.cotT[...] = r.cot[...].T
    for k in range(4):
        r.up_rows[k : k + 1] = r.v_up_bias[k * D : (k + 1) * D].reshape(1, D)

    def act_grad(i):
        down_load(i).wait()
        r.act_grad[lax.rem(i, 2)] = dot_nt(r.cot[...], pool[4 + i])

    lax.fori_loop(0, 2, lambda i, _: (act_grad(i), 0)[1], 0)

    def earlier_block(s, _):
        for half in range(2):
            nx_pass(s, half)
            rows = slice(half * (T // 2), (half + 1) * (T // 2))
            project(s, nx[s - 1, rows], rows)
        attend(s, False)
        pl.when((s == 1) & (p.z < 3))(functools.partial(q_pass, 0))
        return 0

    lax.fori_loop(1, p.z + 1, earlier_block, 0)
    for i in (0, 1, 2):
        up_load(i).start()

    def finish(h, _):
        rows = head_rows(h)
        value = outT[rows] * (1.0 / mass[pl.ds(h, 1)])
        outT[rows] = value
        r.attT[rows] = value.astype(BF)
        return 0

    lax.fori_loop(0, HEADS, finish, 0, unroll=True)
    stat[0:HEADS] = stat[0:HEADS] + jnp.log2(mass[...])
    attT = r.attT

    out_load.wait()
    after = r.tok[...].astype(F32) + table_row + dot(attT[...].T, pool[0]) + row_of(r.v_out_bias)
    r.after[...] = after
    mean, inverse = norm_stats(after)
    norm_two = ((after - mean) * inverse * row_of(r.v_second_gain) + row_of(r.v_second_shift)).astype(BF)
    for half in range(2):
        pl.when(p.z < 3)(functools.partial(lambda half: nx_copy(0, half).wait_send(), half))
    r.norm_two[...] = norm_two
    r.norm_twoT[...] = norm_two.T
    r.total[...] = after + row_of(r.v_down_bias)
    r.t[...] = jnp.zeros((T, D), F32)

    g_down, g_up, g_out = r.g_down, r.g_up, r.g_out

    def scatter(name, parts, out, columns=None):
        return ReduceScatter(
            p,
            getattr(r, "g_" + name),
            getattr(r, "rc_" + name),
            getattr(r, "r1_" + name),
            getattr(r, "r2_" + name),
            getattr(r, "rz1_" + name),
            getattr(r, "rz2_" + name),
            getattr(r, "cs_" + name),
            getattr(r, "ss_" + name),
            parts,
            out,
            getattr(r, "zb_" + name, None),
            columns,
        )

    narrow, width = D // 4, D // 2
    down = scatter("down", "yx", r.s_down)
    up = scatter("up", "z", r.s_up)
    out = scatter("out", "", r.s_out, [(z * narrow, (z + 1) * narrow) for z in range(4)])
    queries, keys, values = [(i * width, (i + 1) * width) for i in range(3)]
    projs = [
        scatter("p0", "", lambda h, v: lay_out(0, h, v), (queries, keys, values, values)),
        scatter("p1", "", lambda h, v: lay_out(1, h, v), (queries, queries, keys, values)),
    ]
    layouts = (
        ((0, width, 0), (0, width, narrow), (0, narrow, width), (narrow, width, 0)),
        ((0, narrow, width), (narrow, width, 0), (0, width, 0), (0, width, narrow)),
    )

    def lay_out(chunk, h, value):
        for z, (first, last, at) in enumerate(layouts[chunk]):

            def store(first=first, last=last, at=at):
                r.s_qkv[h, :, at : at + last - first] = value[:, first:last]

            pl.when(p.z == z)(store)


    def spread(rows):
        table_grad = jnp.where(group_rows == gid, rows[0:1], 0.0)
        return jnp.concatenate([table_grad, rows[1:5]], axis=0)

    early = SmallSum(
        p, r.early_z, r.early_c, r.early_x, r.early_sems, r.early_out, lambda rows: rows
    )
    late = SmallSum(p, r.late_z, r.late_c, r.late_x, r.late_sems, r.late_out, spread)
    small = r.early_z.at[p.z]
    gelu_c = math.sqrt(2.0 / math.pi)

    def pass_on(k):
        down.core_sum(k)
        down.first_start(k)
        up.core_sum(k)
        up.first_start(k)

    def chunk(i, _):
        k = chunk_of(i)
        kh, kl = k // 2, lax.rem(k, 2)
        up_load(i).wait()
        pl.when(i >= 2)(lambda: act_grad(i))
        weight = pool[1 + i]
        weight_down = pool[4 + i]
        hidden = dot(r.norm_two[...], weight) + r.up_rows[pl.ds(k, 1), :]
        square = hidden * hidden
        th = jnp.tanh(gelu_c * hidden * (1.0 + 0.044715 * square))
        half = 0.5 + 0.5 * th
        act = (hidden * half).astype(BF)
        slope = half + 0.5 * hidden * (1.0 - th * th) * gelu_c * (1.0 + 3 * 0.044715 * square)
        grad = r.act_grad[lax.rem(i, 2)] * slope
        small[pl.ds(4 + k, 1), :] = column_sum(grad)
        low = grad.astype(BF)
        piece = D // 2
        for cc in range(2):
            rows = dot(r.cotT[...], act[:, cc * piece : (cc + 1) * piece]).astype(BF)
            part = D // 4
            for z in range(4):
                for h in range(2):
                    at = z * part + h * (part // 2)
                    g_down[h, kh, kl, cc, z // 2, z % 2] = rows[at : at + part // 2]
        down.core_start(k)
        part = D // 8
        for y in range(2):
            rows = dot(r.norm_twoT[y * 4 * part : (y + 1) * 4 * part], low).astype(BF)
            for d in range(4):
                for h in range(2):
                    at = d * part + h * (part // 2)
                    g_up[h, y, d // 2, d % 2, kh, kl] = rows[at : at + part // 2]
        up.core_start(k)
        pl.when(i > 0)(lambda: pass_on(chunk_of(i - 1)))
        r.total[...] += dot(act, weight_down)
        r.t[...] += dot_nt(low, weight)
        pl.when(i == 0)(lambda: up_load(3).start())
        return 0

    lax.fori_loop(0, 4, chunk, 0)
    pass_on(chunk_of(3))
    pl.when(p.z == 1)(functools.partial(q_pass, 1))

    qkv_loads = [
        load(r.qkv_weight.at[:, pl.ds(i * D, D)], pool.at[1 + i], 14 + i) for i in range(3)
    ]
    for copy in qkv_loads:
        copy.start()

    nx[2] = r.total[...].astype(BF)
    result_store = pltpu.make_async_copy(nx.at[2], r.result, r.load_sems.at[17])
    result_store.start()
    cot = r.cot[...].astype(F32)
    after = r.after[...]
    mean, inverse = norm_stats(after)
    n = (after - mean) * inverse
    t = r.t[...]
    after_grad = cot + norm_back(t, row_of(r.v_second_gain), n, inverse)
    r.after[...] = after_grad
    after_low = after_grad.astype(BF)
    doT = r.doT
    doT[...] = dot_nt(pool[0], after_low).astype(BF)
    for h in range(HEADS):
        rows = slice(h * HEAD, (h + 1) * HEAD)
        stat[HEADS + h : HEADS + h + 1] = column_sum(doT[rows].astype(F32) * outT[rows])
    def group_rows_of(group):
        return pl.ds(pl.multiple_of(group * width, width), width)

    def do_copy(t, group):
        rows = group_rows_of(group)
        src = doT.at[rows] if isinstance(t, int) and t == 0 else doin.at[t - 1, rows]
        return send(src, doin.at[t, rows], r.do_sems, 2 * t + group, p.along_z(-1))

    def stat_copy(t):
        src = stat if isinstance(t, int) and t == 0 else stat_in.at[t - 1]
        return send(src, stat_in.at[t], r.stat_sems, t, p.along_z(-1))

    def do_send(t, group):
        pl.when(group == 0)(lambda: stat_copy(t).start())
        do_copy(t, group).start()

    def stat_wait(t):
        send(stat, stat_in.at[t], r.stat_sems, t, p.along_z(1)).wait_recv()

    def do_wait(t, group):
        rows = group_rows_of(group)
        send(doT.at[rows], doin.at[t, rows], r.do_sems, 2 * t + group, p.along_z(1)).wait_recv()
        pl.when(group == 0)(lambda: stat_wait(t))

    for group in range(2):
        pl.when(p.z >= 1)(functools.partial(do_send, 0, group))
    small[pl.ds(0, 1), :] = column_sum(after_grad)
    small[pl.ds(1, 1), :] = column_sum(t * n)
    small[pl.ds(2, 1), :] = column_sum(t)
    small[pl.ds(3, 1), :] = column_sum(cot)
    rows = dot(attT[...], after_low).astype(BF)
    part = D // 8
    for d in range(8):
        for h in range(2):
            at = d * part + h * (part // 2)
            g_out[h, d // 4, (d // 2) % 2, d % 2] = rows[at : at + part // 2]
    out.core_start(0)

    outT[...] = jnp.zeros((D, T), F32)
    key_grad, value_grad = r.key_grad, r.value_grad
    mixed = (kv.at[1, 0], kv.at[1, 1], kv.at[2, 0])

    def grads_of(s, group, queries, out_grads, sums, causal, for_queries, for_keys):
        heads = [group * GROUP + i for i in range(GROUP)]
        places = [head_rows(h) for h in heads]
        scores = [dot_tn(kv[s, 0, rows], queries[rows]) for rows in places]
        prob_grad = [dot_tn(kv[s, 1, rows], out_grads[rows]) for rows in places]
        scores = [masked(v, p.z - s, causal) for v in scores]
        probs = [jnp.exp2(v - sums[pl.ds(h, 1)]) for v, h in zip(scores, heads)]
        score_grad = [
            (v * (w - sums[pl.ds(HEADS + h, 1)])).astype(BF)
            for v, w, h in zip(probs, prob_grad, heads)
        ]
        if for_queries:
            query_add = [dot(kv[s, 0, rows], v) for v, rows in zip(score_grad, places)]
        if for_keys:
            probs = [v.astype(BF) for v in probs]
            key_add = [dot_nt(queries[rows], v) for v, rows in zip(score_grad, places)]
            value_add = [dot_nt(out_grads[rows], v) for v, rows in zip(probs, places)]
        for i, rows in enumerate(places):
            if for_queries:
                outT[rows] = outT[rows] + query_add[i]
            if for_keys and for_queries:
                key_grad[rows] = key_add[i]
                value_grad[rows] = value_add[i]
            elif for_keys:
                key_grad[rows] = key_grad[rows] + key_add[i]
                value_grad[rows] = value_grad[rows] + value_add[i]

    def query_step(i, _):
        grads_of(p.z - i // 2, lax.rem(i, 2), qT, doT, stat, False, True, False)
        return 0

    def own_step(group, _):
        grads_of(0, group, qT, doT, stat, True, True, True)
        return 0

    def key_step(t, group):
        pl.when((p.z == 0) & (group == 0))(lambda: q_wait(t))
        do_wait(t, group)
        pl.when(p.z >= 1)(lambda: do_send(t + 1, group))
        grads_of(0, group, qin.at[t], doin.at[t], stat_in.at[t], False, False, True)

    def proj_grad(group):
        rows = slice(group * width, (group + 1) * width)
        mixed[0][rows] = (outT[rows] * HEAD**-0.5).astype(BF)
        mixed[1][rows] = (key_grad[rows] * HEAD**-0.5).astype(BF)
        mixed[2][rows] = value_grad[rows].astype(BF)
        target = (r.g_p0, r.g_p1)[group]
        part = D // 8
        for i in range(3):
            piece = dot_nt(nxT[...], mixed[i][rows]).astype(BF)
            for d in range(8):
                for h in range(2):
                    at = d * part + h * (part // 2)
                    target[h, d // 4, (d // 2) % 2, d % 2, :, i * width : (i + 1) * width] = piece[
                        at : at + part // 2
                    ]
        projs[group].core_start(0)

    def norm_back_one():
        outT[...] = sum(dot(pool[1 + i], mixed[i][...]) for i in range(3))
        ones = jnp.ones((8, T), BF)
        rows = r.late_z.at[p.z]
        rows[pl.ds(3, 1), :] = dot_nt(ones, mixed[0][...])[0:1]
        rows[pl.ds(4, 1), :] = dot_nt(ones, mixed[2][...])[0:1]
        t1 = outT[...].T
        start = r.tok[...].astype(F32) + table_row
        mean, inverse = norm_stats(start)
        n = (start - mean) * inverse
        start_grad = r.after[...] + norm_back(t1, row_of(r.v_first_gain), n, inverse)
        r.norm_two[...] = start_grad.astype(BF)
        tokens_store.start()
        rows[pl.ds(0, 1), :] = column_sum(start_grad)
        rows[pl.ds(1, 1), :] = column_sum(t1 * n)
        rows[pl.ds(2, 1), :] = column_sum(t1)
        late.advance(0)

    tokens_store = pltpu.make_async_copy(r.norm_two, r.grad_tokens, r.load_sems.at[18])

    for copy in qkv_loads:
        copy.wait()
    lax.fori_loop(0, 2 * p.z, query_step, 0)
    lax.fori_loop(0, 2, own_step, 0)
    step = functools.partial

    ahead = (
        (
            (1, step(up.advance, 1)),
            (1, step(down.advance, 1)),
            (3, step(out.advance, 0)),
            (3, step(down.advance, 2)),
            (5, step(proj_grad, 0)),
        ),
        (
            (2, step(down.advance, 1)),
        ),
        (
        ),
        (
        ),
    )
    rest = (
        ((0, 1), step(down.advance, 1)),
        ((0,), step(up.advance, 1)),
        ((), step(early.advance, 0)),
        ((0,), step(proj_grad, 0)),
        ((0,), step(down.advance, 2)),
        ((), step(projs[0].advance, 0)),
        ((), step(proj_grad, 1)),
        ((), step(up.advance, 2)),
        ((), step(projs[1].advance, 0)),
        ((), norm_back_one),
        ((), step(projs[0].advance, 1)),
        ((), step(down.advance, 3)),
        ((), step(early.advance, 1)),
        ((), step(projs[1].advance, 1)),
        ((0,), step(out.advance, 0)),
        ((), step(up.advance, 3)),
        ((), step(early.advance, 2)),
        ((), step(projs[0].advance, 2)),
        ((), step(late.advance, 1)),
        ((), step(projs[1].advance, 2)),
        ((), step(down.advance, 4)),
        ((), step(out.advance, 1)),
        ((), step(projs[0].advance, 3)),
        ((), step(late.advance, 2)),
        ((), step(out.advance, 2)),
        ((), step(projs[1].advance, 3)),
        ((), step(early.advance, 3)),
        ((), step(late.advance, 3)),
        ((), step(up.advance, 4)),
        ((), step(out.advance, 3)),
        ((), step(projs[1].advance, 4)),
        ((), step(projs[0].advance, 4)),
        ((), step(out.advance, 4)),
    )

    def half_round(i, _):
        for z in range(3):
            for at, one in ahead[z]:
                pl.when((p.z == z) & (i == at))(one)
        pl.when(p.z + i // 2 < 3)(lambda: key_step(i // 2, lax.rem(i, 2)))
        return 0

    for _, one in ahead[3]:
        pl.when(p.z == 3)(one)
    lax.fori_loop(0, 7, half_round, 0)
    for done, one in rest:
        if len(done) == 0:
            one()
        else:
            planes = [z for z in range(4) if z not in done]
            if planes:
                pl.when(functools.reduce(jnp.logical_or, [p.z == z for z in planes]))(one)
    for s in (1, 2):
        for half in range(2):
            pl.when((p.z < 3) & (p.z >= s))(lambda s=s, half=half: nx_copy(s, half).wait_send())
    def sent(t):
        q_copy(t).wait_send()
        stat_copy(t).wait_send()
        do_copy(t, 0).wait_send()
        do_copy(t, 1).wait_send()

    for t in range(3):
        pl.when((p.z >= 1) & (p.z + t <= 3))(functools.partial(sent, t))
    result_store.wait()
    tokens_store.wait()

def row_of(ref):
    return ref[...].reshape(1, ref.shape[0])


def outputs_kernel(result, grad_tokens, early, late, s_qkv, s_out, s_up, s_down, *outs):
    (
        o_result,
        o_tokens,
        o_table,
        o_first_gain,
        o_first_shift,
        o_qkv,
        o_qv_bias,
        o_out,
        o_out_bias,
        o_second_gain,
        o_second_shift,
        o_up,
        o_up_bias,
        o_down,
        o_down_bias,
    ) = outs
    D = early.shape[1]
    o_result[...] = result[...].reshape(o_result.shape)
    o_tokens[...] = grad_tokens[...].reshape(o_tokens.shape)
    o_table[...] = late[0:16]
    o_first_gain[...] = late[16]
    o_first_shift[...] = late[17]
    o_out_bias[...] = early[0]
    o_second_gain[...] = early[1]
    o_second_shift[...] = early[2]
    o_down_bias[...] = early[3]
    for k in range(4):
        o_up_bias[pl.ds(k * D, D)] = early[4 + k]
    o_qv_bias[...] = late[18:20]
    for ref, value in ((o_qkv, s_qkv), (o_out, s_out), (o_up, s_up), (o_down, s_down)):
        half = value.shape[1]
        for h in range(2):
            ref[h * half : (h + 1) * half] = value[h]


def fused(
    tokens,
    group_ids,
    lengths,
    cotangent,
    group_table,
    first_gain,
    first_shift,
    qkv_weight,
    query_value_bias,
    out_weight,
    out_bias,
    second_gain,
    second_shift,
    up_weight,
    up_bias,
    down_weight,
    down_bias,
):
    _, T, D = tokens.shape
    F = up_weight.shape[1]
    any_spec = pl.BlockSpec(memory_space=pl.ANY)
    vmem = pl.BlockSpec(memory_space=pltpu.VMEM)
    smem = pl.BlockSpec(memory_space=pltpu.SMEM)
    inputs = dict(
        tokens=(tokens.reshape(T, D), any_spec),
        group_ids=(group_ids, smem),
        lengths=(lengths, smem),
        cotangent=(cotangent.reshape(T, D), any_spec),
        group_table=(group_table, any_spec),
        first_gain=(first_gain, any_spec),
        first_shift=(first_shift, any_spec),
        qkv_weight=(qkv_weight, any_spec),
        qv_bias=(query_value_bias, any_spec),
        out_weight=(out_weight, any_spec),
        out_bias=(out_bias, any_spec),
        second_gain=(second_gain, any_spec),
        second_shift=(second_shift, any_spec),
        up_weight=(up_weight, any_spec),
        up_bias=(up_bias, any_spec),
        down_weight=(down_weight, any_spec),
        down_bias=(down_bias, any_spec),
    )
    shares = dict(
        down=(D // 8, F // 8),
        up=(D // 16, F // 4),
        out=(D // 16, D // 4),
        qkv=(D // 16, 3 * D // 4),
    )
    outputs = dict(
        result=((T, D), BF),
        grad_tokens=((T, D), BF),
        early_out=((8, D), F32),
        late_out=((20, D), F32),
    )
    outputs.update({"s_" + k: ((2,) + shares[k], F32) for k in ("qkv", "out", "up", "down")})
    dma = pltpu.SemaphoreType.DMA
    scratch = dict(
        pool=pltpu.VMEM((8, D, D), BF),
        v_group_table=pltpu.VMEM(group_table.shape, F32),
        v_first_gain=pltpu.VMEM((D,), F32),
        v_first_shift=pltpu.VMEM((D,), F32),
        v_qv_bias=pltpu.VMEM((2, D), F32),
        v_out_bias=pltpu.VMEM((D,), F32),
        v_second_gain=pltpu.VMEM((D,), F32),
        v_second_shift=pltpu.VMEM((D,), F32),
        v_up_bias=pltpu.VMEM((F,), F32),
        v_down_bias=pltpu.VMEM((D,), F32),
        tok=pltpu.VMEM((T, D), BF),
        cot=pltpu.VMEM((T, D), BF),
        cotT=pltpu.VMEM((D, T), BF),
        nx=pltpu.VMEM((3, T, D), BF),
        nxT=pltpu.VMEM((D, T), BF),
        qT=pltpu.VMEM((D, T), BF),
        kv=pltpu.VMEM((4, 2, D, T), BF),
        outT=pltpu.VMEM((D, T), F32),
        stat=pltpu.VMEM((2 * HEADS, T), F32),
        mass=pltpu.VMEM((HEADS, T), F32),
        qin=pltpu.VMEM((3, D, T), BF),
        doin=pltpu.VMEM((3, D, T), BF),
        stat_in=pltpu.VMEM((3, 2 * HEADS, T), F32),
        key_grad=pltpu.VMEM((D, T), F32),
        value_grad=pltpu.VMEM((D, T), F32),
        attT=pltpu.VMEM((D, T), BF),
        after=pltpu.VMEM((T, D), F32),
        norm_two=pltpu.VMEM((T, D), BF),
        norm_twoT=pltpu.VMEM((D, T), BF),
        act_grad=pltpu.VMEM((2, T, D), F32),
        total=pltpu.VMEM((T, D), F32),
        t=pltpu.VMEM((T, D), F32),
        doT=pltpu.VMEM((D, T), BF),
        up_rows=pltpu.VMEM((4, D), F32),
        early_z=pltpu.VMEM((4, 8, D), F32),
        early_c=pltpu.VMEM((2, 8, D), F32),
        early_x=pltpu.VMEM((4, 8, D), F32),
        late_z=pltpu.VMEM((4, 5, D), F32),
        late_c=pltpu.VMEM((2, 20, D), F32),
        late_x=pltpu.VMEM((4, 20, D), F32),
        load_sems=dma((29,)),
        nx_sems=dma((2, 6)),
        q_sems=dma((2, 3)),
        do_sems=dma((2, 6)),
        stat_sems=dma((2, 3)),
        early_sems=dma((2, 7)),
        late_sems=dma((2, 7)),
    )
    places = dict(
        down=(2, 2, D // 8, F // 8),
        up=(2, 2, D // 16, F // 4),
        out=(D // 16, D),
        p0=(D // 16, 3 * D // 2),
        p1=(D // 16, 3 * D // 2),
    )
    columns_of = dict(shares, p0=(D // 16, D // 2), p1=(D // 16, D // 2))
    for name, place in places.items():
        rows, columns = columns_of[name]
        extra = {
            "g_" + name: pltpu.VMEM((2, 2, 2, 2) + place, BF),
            "rc_" + name: pltpu.VMEM((2, 2, 2) + place, BF),
            "r1_" + name: pltpu.VMEM((2, 2) + place, BF),
            "r2_" + name: pltpu.VMEM((2,) + place, BF),
            "rz1_" + name: pltpu.VMEM((2, 2, rows, columns), BF),
            "rz2_" + name: pltpu.VMEM((2, rows, columns), BF),
            "cs_" + name: dma((2, 4)),
            "ss_" + name: dma((2, 12)),
        }
        if len(place) == 2:
            extra["zb_" + name] = pltpu.VMEM((2, 2, 2, rows, columns), BF)
        scratch.update(extra)
    names = list(inputs) + list(outputs) + list(scratch)
    done = pl.pallas_call(
        functools.partial(layer_kernel, names),
        name="layer",
        out_shape=[jax.ShapeDtypeStruct(*o) for o in outputs.values()],
        in_specs=[i[1] for i in inputs.values()],
        out_specs=[any_spec] * 2 + [vmem] * (len(outputs) - 2),
        scratch_shapes=list(scratch.values()),
        compiler_params=pltpu.CompilerParams(
            collective_id=0, has_side_effects=True, vmem_limit_bytes=VMEM_LIMIT
        ),
    )(*[i[0] for i in inputs.values()])
    shape = jax.ShapeDtypeStruct
    outs = pl.pallas_call(
        outputs_kernel,
        name="outputs",
        out_shape=[
            shape((1, T, D), BF),
            shape((1, T, D), BF),
            shape((16, D), F32),
            shape((D,), F32),
            shape((D,), F32),
            shape((D // 8, 3 * D // 4), F32),
            shape((2, D), F32),
            shape((D // 8, D // 4), F32),
            shape((D,), F32),
            shape((D,), F32),
            shape((D,), F32),
            shape((D // 8, F // 4), F32),
            shape((F,), F32),
            shape((D // 4, F // 8), F32),
            shape((D,), F32),
        ],
        in_specs=[vmem] * len(done),
        out_specs=[vmem] * 15,
    )(*done)
    return (*outs[:13], outs[13].T, outs[14])


def shifted(array, axis, by):
    devices = lax.axis_size(axis)
    pairs = [(i, i + by) for i in range(devices) if 0 <= i + by < devices]
    return lax.ppermute(array, axis, pairs)


def as_sent(array):
    return jax.tree.map(lambda a: a.astype(jnp.bfloat16) if a.dtype == jnp.float32 else a, array)


def shifted_2(block, axis, distance):
    devices = range(lax.axis_size(axis))
    route = [((i - distance) % len(devices), i) for i in devices]
    return lax.ppermute(block, axis, route)


def layer_norm(inputs, norm_gain, norm_shift):
    average = jnp.mean(inputs, -1, keepdims=True)
    centred = inputs - average
    inverse = lax.rsqrt(jnp.mean(centred * centred, -1, keepdims=True) + EPSILON)
    return centred * inverse * norm_gain + norm_shift


def tanh_gelu(inputs):
    return jax.nn.gelu(inputs, approximate=True)


def keep_same(state_value):
    return state_value


def scores_of(queries, key_piece, key_start, query_start, lengths):
    sequences, block_len = (queries.shape[0], queries.shape[1])
    key_heads = key_piece.reshape(sequences, key_piece.shape[1], HEADS, HEAD)
    raw_scores = jnp.einsum(
        "gqhe,gkhe->ghqk", queries, key_heads, preferred_element_type=jnp.float32
    ) * HEAD ** (-0.5)
    key_pos = key_start + jnp.arange(key_piece.shape[1])
    query_pos = query_start + jnp.arange(block_len)
    allowed = (query_pos[:, None] >= key_pos[None, :])[None] & (
        key_pos[None, None, :] < lengths[:, None, None]
    )
    return (raw_scores, allowed[:, None])


def plain(
    tokens,
    group_ids,
    lengths,
    cotangent,
    group_table,
    first_gain,
    first_shift,
    qkv_weight,
    query_value_bias,
    out_weight,
    out_bias,
    second_gain,
    second_shift,
    up_weight,
    up_bias,
    down_weight,
    down_bias,
):
    sequences, block_len, features = tokens.shape
    token_rows = sequences * block_len
    seq_count = lax.axis_size("seq")
    seq_index = lax.axis_index("seq")
    query_start = seq_index * block_len
    score_scale = HEAD ** (-0.5)
    one_hot = (group_ids[:, None] == jnp.arange(group_table.shape[0])[None, :]).astype(jnp.float32)
    table_rows = jnp.dot(one_hot, group_table, precision=EXACT)
    start_rows = (tokens.astype(jnp.float32) + table_rows[:, None, :]).reshape(token_rows, features)
    norm_one, pull_one = jax.vjp(layer_norm, start_rows, first_gain, first_shift)
    norm_one_low = norm_one.astype(jnp.bfloat16)
    full_bias = jnp.concatenate(
        [query_value_bias[0], jnp.zeros((features,), jnp.float32), query_value_bias[1]]
    )
    mixed_rows = (
        jnp.dot(norm_one_low, qkv_weight, preferred_element_type=jnp.float32) + full_bias
    ).astype(jnp.bfloat16)
    mixed_rows = mixed_rows.reshape(sequences, block_len, 3 * features)
    queries = mixed_rows[:, :, :features].reshape(sequences, block_len, HEADS, HEAD)
    key_rows = mixed_rows[:, :, features : 2 * features]
    values = mixed_rows[:, :, 2 * features :]
    pieces = []
    current = (key_rows, values)
    for cycle_step in range(seq_count):
        if cycle_step > 0:
            current = shifted((current[0], current[1]), "seq", 1)
        anchor = (seq_index - cycle_step) % seq_count
        pieces.append((current[0], current[1], anchor * block_len, cycle_step <= seq_index))
    shape_rows = (sequences, HEADS, block_len)
    row_max = jnp.full(shape_rows, NEG_LARGE, jnp.float32)
    row_sum = jnp.zeros(shape_rows, jnp.float32)
    stored = []
    for key_piece, value_piece, key_start, active in pieces:

        def visit_block(state_pair, key_piece=key_piece, key_start=key_start):
            raw_scores, allowed = scores_of(queries, key_piece, key_start, query_start, lengths)
            masked_scores = jnp.where(allowed, raw_scores, NEG_LARGE)
            new_max = jnp.maximum(state_pair[0], jnp.max(masked_scores, -1))
            weights = jnp.where(allowed, jnp.exp(masked_scores - new_max[..., None]), 0.0)
            return (
                new_max,
                state_pair[1] * jnp.exp(state_pair[0] - new_max) + jnp.sum(weights, -1),
                masked_scores,
            )

        def pass_block(state_pair):
            return (
                state_pair[0],
                state_pair[1],
                jnp.full(shape_rows + (block_len,), NEG_LARGE, jnp.float32),
            )

        row_max, row_sum, masked_scores = lax.cond(
            active, visit_block, pass_block, (row_max, row_sum)
        )
        stored.append(masked_scores)
    log_sum = row_max + jnp.log(row_sum)
    attended = jnp.zeros((sequences, block_len, HEADS, HEAD), jnp.float32)
    for piece_data, masked_scores in zip(pieces, stored):

        def attend_block(total_out, value_piece=piece_data[1], masked_scores=masked_scores):
            probs = jnp.exp(masked_scores - log_sum[..., None]).astype(jnp.bfloat16)
            value_heads = value_piece.reshape(sequences, block_len, HEADS, HEAD)
            return total_out + jnp.einsum(
                "ghqk,gkhe->gqhe", probs, value_heads, preferred_element_type=jnp.float32
            )

        attended = lax.cond(piece_data[3], attend_block, keep_same, attended)
    attended_low = attended.reshape(token_rows, features).astype(jnp.bfloat16)
    after_attn = (
        start_rows
        + jnp.dot(attended_low, out_weight, preferred_element_type=jnp.float32)
        + out_bias
    )
    norm_two, pull_two = jax.vjp(layer_norm, after_attn, second_gain, second_shift)
    norm_two_low = norm_two.astype(jnp.bfloat16)
    up_rows = jnp.dot(norm_two_low, up_weight, preferred_element_type=jnp.float32) + up_bias
    activated, pull_gelu = jax.vjp(tanh_gelu, up_rows)
    activated_low = activated.astype(jnp.bfloat16)
    result_rows = (
        after_attn
        + jnp.dot(activated_low, down_weight, preferred_element_type=jnp.float32)
        + down_bias
    )
    result = result_rows.astype(jnp.bfloat16).reshape(tokens.shape)
    outer_low = cotangent.reshape(token_rows, features)
    outer_grad = outer_low.astype(jnp.float32)
    grad_down_weight = jnp.dot(activated_low.T, outer_low, preferred_element_type=jnp.float32)
    grad_down_bias = jnp.sum(outer_grad, 0)
    up_grad = pull_gelu(jnp.dot(outer_low, down_weight.T, preferred_element_type=jnp.float32))[0]
    grad_up_bias = jnp.sum(up_grad, 0)
    up_low = up_grad.astype(jnp.bfloat16)
    grad_up_weight = jnp.dot(norm_two_low.T, up_low, preferred_element_type=jnp.float32)
    part_after, grad_second_gain, grad_second_shift = pull_two(
        jnp.dot(up_low, up_weight.T, preferred_element_type=jnp.float32)
    )
    after_grad = outer_grad + part_after
    grad_out_bias = jnp.sum(after_grad, 0)
    after_low = after_grad.astype(jnp.bfloat16)
    grad_out_weight = jnp.dot(attended_low.T, after_low, preferred_element_type=jnp.float32)
    out_grad = jnp.dot(after_low, out_weight.T, preferred_element_type=jnp.float32).astype(
        jnp.bfloat16
    )
    out_grad = out_grad.reshape(sequences, block_len, HEADS, HEAD)
    delta = jnp.transpose(jnp.sum(out_grad.astype(jnp.float32) * attended, -1), (0, 2, 1))

    def back_block(query_grad, key_piece, value_piece, key_start):
        raw_scores, allowed = scores_of(queries, key_piece, key_start, query_start, lengths)
        probs = jnp.where(allowed, jnp.exp(raw_scores - log_sum[..., None]), 0.0)
        value_heads = value_piece.reshape(sequences, block_len, HEADS, HEAD)
        key_heads = key_piece.reshape(sequences, block_len, HEADS, HEAD)
        prob_grad = jnp.einsum(
            "gqhe,gkhe->ghqk", out_grad, value_heads, preferred_element_type=jnp.float32
        )
        score_grad = (probs * (prob_grad - delta[..., None])).astype(jnp.bfloat16)
        query_grad = (
            query_grad
            + jnp.einsum(
                "ghqk,gkhe->gqhe", score_grad, key_heads, preferred_element_type=jnp.float32
            )
            * score_scale
        )
        key_add = (
            jnp.einsum("ghqk,gqhe->gkhe", score_grad, queries, preferred_element_type=jnp.float32)
            * score_scale
        )
        value_add = jnp.einsum(
            "ghqk,gqhe->gkhe",
            probs.astype(jnp.bfloat16),
            out_grad,
            preferred_element_type=jnp.float32,
        )
        return (
            query_grad,
            key_add.reshape(sequences, block_len, features),
            value_add.reshape(sequences, block_len, features),
        )

    empty_rows = jnp.zeros((sequences, block_len, features), jnp.float32)

    def skip_back(query_grad):
        return (query_grad, empty_rows, empty_rows)

    query_grad = jnp.zeros((sequences, block_len, HEADS, HEAD), jnp.float32)
    carried = (empty_rows, empty_rows)
    for cycle_step in range(seq_count):
        piece_data = pieces[cycle_step]

        def visit_back(state_grad, piece_data=piece_data):
            return back_block(state_grad, piece_data[0], piece_data[1], piece_data[2])

        query_grad, key_add, value_add = lax.cond(piece_data[3], visit_back, skip_back, query_grad)
        carried = shifted_2(
            (as_sent(carried[0] + key_add), as_sent(carried[1] + value_add)), "seq", 1
        )
    key_grad, value_grad = carried
    query_flat = query_grad.reshape(token_rows, features)
    key_flat = key_grad.reshape(token_rows, features)
    value_flat = value_grad.reshape(token_rows, features)
    grad_query_value_bias = jnp.stack([jnp.sum(query_flat, 0), jnp.sum(value_flat, 0)])
    mixed_grad = jnp.concatenate([query_flat, key_flat, value_flat], -1).astype(jnp.bfloat16)
    grad_qkv_weight = jnp.dot(norm_one_low.T, mixed_grad, preferred_element_type=jnp.float32)
    part_start, grad_first_gain, grad_first_shift = pull_one(
        jnp.dot(mixed_grad, qkv_weight.T, preferred_element_type=jnp.float32)
    )
    start_grad = after_grad + part_start
    grad_tokens = start_grad.astype(jnp.bfloat16).reshape(tokens.shape)
    grad_group_table = jnp.dot(
        one_hot.T, jnp.sum(start_grad.reshape(sequences, block_len, features), 1), precision=EXACT
    )
    small_sums = lax.psum(
        (
            grad_group_table,
            grad_first_gain,
            grad_first_shift,
            grad_query_value_bias,
            grad_out_bias,
            grad_second_gain,
            grad_second_shift,
            grad_up_bias,
            grad_down_bias,
        ),
        ("dp", "seq"),
    )
    matrices = (grad_qkv_weight, grad_out_weight, grad_up_weight, grad_down_weight)
    shares = (
        lax.psum_scatter(
            matrices[0].astype(jnp.bfloat16), "seq", scatter_dimension=1, tiled=True
        ).astype(jnp.float32),
        lax.psum_scatter(
            matrices[1].astype(jnp.bfloat16), "seq", scatter_dimension=1, tiled=True
        ).astype(jnp.float32),
        lax.psum_scatter(
            matrices[2].astype(jnp.bfloat16), "seq", scatter_dimension=1, tiled=True
        ).astype(jnp.float32),
        lax.psum_scatter(
            matrices[3].astype(jnp.bfloat16), "seq", scatter_dimension=1, tiled=True
        ).astype(jnp.float32),
    )
    shares = (
        lax.psum_scatter(
            shares[0].astype(jnp.bfloat16), "dp", scatter_dimension=0, tiled=True
        ).astype(jnp.float32),
        lax.psum_scatter(
            shares[1].astype(jnp.bfloat16), "dp", scatter_dimension=0, tiled=True
        ).astype(jnp.float32),
        lax.psum_scatter(
            shares[2].astype(jnp.bfloat16), "dp", scatter_dimension=0, tiled=True
        ).astype(jnp.float32),
        lax.psum_scatter(
            shares[3].astype(jnp.bfloat16), "dp", scatter_dimension=0, tiled=True
        ).astype(jnp.float32),
    )
    return (
        result,
        grad_tokens,
        small_sums[0],
        small_sums[1],
        small_sums[2],
        shares[0],
        small_sums[3],
        shares[1],
        small_sums[4],
        small_sums[5],
        small_sums[6],
        shares[2],
        small_sums[7],
        shares[3],
        small_sums[8],
    )


def solution(mesh):
    in_specs = (
        P("dp", "seq", None),
        P("dp"),
        P("dp"),
        P("dp", "seq", None),
        P(),
        P(),
        P(),
        P(),
        P(),
        P(),
        P(),
        P(),
        P(),
        P(),
        P(),
        P(),
        P(),
    )
    out_specs = (
        P("dp", "seq", None),
        P("dp", "seq", None),
        P(),
        P(),
        P(),
        P("dp", "seq"),
        P(),
        P("dp", "seq"),
        P(),
        P(),
        P(),
        P("dp", "seq"),
        P(),
        P("dp", "seq"),
        P(),
    )
    def shards(*arrays):
        sizes = (mesh.shape["dp"], mesh.shape["seq"]) + arrays[0].shape
        return (fused if sizes == (8, 4, 1, 256, 768) else plain)(*arrays)

    return jax.shard_map(shards, mesh=mesh, in_specs=in_specs, out_specs=out_specs, check_vma=False)
```

```python
import functools
import math
import types

import jax
import jax.numpy as jnp
from jax import lax
from jax.experimental import pallas as pl
from jax.experimental.pallas import tpu as pltpu
from jax.sharding import PartitionSpec as P

HEADS = 12
HEAD = 64


EPSILON = 1e-05
NEG_LARGE = -1e30
EXACT = lax.Precision.HIGHEST


VMEM_LIMIT = 64 << 20
GROUP = 6


BF = jnp.bfloat16
RESULTS = ("early_out", "late_out", "s_qkv", "s_out", "s_up", "s_down")
VECTORS = (
    "group_table",
    "first_gain",
    "first_shift",
    "qv_bias",
    "out_bias",
    "second_gain",
    "second_shift",
    "up_bias",
    "down_bias",
)
F32 = jnp.float32
MESH = pl.DeviceIdType.MESH
LOG2E = 1.4426950408889634


def dot(a, b):
    return lax.dot_general(a, b, (((1,), (0,)), ((), ())), preferred_element_type=F32)


def dot_nt(a, b):
    return lax.dot_general(a, b, (((1,), (1,)), ((), ())), preferred_element_type=F32)


def dot_tn(a, b):
    return lax.dot_general(a, b, (((0,), (0,)), ((), ())), preferred_element_type=F32)


def flipped(index, bit):
    return index + bit - 2 * bit * lax.rem(index // bit, 2)


class Place:
    def __init__(self):
        self.d = lax.axis_index("dp")
        self.z = lax.axis_index("seq")
        self.c = lax.rem(self.d, 2)
        self.x = lax.rem(self.d // 2, 2)
        self.y = lax.rem(self.d // 4, 2)
        self.zl = lax.rem(self.z, 2)
        self.zh = lax.rem(self.z // 2, 2)
        self.core = (flipped(self.d, 1), self.z)
        self.along_x = (flipped(self.d, 2), self.z)
        self.along_y = (flipped(self.d, 4), self.z)
        self.z_near = (self.d, flipped(self.z, 1))
        self.z_far = (self.d, flipped(self.z, 2))
        self.z_mirror = (self.d, 3 - self.z)
        self.diagonal = (flipped(flipped(self.d, 2), 4), self.z)

    def along_z(self, k):
        return (self.d, self.z + k)


def send(src, dst, sems, index, to):
    copy = pltpu.make_async_remote_copy(
        src_ref=src,
        dst_ref=dst,
        send_sem=sems.at[0, index],
        recv_sem=sems.at[1, index],
        device_id=to,
        device_id_type=MESH,
    )
    return copy


class ReduceScatter:
    def __init__(
        self, place, g, rc, r1, r2, rz1, rz2, core_sems, sems, parts, out, zb=None, columns=None
    ):
        self.p, self.g, self.rc, self.r1, self.r2 = place, g, rc, r1, r2
        self.rz1, self.rz2, self.core_sems, self.sems, self.parts = rz1, rz2, core_sems, sems, parts
        self.count = 4 if parts else 1
        self.out, self.columns = out, columns
        self.zb = g.at[:, place.y, place.x, place.c] if zb is None else zb

    def core_copy(self, k):
        p = self.p
        kh, kl = k // 2, lax.rem(k, 2)
        if self.parts == "yx":
            src, dst = self.g.at[:, kh, kl, 1 - p.c], self.rc.at[:, kh, kl]
        elif self.parts == "z":
            src, dst = self.g.at[:, :, :, 1 - p.c, kh, kl], self.rc.at[:, :, :, kh, kl]
        else:
            src, dst = self.g.at[:, :, :, 1 - p.c], self.rc
        return send(src, dst, self.core_sems, k, p.core)

    def core_start(self, k):
        self.core_copy(k).start()

    def core_sum(self, k):
        p, g, rc = self.p, self.g, self.rc
        kh, kl = k // 2, lax.rem(k, 2)
        self.core_copy(k).wait()
        if self.parts == "yx":
            for h in range(2):
                g[h, kh, kl, p.c] = g[h, kh, kl, p.c] + rc[h, kh, kl]
            return

        def add(i, _):
            h, y, x = i // 4, lax.rem(i // 2, 2), lax.rem(i, 2)
            if self.parts == "z":
                g[h, y, x, p.c, kh, kl] = g[h, y, x, p.c, kh, kl] + rc[h, y, x, kh, kl]
            else:
                g[h, y, x, p.c] = g[h, y, x, p.c] + rc[h, y, x]
            return 0

        lax.fori_loop(0, 8, add, 0)

    def first_x(self, k):
        p, g, r1 = self.p, self.g, self.r1
        kh, kl = k // 2, lax.rem(k, 2)
        if self.parts == "yx":
            return send(g.at[0, kh, 1 - p.x, p.c], r1.at[0, kh], self.sems, kh, p.along_x)
        if self.parts == "z":
            return send(
                g.at[0, :, 1 - p.x, p.c, kh, kl], r1.at[0, :, kh, kl], self.sems, k, p.along_x
            )
        return send(g.at[0, :, 1 - p.x, p.c], r1.at[0], self.sems, 0, p.along_x)

    def first_y(self, k):
        p, g, r1 = self.p, self.g, self.r1
        kh, kl = k // 2, lax.rem(k, 2)
        if self.parts == "yx":
            return send(g.at[1, 1 - p.y, kl, p.c], r1.at[1, kl], self.sems, 4 + kl, p.along_y)
        if self.parts == "z":
            return send(
                g.at[1, 1 - p.y, :, p.c, kh, kl], r1.at[1, :, kh, kl], self.sems, 4 + k, p.along_y
            )
        return send(g.at[1, 1 - p.y, :, p.c], r1.at[1], self.sems, 4, p.along_y)

    def first_start(self, k):
        p = self.p
        if self.parts == "yx":
            pl.when(lax.rem(k, 2) != p.x)(lambda: self.first_x(k).start())
            pl.when(k // 2 != p.y)(lambda: self.first_y(k).start())
        else:
            self.first_x(k).start()
            self.first_y(k).start()

    def first_sum(self):
        p, g = self.p, self.g
        if self.parts == "yx":
            for i in range(2):
                self.first_x(2 * i).wait()
                self.first_y(i).wait()
        else:
            for k in range(self.count):
                self.first_x(k).wait()
                self.first_y(k).wait()
        for i in range(2):
            g[0, i, p.x, p.c] = g[0, i, p.x, p.c] + self.r1[0, i]
            g[1, p.y, i, p.c] = g[1, p.y, i, p.c] + self.r1[1, i]

    def second_copies(self):
        p, g = self.p, self.g
        return (
            send(g.at[0, 1 - p.y, p.x, p.c], self.r2.at[0], self.sems, 8, p.along_y),
            send(g.at[1, p.y, 1 - p.x, p.c], self.r2.at[1], self.sems, 9, p.along_x),
        )

    def second_start(self):
        for copy in self.second_copies():
            copy.start()

    def second_sum(self):
        p, g = self.p, self.g
        for copy in self.second_copies():
            copy.wait()
        for h in range(2):
            total = g[h, p.y, p.x, p.c] + self.r2[h]
            if self.columns is None:
                g[h, p.y, p.x, p.c] = total
            else:
                for z, (first, last) in enumerate(self.columns):
                    self.zb[h, z // 2, z % 2] = total[:, first:last]

    def third_copy(self):
        p = self.p
        return send(self.zb.at[:, :, 1 - p.zl], self.rz1, self.sems, 10, p.z_near)

    def third_start(self):
        self.third_copy().start()

    def third_sum(self):
        p, zb = self.p, self.zb
        self.third_copy().wait()
        for h in range(2):
            for i in range(2):
                zb[h, i, p.zl] = zb[h, i, p.zl] + self.rz1[h, i]

    def fourth_copy(self):
        p = self.p
        return send(self.zb.at[:, 1 - p.zh, p.zl], self.rz2, self.sems, 11, p.z_far)

    def fourth_start(self):
        self.fourth_copy().start()

    def fourth_sum(self):
        p, zb = self.p, self.zb
        self.fourth_copy().wait()
        for h in range(2):
            total = zb[h, p.zh, p.zl].astype(F32) + self.rz2[h].astype(F32)
            if callable(self.out):
                self.out(h, total)
            else:
                self.out[0][h] = total
        if not callable(self.out):
            self.out[1].start()

    def advance(self, step):
        if step == 0:
            self.core_sum(0)
            self.first_start(0)
        elif step == 1:
            self.first_sum()
            self.second_start()
        elif step == 2:
            self.second_sum()
            self.third_start()
        elif step == 3:
            self.third_sum()
            self.fourth_start()
        else:
            self.fourth_sum()


class SmallSum:
    def __init__(self, place, zin, cin, xin, sems, out, spread):
        self.p, self.zin, self.cin, self.xin, self.sems = place, zin, cin, xin, sems
        self.out, self.spread = out, spread
        self.corner = place.d // 2

    def z_copies(self):
        p, mine = self.p, self.zin.at[self.p.z]
        peers = (p.z_near, p.z_far, p.z_mirror)
        return [send(mine, mine, self.sems, i, to) for i, to in enumerate(peers)]

    def core_copy(self):
        return send(self.cin.at[0], self.cin.at[1], self.sems, 3, self.p.core)

    def xy_copies(self):
        p, mine = self.p, self.xin.at[self.corner]
        peers = (p.along_x, p.along_y, p.diagonal)
        return [send(mine, mine, self.sems, 4 + i, to) for i, to in enumerate(peers)]

    def advance(self, step):
        cin, zin, xin = self.cin, self.zin, self.xin
        if step == 0:
            for copy in self.z_copies():
                copy.start()
        elif step == 1:
            for copy in self.z_copies():
                copy.wait()
            cin[0] = self.spread(zin[0] + zin[1] + zin[2] + zin[3])
            self.core_copy().start()
        elif step == 2:
            self.core_copy().wait()
            xin[self.corner] = cin[0] + cin[1]
            for copy in self.xy_copies():
                copy.start()
        else:
            for copy in self.xy_copies():
                copy.wait()
            self.out[0][...] = xin[0] + xin[1] + xin[2] + xin[3]
            self.out[1].start()


def norm_stats(v):
    mean = jnp.mean(v, axis=-1, keepdims=True)
    centred = v - mean
    inverse = lax.rsqrt(jnp.mean(centred * centred, axis=-1, keepdims=True) + EPSILON)
    return mean, inverse


def norm_back(t, gain, n, inverse):
    u = t * gain
    return inverse * (
        u - jnp.mean(u, axis=-1, keepdims=True) - n * jnp.mean(u * n, axis=-1, keepdims=True)
    )


def column_sum(v):
    return jnp.sum(v, axis=0, keepdims=True)


def layer_kernel(names, *refs):
    r = types.SimpleNamespace(**dict(zip(names, refs)))
    p = Place()
    T, D = r.tokens.shape

    barrier = pltpu.get_barrier_semaphore()
    partners = (p.core, p.along_x, p.along_y, p.diagonal, p.z_near, p.z_far, p.z_mirror)
    for partner in partners:
        pl.semaphore_signal(barrier, inc=1, device_id=partner, device_id_type=MESH)

    pool = r.pool

    def load(src, dst, index):
        return pltpu.make_async_copy(src, dst, r.load_sems.at[index])

    def chunk_of(i):
        flip_y, flip_x = 1 - lax.rem(i, 2), 1 - i // 2
        return 2 * (p.y + flip_y - 2 * flip_y * p.y) + p.x + flip_x - 2 * flip_x * p.x

    def up_load(i):
        src = r.up_weight.at[:, pl.ds(pl.multiple_of(chunk_of(i) * D, D), D)]
        return load(src, pool.at[1 + i], 6 + i)

    def down_load(i):
        src = r.down_weight.at[pl.ds(pl.multiple_of(chunk_of(i) * D, D), D), :]
        return load(src, pool.at[4 + i], 10 + i)

    tokens_load = load(r.tokens, r.tok, 0)
    tokens_load.start()
    vectors = [
        load(getattr(r, name), getattr(r, "v_" + name), 20 + i) for i, name in enumerate(VECTORS)
    ]
    for copy in vectors:
        copy.start()
    qkv_loads = [
        load(r.qkv_weight.at[:, pl.ds(i * D, D)], pool.at[1 + i], 1 + i) for i in range(3)
    ]
    for i in (1, 2, 0):
        qkv_loads[i].start()
    cot_load = load(r.cotangent, r.cot, 4)
    out_load = load(r.out_weight, pool.at[0], 5)
    for copy in [cot_load] + [down_load(i) for i in range(4)] + [out_load]:
        copy.start()

    gid = r.group_ids[0]
    length = r.lengths[0]
    for copy in vectors:
        copy.wait()
    table = r.v_group_table[...]
    group_rows = lax.broadcasted_iota(jnp.int32, table.shape, 0)
    table_row = jnp.sum(jnp.where(group_rows == gid, table, 0.0), axis=0, keepdims=True)
    tokens_load.wait()
    start = r.tok[...].astype(F32) + table_row
    mean, inverse = norm_stats(start)
    nx, nxT = r.nx, r.nxT
    r.norm_two[...] = ((start - mean) * inverse * row_of(r.v_first_gain) + row_of(r.v_first_shift)).astype(BF)

    pl.semaphore_wait(barrier, len(partners))

    def nx_copy(s, half):
        rows = pl.ds(half * (T // 2), T // 2)
        own = isinstance(s, int) and s == 0
        src = r.norm_two.at[rows] if own else nx.at[s - 1, rows]
        return send(src, nx.at[s, rows], r.nx_sems, 2 * s + half, p.along_z(1))

    def nx_pass(s, half):
        rows = pl.ds(half * (T // 2), T // 2)
        here = nx.at[s - 1, rows]
        send(here, here, r.nx_sems, 2 * (s - 1) + half, p.along_z(-1)).wait_recv()
        pl.when((s < 3) & (p.z < 3))(lambda: nx_copy(s, half).start())

    kv, qT, outT, stat, mass = r.kv, r.qT, r.outT, r.stat, r.mass
    qin, doin, stat_in = r.qin, r.doin, r.stat_in
    key_iota = lax.broadcasted_iota(jnp.int32, (T, T), 0)
    query_iota = lax.broadcasted_iota(jnp.int32, (T, T), 1)
    scale2 = HEAD**-0.5 * LOG2E

    def q_copy(t):
        src = qT if t == 0 else qin.at[t - 1]
        return send(src, qin.at[t], r.q_sems, t, p.along_z(-1))

    def q_wait(t):
        send(qT, qin.at[t], r.q_sems, t, p.along_z(1)).wait_recv()

    def q_pass(t):
        q_wait(t)
        q_copy(t + 1).start()

    def head_rows(h):
        return pl.ds(pl.multiple_of(h * HEAD, HEAD), HEAD)

    def masked(scores, block, causal):
        allowed = key_iota < length - block * T
        if causal:
            allowed = allowed & (key_iota <= query_iota)
        return jnp.where(allowed, scores * scale2, NEG_LARGE)

    def attend(s, own):
        def some_heads(g, _):
            heads = [g * GROUP + i for i in range(GROUP)]
            places = [head_rows(h) for h in heads]
            scores = [masked(dot_tn(kv[s, 0, rows], qT[rows]), p.z - s, own) for rows in places]
            highest = [jnp.max(v, axis=0, keepdims=True) for v in scores]
            if not own:
                highest = [jnp.maximum(v, stat[pl.ds(h, 1)]) for v, h in zip(highest, heads)]
                fade = [jnp.exp2(stat[pl.ds(h, 1)] - v) for v, h in zip(highest, heads)]
            weights = [jnp.exp2(v - m) for v, m in zip(scores, highest)]
            total = [column_sum(v) for v in weights]
            value = [dot(kv[s, 1, rows], v.astype(BF)) for v, rows in zip(weights, places)]
            for i, (h, rows) in enumerate(zip(heads, places)):
                if not own:
                    total[i] = total[i] + mass[pl.ds(h, 1)] * fade[i]
                    value[i] = value[i] + outT[rows] * fade[i]
                stat[pl.ds(h, 1)] = highest[i]
                mass[pl.ds(h, 1)] = total[i]
                outT[rows] = value[i]
            return 0

        lax.fori_loop(0, HEADS // GROUP, some_heads, 0)

    def project(s, block, rows):
        kv[s, 0, :, rows] = dot(block, pool[2]).astype(BF).T
        kv[s, 1, :, rows] = (dot(block, pool[3]) + r.v_qv_bias[1:2]).astype(BF).T

    for half in range(2):
        pl.when(p.z < 3)(functools.partial(lambda half: nx_copy(0, half).start(), half))
    nxT[...] = r.norm_two[...].T
    for copy in qkv_loads:
        copy.wait()
    qT[...] = (dot(r.norm_two[...], pool[1]) + r.v_qv_bias[0:1]).astype(BF).T
    pl.when(p.z >= 1)(lambda: q_copy(0).start())
    project(0, r.norm_two[...], slice(0, T))
    attend(0, True)
    cot_load.wait()
    r.cotT[...] = r.cot[...].T
    for k in range(4):
        r.up_rows[k : k + 1] = r.v_up_bias[k * D : (k + 1) * D].reshape(1, D)

    def act_grad(i):
        down_load(i).wait()
        r.act_grad[lax.rem(i, 2)] = dot_nt(r.cot[...], pool[4 + i])

    lax.fori_loop(0, 2, lambda i, _: (act_grad(i), 0)[1], 0)

    def earlier_block(s, _):
        for half in range(2):
            nx_pass(s, half)
            rows = slice(half * (T // 2), (half + 1) * (T // 2))
            project(s, nx[s - 1, rows], rows)
        attend(s, False)
        pl.when((s == 1) & (p.z < 3))(functools.partial(q_pass, 0))
        return 0

    lax.fori_loop(1, p.z + 1, earlier_block, 0)
    for i in (0, 1, 2):
        up_load(i).start()

    def finish(h, _):
        rows = head_rows(h)
        value = outT[rows] * (1.0 / mass[pl.ds(h, 1)])
        outT[rows] = value
        r.attT[rows] = value.astype(BF)
        return 0

    lax.fori_loop(0, HEADS, finish, 0, unroll=True)
    stat[0:HEADS] = stat[0:HEADS] + jnp.log2(mass[...])
    attT = r.attT

    out_load.wait()
    after = r.tok[...].astype(F32) + table_row + dot(attT[...].T, pool[0]) + row_of(r.v_out_bias)
    r.after[...] = after
    mean, inverse = norm_stats(after)
    norm_two = ((after - mean) * inverse * row_of(r.v_second_gain) + row_of(r.v_second_shift)).astype(BF)
    for half in range(2):
        pl.when(p.z < 3)(functools.partial(lambda half: nx_copy(0, half).wait_send(), half))
    r.norm_two[...] = norm_two
    r.norm_twoT[...] = norm_two.T
    r.total[...] = after + row_of(r.v_down_bias)
    r.t[...] = jnp.zeros((T, D), F32)

    g_down, g_up, g_out = r.g_down, r.g_up, r.g_out

    def scatter(name, parts, out, columns=None):
        return ReduceScatter(
            p,
            getattr(r, "g_" + name),
            getattr(r, "rc_" + name),
            getattr(r, "r1_" + name),
            getattr(r, "r2_" + name),
            getattr(r, "rz1_" + name),
            getattr(r, "rz2_" + name),
            getattr(r, "cs_" + name),
            getattr(r, "ss_" + name),
            parts,
            out,
            getattr(r, "zb_" + name, None),
            columns,
        )

    stores = {
        name: pltpu.make_async_copy(
            getattr(r, "o_" + name), getattr(r, name), r.store_sems.at[i]
        )
        for i, name in enumerate(RESULTS)
    }

    def result_of(name):
        return getattr(r, "o_" + name), stores[name]

    narrow, width = D // 4, D // 2
    down = scatter("down", "yx", result_of("s_down"))
    up = scatter("up", "z", result_of("s_up"))
    out = scatter("out", "", result_of("s_out"), [(z * narrow, (z + 1) * narrow) for z in range(4)])
    queries, keys, values = [(i * width, (i + 1) * width) for i in range(3)]
    projs = [
        scatter("p0", "", lambda h, v: lay_out(0, h, v), (queries, keys, values, values)),
        scatter("p1", "", lambda h, v: lay_out(1, h, v), (queries, queries, keys, values)),
    ]
    layouts = (
        ((0, width, 0), (0, width, narrow), (0, narrow, width), (narrow, width, 0)),
        ((0, narrow, width), (narrow, width, 0), (0, width, 0), (0, width, narrow)),
    )

    def lay_out(chunk, h, value):
        for z, (first, last, at) in enumerate(layouts[chunk]):

            def store(first=first, last=last, at=at):
                r.o_s_qkv[h, :, at : at + last - first] = value[:, first:last]

            pl.when(p.z == z)(store)


    def spread(rows):
        table_grad = jnp.where(group_rows == gid, rows[0:1], 0.0)
        return jnp.concatenate([table_grad, rows[1:5]], axis=0)

    early = SmallSum(
        p, r.early_z, r.early_c, r.early_x, r.early_sems, result_of("early_out"), lambda rows: rows
    )
    late = SmallSum(p, r.late_z, r.late_c, r.late_x, r.late_sems, result_of("late_out"), spread)
    small = r.early_z.at[p.z]
    gelu_c = math.sqrt(2.0 / math.pi)

    def pass_on(k):
        down.core_sum(k)
        down.first_start(k)
        up.core_sum(k)
        up.first_start(k)

    def chunk(i, _):
        k = chunk_of(i)
        kh, kl = k // 2, lax.rem(k, 2)
        up_load(i).wait()
        pl.when(i >= 2)(lambda: act_grad(i))
        weight = pool[1 + i]
        weight_down = pool[4 + i]
        hidden = dot(r.norm_two[...], weight) + r.up_rows[pl.ds(k, 1), :]
        square = hidden * hidden
        th = jnp.tanh(gelu_c * hidden * (1.0 + 0.044715 * square))
        half = 0.5 + 0.5 * th
        act = (hidden * half).astype(BF)
        slope = half + 0.5 * hidden * (1.0 - th * th) * gelu_c * (1.0 + 3 * 0.044715 * square)
        grad = r.act_grad[lax.rem(i, 2)] * slope
        small[pl.ds(4 + k, 1), :] = column_sum(grad)
        low = grad.astype(BF)
        piece = D // 2
        for cc in range(2):
            rows = dot(r.cotT[...], act[:, cc * piece : (cc + 1) * piece]).astype(BF)
            part = D // 4
            for z in range(4):
                for h in range(2):
                    at = z * part + h * (part // 2)
                    g_down[h, kh, kl, cc, z // 2, z % 2] = rows[at : at + part // 2]
        down.core_start(k)
        part = D // 8
        for y in range(2):
            rows = dot(r.norm_twoT[y * 4 * part : (y + 1) * 4 * part], low).astype(BF)
            for d in range(4):
                for h in range(2):
                    at = d * part + h * (part // 2)
                    g_up[h, y, d // 2, d % 2, kh, kl] = rows[at : at + part // 2]
        up.core_start(k)
        pl.when(i > 0)(lambda: pass_on(chunk_of(i - 1)))
        r.total[...] += dot(act, weight_down)
        r.t[...] += dot_nt(low, weight)
        pl.when(i == 0)(lambda: up_load(3).start())
        return 0

    lax.fori_loop(0, 4, chunk, 0)
    pass_on(chunk_of(3))
    pl.when(p.z == 1)(functools.partial(q_pass, 1))

    qkv_loads = [
        load(r.qkv_weight.at[:, pl.ds(i * D, D)], pool.at[1 + i], 14 + i) for i in range(3)
    ]
    for copy in qkv_loads:
        copy.start()

    nx[2] = r.total[...].astype(BF)
    result_store = pltpu.make_async_copy(nx.at[2], r.result, r.load_sems.at[17])
    result_store.start()
    cot = r.cot[...].astype(F32)
    after = r.after[...]
    mean, inverse = norm_stats(after)
    n = (after - mean) * inverse
    t = r.t[...]
    after_grad = cot + norm_back(t, row_of(r.v_second_gain), n, inverse)
    r.after[...] = after_grad
    after_low = after_grad.astype(BF)
    doT = r.doT
    doT[...] = dot_nt(pool[0], after_low).astype(BF)
    for h in range(HEADS):
        rows = slice(h * HEAD, (h + 1) * HEAD)
        stat[HEADS + h : HEADS + h + 1] = column_sum(doT[rows].astype(F32) * outT[rows])
    def group_rows_of(group):
        return pl.ds(pl.multiple_of(group * width, width), width)

    def do_copy(t, group):
        rows = group_rows_of(group)
        src = doT.at[rows] if isinstance(t, int) and t == 0 else doin.at[t - 1, rows]
        return send(src, doin.at[t, rows], r.do_sems, 2 * t + group, p.along_z(-1))

    def stat_copy(t):
        src = stat if isinstance(t, int) and t == 0 else stat_in.at[t - 1]
        return send(src, stat_in.at[t], r.stat_sems, t, p.along_z(-1))

    def do_send(t, group):
        pl.when(group == 0)(lambda: stat_copy(t).start())
        do_copy(t, group).start()

    def stat_wait(t):
        send(stat, stat_in.at[t], r.stat_sems, t, p.along_z(1)).wait_recv()

    def do_wait(t, group):
        rows = group_rows_of(group)
        send(doT.at[rows], doin.at[t, rows], r.do_sems, 2 * t + group, p.along_z(1)).wait_recv()
        pl.when(group == 0)(lambda: stat_wait(t))

    for group in range(2):
        pl.when(p.z >= 1)(functools.partial(do_send, 0, group))
    small[pl.ds(0, 1), :] = column_sum(after_grad)
    small[pl.ds(1, 1), :] = column_sum(t * n)
    small[pl.ds(2, 1), :] = column_sum(t)
    small[pl.ds(3, 1), :] = column_sum(cot)
    rows = dot(attT[...], after_low).astype(BF)
    part = D // 8
    for d in range(8):
        for h in range(2):
            at = d * part + h * (part // 2)
            g_out[h, d // 4, (d // 2) % 2, d % 2] = rows[at : at + part // 2]
    out.core_start(0)

    outT[...] = jnp.zeros((D, T), F32)
    key_grad, value_grad = r.key_grad, r.value_grad
    mixed = (kv.at[1, 0], kv.at[1, 1], kv.at[2, 0])

    def grads_of(s, group, queries, out_grads, sums, causal, for_queries, for_keys):
        heads = [group * GROUP + i for i in range(GROUP)]
        places = [head_rows(h) for h in heads]
        scores = [dot_tn(kv[s, 0, rows], queries[rows]) for rows in places]
        prob_grad = [dot_tn(kv[s, 1, rows], out_grads[rows]) for rows in places]
        scores = [masked(v, p.z - s, causal) for v in scores]
        probs = [jnp.exp2(v - sums[pl.ds(h, 1)]) for v, h in zip(scores, heads)]
        score_grad = [
            (v * (w - sums[pl.ds(HEADS + h, 1)])).astype(BF)
            for v, w, h in zip(probs, prob_grad, heads)
        ]
        if for_queries:
            query_add = [dot(kv[s, 0, rows], v) for v, rows in zip(score_grad, places)]
        if for_keys:
            probs = [v.astype(BF) for v in probs]
            key_add = [dot_nt(queries[rows], v) for v, rows in zip(score_grad, places)]
            value_add = [dot_nt(out_grads[rows], v) for v, rows in zip(probs, places)]
        for i, rows in enumerate(places):
            if for_queries:
                outT[rows] = outT[rows] + query_add[i]
            if for_keys and for_queries:
                key_grad[rows] = key_add[i]
                value_grad[rows] = value_add[i]
            elif for_keys:
                key_grad[rows] = key_grad[rows] + key_add[i]
                value_grad[rows] = value_grad[rows] + value_add[i]

    def query_step(i, _):
        grads_of(p.z - i // 2, lax.rem(i, 2), qT, doT, stat, False, True, False)
        return 0

    def own_step(group, _):
        grads_of(0, group, qT, doT, stat, True, True, True)
        return 0

    def key_step(t, group):
        pl.when((p.z == 0) & (group == 0))(lambda: q_wait(t))
        do_wait(t, group)
        pl.when(p.z >= 1)(lambda: do_send(t + 1, group))
        grads_of(0, group, qin.at[t], doin.at[t], stat_in.at[t], False, False, True)

    def proj_grad(group):
        rows = slice(group * width, (group + 1) * width)
        mixed[0][rows] = (outT[rows] * HEAD**-0.5).astype(BF)
        mixed[1][rows] = (key_grad[rows] * HEAD**-0.5).astype(BF)
        mixed[2][rows] = value_grad[rows].astype(BF)
        target = (r.g_p0, r.g_p1)[group]
        part = D // 8
        for i in range(3):
            piece = dot_nt(nxT[...], mixed[i][rows]).astype(BF)
            for d in range(8):
                for h in range(2):
                    at = d * part + h * (part // 2)
                    target[h, d // 4, (d // 2) % 2, d % 2, :, i * width : (i + 1) * width] = piece[
                        at : at + part // 2
                    ]
        projs[group].core_start(0)

    def norm_back_one():
        outT[...] = sum(dot(pool[1 + i], mixed[i][...]) for i in range(3))
        ones = jnp.ones((8, T), BF)
        rows = r.late_z.at[p.z]
        rows[pl.ds(3, 1), :] = dot_nt(ones, mixed[0][...])[0:1]
        rows[pl.ds(4, 1), :] = dot_nt(ones, mixed[2][...])[0:1]
        t1 = outT[...].T
        start = r.tok[...].astype(F32) + table_row
        mean, inverse = norm_stats(start)
        n = (start - mean) * inverse
        start_grad = r.after[...] + norm_back(t1, row_of(r.v_first_gain), n, inverse)
        r.norm_two[...] = start_grad.astype(BF)
        tokens_store.start()
        rows[pl.ds(0, 1), :] = column_sum(start_grad)
        rows[pl.ds(1, 1), :] = column_sum(t1 * n)
        rows[pl.ds(2, 1), :] = column_sum(t1)
        late.advance(0)

    tokens_store = pltpu.make_async_copy(r.norm_two, r.grad_tokens, r.load_sems.at[18])

    for copy in qkv_loads:
        copy.wait()
    lax.fori_loop(0, 2 * p.z, query_step, 0)
    lax.fori_loop(0, 2, own_step, 0)
    step = functools.partial

    ahead = (
        (
            (1, step(up.advance, 1)),
            (1, step(down.advance, 1)),
            (3, step(out.advance, 0)),
            (3, step(down.advance, 2)),
            (5, step(proj_grad, 0)),
        ),
        (
            (2, step(down.advance, 1)),
        ),
        (
        ),
        (
        ),
    )
    rest = (
        ((0, 1), step(down.advance, 1)),
        ((0,), step(up.advance, 1)),
        ((), step(early.advance, 0)),
        ((0,), step(proj_grad, 0)),
        ((0,), step(down.advance, 2)),
        ((), step(projs[0].advance, 0)),
        ((), step(proj_grad, 1)),
        ((), step(up.advance, 2)),
        ((), step(projs[1].advance, 0)),
        ((), norm_back_one),
        ((), step(projs[0].advance, 1)),
        ((), step(down.advance, 3)),
        ((), step(early.advance, 1)),
        ((), step(projs[1].advance, 1)),
        ((0,), step(out.advance, 0)),
        ((), step(up.advance, 3)),
        ((), step(early.advance, 2)),
        ((), step(projs[0].advance, 2)),
        ((), step(late.advance, 1)),
        ((), step(projs[1].advance, 2)),
        ((), step(down.advance, 4)),
        ((), step(out.advance, 1)),
        ((), step(projs[0].advance, 3)),
        ((), step(late.advance, 2)),
        ((), step(out.advance, 2)),
        ((), step(projs[1].advance, 3)),
        ((), step(early.advance, 3)),
        ((), step(late.advance, 3)),
        ((), step(up.advance, 4)),
        ((), step(out.advance, 3)),
        ((), step(projs[1].advance, 4)),
        ((), step(projs[0].advance, 4)),
        ((), step(out.advance, 4)),
    )

    def half_round(i, _):
        for z in range(3):
            for at, one in ahead[z]:
                pl.when((p.z == z) & (i == at))(one)
        pl.when(p.z + i // 2 < 3)(lambda: key_step(i // 2, lax.rem(i, 2)))
        return 0

    for _, one in ahead[3]:
        pl.when(p.z == 3)(one)
    lax.fori_loop(0, 7, half_round, 0)
    for done, one in rest:
        if len(done) == 0:
            one()
        else:
            planes = [z for z in range(4) if z not in done]
            if planes:
                pl.when(functools.reduce(jnp.logical_or, [p.z == z for z in planes]))(one)
    for s in (1, 2):
        for half in range(2):
            pl.when((p.z < 3) & (p.z >= s))(lambda s=s, half=half: nx_copy(s, half).wait_send())
    def sent(t):
        q_copy(t).wait_send()
        stat_copy(t).wait_send()
        do_copy(t, 0).wait_send()
        do_copy(t, 1).wait_send()

    for t in range(3):
        pl.when((p.z >= 1) & (p.z + t <= 3))(functools.partial(sent, t))
    stores["s_qkv"].start()
    result_store.wait()
    tokens_store.wait()
    for copy in stores.values():
        copy.wait()

def row_of(ref):
    return ref[...].reshape(1, ref.shape[0])


def outputs_kernel(result, grad_tokens, early, late, s_qkv, s_out, s_up, s_down, *outs):
    (
        o_result,
        o_tokens,
        o_table,
        o_first_gain,
        o_first_shift,
        o_qkv,
        o_qv_bias,
        o_out,
        o_out_bias,
        o_second_gain,
        o_second_shift,
        o_up,
        o_up_bias,
        o_down,
        o_down_bias,
    ) = outs
    D = early.shape[1]
    o_result[...] = result[...].reshape(o_result.shape)
    o_tokens[...] = grad_tokens[...].reshape(o_tokens.shape)
    o_table[...] = late[0:16]
    o_first_gain[...] = late[16]
    o_first_shift[...] = late[17]
    o_out_bias[...] = early[0]
    o_second_gain[...] = early[1]
    o_second_shift[...] = early[2]
    o_down_bias[...] = early[3]
    for k in range(4):
        o_up_bias[pl.ds(k * D, D)] = early[4 + k]
    o_qv_bias[...] = late[18:20]
    for ref, value in ((o_qkv, s_qkv), (o_out, s_out), (o_up, s_up), (o_down, s_down)):
        half = value.shape[1]
        for h in range(2):
            ref[h * half : (h + 1) * half] = value[h]


def fused(
    tokens,
    group_ids,
    lengths,
    cotangent,
    group_table,
    first_gain,
    first_shift,
    qkv_weight,
    query_value_bias,
    out_weight,
    out_bias,
    second_gain,
    second_shift,
    up_weight,
    up_bias,
    down_weight,
    down_bias,
):
    _, T, D = tokens.shape
    F = up_weight.shape[1]
    any_spec = pl.BlockSpec(memory_space=pl.ANY)
    vmem = pl.BlockSpec(memory_space=pltpu.VMEM)
    smem = pl.BlockSpec(memory_space=pltpu.SMEM)
    inputs = dict(
        tokens=(tokens.reshape(T, D), any_spec),
        group_ids=(group_ids, smem),
        lengths=(lengths, smem),
        cotangent=(cotangent.reshape(T, D), any_spec),
        group_table=(group_table, any_spec),
        first_gain=(first_gain, any_spec),
        first_shift=(first_shift, any_spec),
        qkv_weight=(qkv_weight, any_spec),
        qv_bias=(query_value_bias, any_spec),
        out_weight=(out_weight, any_spec),
        out_bias=(out_bias, any_spec),
        second_gain=(second_gain, any_spec),
        second_shift=(second_shift, any_spec),
        up_weight=(up_weight, any_spec),
        up_bias=(up_bias, any_spec),
        down_weight=(down_weight, any_spec),
        down_bias=(down_bias, any_spec),
    )
    shares = dict(
        down=(D // 8, F // 8),
        up=(D // 16, F // 4),
        out=(D // 16, D // 4),
        qkv=(D // 16, 3 * D // 4),
    )
    outputs = dict(
        result=((T, D), BF),
        grad_tokens=((T, D), BF),
        early_out=((8, D), F32),
        late_out=((20, D), F32),
    )
    outputs.update({"s_" + k: ((2,) + shares[k], F32) for k in ("qkv", "out", "up", "down")})
    dma = pltpu.SemaphoreType.DMA
    scratch = dict(
        pool=pltpu.VMEM((8, D, D), BF),
        v_group_table=pltpu.VMEM(group_table.shape, F32),
        v_first_gain=pltpu.VMEM((D,), F32),
        v_first_shift=pltpu.VMEM((D,), F32),
        v_qv_bias=pltpu.VMEM((2, D), F32),
        v_out_bias=pltpu.VMEM((D,), F32),
        v_second_gain=pltpu.VMEM((D,), F32),
        v_second_shift=pltpu.VMEM((D,), F32),
        v_up_bias=pltpu.VMEM((F,), F32),
        v_down_bias=pltpu.VMEM((D,), F32),
        tok=pltpu.VMEM((T, D), BF),
        cot=pltpu.VMEM((T, D), BF),
        cotT=pltpu.VMEM((D, T), BF),
        nx=pltpu.VMEM((3, T, D), BF),
        nxT=pltpu.VMEM((D, T), BF),
        qT=pltpu.VMEM((D, T), BF),
        kv=pltpu.VMEM((4, 2, D, T), BF),
        outT=pltpu.VMEM((D, T), F32),
        stat=pltpu.VMEM((2 * HEADS, T), F32),
        mass=pltpu.VMEM((HEADS, T), F32),
        qin=pltpu.VMEM((3, D, T), BF),
        doin=pltpu.VMEM((3, D, T), BF),
        stat_in=pltpu.VMEM((3, 2 * HEADS, T), F32),
        key_grad=pltpu.VMEM((D, T), F32),
        value_grad=pltpu.VMEM((D, T), F32),
        attT=pltpu.VMEM((D, T), BF),
        after=pltpu.VMEM((T, D), F32),
        norm_two=pltpu.VMEM((T, D), BF),
        norm_twoT=pltpu.VMEM((D, T), BF),
        act_grad=pltpu.VMEM((2, T, D), F32),
        total=pltpu.VMEM((T, D), F32),
        t=pltpu.VMEM((T, D), F32),
        doT=pltpu.VMEM((D, T), BF),
        up_rows=pltpu.VMEM((4, D), F32),
        early_z=pltpu.VMEM((4, 8, D), F32),
        early_c=pltpu.VMEM((2, 8, D), F32),
        early_x=pltpu.VMEM((4, 8, D), F32),
        late_z=pltpu.VMEM((4, 5, D), F32),
        late_c=pltpu.VMEM((2, 20, D), F32),
        late_x=pltpu.VMEM((4, 20, D), F32),
        load_sems=dma((29,)),
        nx_sems=dma((2, 6)),
        q_sems=dma((2, 3)),
        do_sems=dma((2, 6)),
        stat_sems=dma((2, 3)),
        early_sems=dma((2, 7)),
        late_sems=dma((2, 7)),
    )
    places = dict(
        down=(2, 2, D // 8, F // 8),
        up=(2, 2, D // 16, F // 4),
        out=(D // 16, D),
        p0=(D // 16, 3 * D // 2),
        p1=(D // 16, 3 * D // 2),
    )
    columns_of = dict(shares, p0=(D // 16, D // 2), p1=(D // 16, D // 2))
    for name, place in places.items():
        rows, columns = columns_of[name]
        extra = {
            "g_" + name: pltpu.VMEM((2, 2, 2, 2) + place, BF),
            "rc_" + name: pltpu.VMEM((2, 2, 2) + place, BF),
            "r1_" + name: pltpu.VMEM((2, 2) + place, BF),
            "r2_" + name: pltpu.VMEM((2,) + place, BF),
            "rz1_" + name: pltpu.VMEM((2, 2, rows, columns), BF),
            "rz2_" + name: pltpu.VMEM((2, rows, columns), BF),
            "cs_" + name: dma((2, 4)),
            "ss_" + name: dma((2, 12)),
        }
        if len(place) == 2:
            extra["zb_" + name] = pltpu.VMEM((2, 2, 2, rows, columns), BF)
        scratch.update(extra)
    scratch.update({"o_" + name: pltpu.VMEM(*outputs[name]) for name in RESULTS})
    scratch["store_sems"] = dma((len(RESULTS),))
    names = list(inputs) + list(outputs) + list(scratch)
    done = pl.pallas_call(
        functools.partial(layer_kernel, names),
        name="layer",
        out_shape=[jax.ShapeDtypeStruct(*o) for o in outputs.values()],
        in_specs=[i[1] for i in inputs.values()],
        out_specs=[any_spec] * len(outputs),
        scratch_shapes=list(scratch.values()),
        compiler_params=pltpu.CompilerParams(
            collective_id=0, has_side_effects=True, vmem_limit_bytes=VMEM_LIMIT
        ),
    )(*[i[0] for i in inputs.values()])
    shape = jax.ShapeDtypeStruct
    outs = pl.pallas_call(
        outputs_kernel,
        name="outputs",
        out_shape=[
            shape((1, T, D), BF),
            shape((1, T, D), BF),
            shape((16, D), F32),
            shape((D,), F32),
            shape((D,), F32),
            shape((D // 8, 3 * D // 4), F32),
            shape((2, D), F32),
            shape((D // 8, D // 4), F32),
            shape((D,), F32),
            shape((D,), F32),
            shape((D,), F32),
            shape((D // 8, F // 4), F32),
            shape((F,), F32),
            shape((D // 4, F // 8), F32),
            shape((D,), F32),
        ],
        in_specs=[vmem] * len(done),
        out_specs=[vmem] * 15,
    )(*done)
    return (*outs[:13], outs[13].T, outs[14])


def shifted(array, axis, by):
    devices = lax.axis_size(axis)
    pairs = [(i, i + by) for i in range(devices) if 0 <= i + by < devices]
    return lax.ppermute(array, axis, pairs)


def as_sent(array):
    return jax.tree.map(lambda a: a.astype(jnp.bfloat16) if a.dtype == jnp.float32 else a, array)


def shifted_2(block, axis, distance):
    devices = range(lax.axis_size(axis))
    route = [((i - distance) % len(devices), i) for i in devices]
    return lax.ppermute(block, axis, route)


def layer_norm(inputs, norm_gain, norm_shift):
    average = jnp.mean(inputs, -1, keepdims=True)
    centred = inputs - average
    inverse = lax.rsqrt(jnp.mean(centred * centred, -1, keepdims=True) + EPSILON)
    return centred * inverse * norm_gain + norm_shift


def tanh_gelu(inputs):
    return jax.nn.gelu(inputs, approximate=True)


def keep_same(state_value):
    return state_value


def scores_of(queries, key_piece, key_start, query_start, lengths):
    sequences, block_len = (queries.shape[0], queries.shape[1])
    key_heads = key_piece.reshape(sequences, key_piece.shape[1], HEADS, HEAD)
    raw_scores = jnp.einsum(
        "gqhe,gkhe->ghqk", queries, key_heads, preferred_element_type=jnp.float32
    ) * HEAD ** (-0.5)
    key_pos = key_start + jnp.arange(key_piece.shape[1])
    query_pos = query_start + jnp.arange(block_len)
    allowed = (query_pos[:, None] >= key_pos[None, :])[None] & (
        key_pos[None, None, :] < lengths[:, None, None]
    )
    return (raw_scores, allowed[:, None])


def plain(
    tokens,
    group_ids,
    lengths,
    cotangent,
    group_table,
    first_gain,
    first_shift,
    qkv_weight,
    query_value_bias,
    out_weight,
    out_bias,
    second_gain,
    second_shift,
    up_weight,
    up_bias,
    down_weight,
    down_bias,
):
    sequences, block_len, features = tokens.shape
    token_rows = sequences * block_len
    seq_count = lax.axis_size("seq")
    seq_index = lax.axis_index("seq")
    query_start = seq_index * block_len
    score_scale = HEAD ** (-0.5)
    one_hot = (group_ids[:, None] == jnp.arange(group_table.shape[0])[None, :]).astype(jnp.float32)
    table_rows = jnp.dot(one_hot, group_table, precision=EXACT)
    start_rows = (tokens.astype(jnp.float32) + table_rows[:, None, :]).reshape(token_rows, features)
    norm_one, pull_one = jax.vjp(layer_norm, start_rows, first_gain, first_shift)
    norm_one_low = norm_one.astype(jnp.bfloat16)
    full_bias = jnp.concatenate(
        [query_value_bias[0], jnp.zeros((features,), jnp.float32), query_value_bias[1]]
    )
    mixed_rows = (
        jnp.dot(norm_one_low, qkv_weight, preferred_element_type=jnp.float32) + full_bias
    ).astype(jnp.bfloat16)
    mixed_rows = mixed_rows.reshape(sequences, block_len, 3 * features)
    queries = mixed_rows[:, :, :features].reshape(sequences, block_len, HEADS, HEAD)
    key_rows = mixed_rows[:, :, features : 2 * features]
    values = mixed_rows[:, :, 2 * features :]
    pieces = []
    current = (key_rows, values)
    for cycle_step in range(seq_count):
        if cycle_step > 0:
            current = shifted((current[0], current[1]), "seq", 1)
        anchor = (seq_index - cycle_step) % seq_count
        pieces.append((current[0], current[1], anchor * block_len, cycle_step <= seq_index))
    shape_rows = (sequences, HEADS, block_len)
    row_max = jnp.full(shape_rows, NEG_LARGE, jnp.float32)
    row_sum = jnp.zeros(shape_rows, jnp.float32)
    stored = []
    for key_piece, value_piece, key_start, active in pieces:

        def visit_block(state_pair, key_piece=key_piece, key_start=key_start):
            raw_scores, allowed = scores_of(queries, key_piece, key_start, query_start, lengths)
            masked_scores = jnp.where(allowed, raw_scores, NEG_LARGE)
            new_max = jnp.maximum(state_pair[0], jnp.max(masked_scores, -1))
            weights = jnp.where(allowed, jnp.exp(masked_scores - new_max[..., None]), 0.0)
            return (
                new_max,
                state_pair[1] * jnp.exp(state_pair[0] - new_max) + jnp.sum(weights, -1),
                masked_scores,
            )

        def pass_block(state_pair):
            return (
                state_pair[0],
                state_pair[1],
                jnp.full(shape_rows + (block_len,), NEG_LARGE, jnp.float32),
            )

        row_max, row_sum, masked_scores = lax.cond(
            active, visit_block, pass_block, (row_max, row_sum)
        )
        stored.append(masked_scores)
    log_sum = row_max + jnp.log(row_sum)
    attended = jnp.zeros((sequences, block_len, HEADS, HEAD), jnp.float32)
    for piece_data, masked_scores in zip(pieces, stored):

        def attend_block(total_out, value_piece=piece_data[1], masked_scores=masked_scores):
            probs = jnp.exp(masked_scores - log_sum[..., None]).astype(jnp.bfloat16)
            value_heads = value_piece.reshape(sequences, block_len, HEADS, HEAD)
            return total_out + jnp.einsum(
                "ghqk,gkhe->gqhe", probs, value_heads, preferred_element_type=jnp.float32
            )

        attended = lax.cond(piece_data[3], attend_block, keep_same, attended)
    attended_low = attended.reshape(token_rows, features).astype(jnp.bfloat16)
    after_attn = (
        start_rows
        + jnp.dot(attended_low, out_weight, preferred_element_type=jnp.float32)
        + out_bias
    )
    norm_two, pull_two = jax.vjp(layer_norm, after_attn, second_gain, second_shift)
    norm_two_low = norm_two.astype(jnp.bfloat16)
    up_rows = jnp.dot(norm_two_low, up_weight, preferred_element_type=jnp.float32) + up_bias
    activated, pull_gelu = jax.vjp(tanh_gelu, up_rows)
    activated_low = activated.astype(jnp.bfloat16)
    result_rows = (
        after_attn
        + jnp.dot(activated_low, down_weight, preferred_element_type=jnp.float32)
        + down_bias
    )
    result = result_rows.astype(jnp.bfloat16).reshape(tokens.shape)
    outer_low = cotangent.reshape(token_rows, features)
    outer_grad = outer_low.astype(jnp.float32)
    grad_down_weight = jnp.dot(activated_low.T, outer_low, preferred_element_type=jnp.float32)
    grad_down_bias = jnp.sum(outer_grad, 0)
    up_grad = pull_gelu(jnp.dot(outer_low, down_weight.T, preferred_element_type=jnp.float32))[0]
    grad_up_bias = jnp.sum(up_grad, 0)
    up_low = up_grad.astype(jnp.bfloat16)
    grad_up_weight = jnp.dot(norm_two_low.T, up_low, preferred_element_type=jnp.float32)
    part_after, grad_second_gain, grad_second_shift = pull_two(
        jnp.dot(up_low, up_weight.T, preferred_element_type=jnp.float32)
    )
    after_grad = outer_grad + part_after
    grad_out_bias = jnp.sum(after_grad, 0)
    after_low = after_grad.astype(jnp.bfloat16)
    grad_out_weight = jnp.dot(attended_low.T, after_low, preferred_element_type=jnp.float32)
    out_grad = jnp.dot(after_low, out_weight.T, preferred_element_type=jnp.float32).astype(
        jnp.bfloat16
    )
    out_grad = out_grad.reshape(sequences, block_len, HEADS, HEAD)
    delta = jnp.transpose(jnp.sum(out_grad.astype(jnp.float32) * attended, -1), (0, 2, 1))

    def back_block(query_grad, key_piece, value_piece, key_start):
        raw_scores, allowed = scores_of(queries, key_piece, key_start, query_start, lengths)
        probs = jnp.where(allowed, jnp.exp(raw_scores - log_sum[..., None]), 0.0)
        value_heads = value_piece.reshape(sequences, block_len, HEADS, HEAD)
        key_heads = key_piece.reshape(sequences, block_len, HEADS, HEAD)
        prob_grad = jnp.einsum(
            "gqhe,gkhe->ghqk", out_grad, value_heads, preferred_element_type=jnp.float32
        )
        score_grad = (probs * (prob_grad - delta[..., None])).astype(jnp.bfloat16)
        query_grad = (
            query_grad
            + jnp.einsum(
                "ghqk,gkhe->gqhe", score_grad, key_heads, preferred_element_type=jnp.float32
            )
            * score_scale
        )
        key_add = (
            jnp.einsum("ghqk,gqhe->gkhe", score_grad, queries, preferred_element_type=jnp.float32)
            * score_scale
        )
        value_add = jnp.einsum(
            "ghqk,gqhe->gkhe",
            probs.astype(jnp.bfloat16),
            out_grad,
            preferred_element_type=jnp.float32,
        )
        return (
            query_grad,
            key_add.reshape(sequences, block_len, features),
            value_add.reshape(sequences, block_len, features),
        )

    empty_rows = jnp.zeros((sequences, block_len, features), jnp.float32)

    def skip_back(query_grad):
        return (query_grad, empty_rows, empty_rows)

    query_grad = jnp.zeros((sequences, block_len, HEADS, HEAD), jnp.float32)
    carried = (empty_rows, empty_rows)
    for cycle_step in range(seq_count):
        piece_data = pieces[cycle_step]

        def visit_back(state_grad, piece_data=piece_data):
            return back_block(state_grad, piece_data[0], piece_data[1], piece_data[2])

        query_grad, key_add, value_add = lax.cond(piece_data[3], visit_back, skip_back, query_grad)
        carried = shifted_2(
            (as_sent(carried[0] + key_add), as_sent(carried[1] + value_add)), "seq", 1
        )
    key_grad, value_grad = carried
    query_flat = query_grad.reshape(token_rows, features)
    key_flat = key_grad.reshape(token_rows, features)
    value_flat = value_grad.reshape(token_rows, features)
    grad_query_value_bias = jnp.stack([jnp.sum(query_flat, 0), jnp.sum(value_flat, 0)])
    mixed_grad = jnp.concatenate([query_flat, key_flat, value_flat], -1).astype(jnp.bfloat16)
    grad_qkv_weight = jnp.dot(norm_one_low.T, mixed_grad, preferred_element_type=jnp.float32)
    part_start, grad_first_gain, grad_first_shift = pull_one(
        jnp.dot(mixed_grad, qkv_weight.T, preferred_element_type=jnp.float32)
    )
    start_grad = after_grad + part_start
    grad_tokens = start_grad.astype(jnp.bfloat16).reshape(tokens.shape)
    grad_group_table = jnp.dot(
        one_hot.T, jnp.sum(start_grad.reshape(sequences, block_len, features), 1), precision=EXACT
    )
    small_sums = lax.psum(
        (
            grad_group_table,
            grad_first_gain,
            grad_first_shift,
            grad_query_value_bias,
            grad_out_bias,
            grad_second_gain,
            grad_second_shift,
            grad_up_bias,
            grad_down_bias,
        ),
        ("dp", "seq"),
    )
    matrices = (grad_qkv_weight, grad_out_weight, grad_up_weight, grad_down_weight)
    shares = (
        lax.psum_scatter(
            matrices[0].astype(jnp.bfloat16), "seq", scatter_dimension=1, tiled=True
        ).astype(jnp.float32),
        lax.psum_scatter(
            matrices[1].astype(jnp.bfloat16), "seq", scatter_dimension=1, tiled=True
        ).astype(jnp.float32),
        lax.psum_scatter(
            matrices[2].astype(jnp.bfloat16), "seq", scatter_dimension=1, tiled=True
        ).astype(jnp.float32),
        lax.psum_scatter(
            matrices[3].astype(jnp.bfloat16), "seq", scatter_dimension=1, tiled=True
        ).astype(jnp.float32),
    )
    shares = (
        lax.psum_scatter(
            shares[0].astype(jnp.bfloat16), "dp", scatter_dimension=0, tiled=True
        ).astype(jnp.float32),
        lax.psum_scatter(
            shares[1].astype(jnp.bfloat16), "dp", scatter_dimension=0, tiled=True
        ).astype(jnp.float32),
        lax.psum_scatter(
            shares[2].astype(jnp.bfloat16), "dp", scatter_dimension=0, tiled=True
        ).astype(jnp.float32),
        lax.psum_scatter(
            shares[3].astype(jnp.bfloat16), "dp", scatter_dimension=0, tiled=True
        ).astype(jnp.float32),
    )
    return (
        result,
        grad_tokens,
        small_sums[0],
        small_sums[1],
        small_sums[2],
        shares[0],
        small_sums[3],
        shares[1],
        small_sums[4],
        small_sums[5],
        small_sums[6],
        shares[2],
        small_sums[7],
        shares[3],
        small_sums[8],
    )


def solution(mesh):
    in_specs = (
        P("dp", "seq", None),
        P("dp"),
        P("dp"),
        P("dp", "seq", None),
        P(),
        P(),
        P(),
        P(),
        P(),
        P(),
        P(),
        P(),
        P(),
        P(),
        P(),
        P(),
        P(),
    )
    out_specs = (
        P("dp", "seq", None),
        P("dp", "seq", None),
        P(),
        P(),
        P(),
        P("dp", "seq"),
        P(),
        P("dp", "seq"),
        P(),
        P(),
        P(),
        P("dp", "seq"),
        P(),
        P("dp", "seq"),
        P(),
    )
    def shards(*arrays):
        sizes = (mesh.shape["dp"], mesh.shape["seq"]) + arrays[0].shape
        return (fused if sizes == (8, 4, 1, 256, 768) else plain)(*arrays)

    return jax.shard_map(shards, mesh=mesh, in_specs=in_specs, out_specs=out_specs, check_vma=False)
```

```python
import functools
import math
import types

import jax
import jax.numpy as jnp
from jax import lax
from jax.experimental import pallas as pl
from jax.experimental.pallas import tpu as pltpu
from jax.sharding import PartitionSpec as P

HEADS = 12
HEAD = 64


EPSILON = 1e-05
NEG_LARGE = -1e30
EXACT = lax.Precision.HIGHEST


VMEM_LIMIT = 64 << 20
GROUP = 6


BF = jnp.bfloat16
VECTORS = (
    "group_table",
    "first_gain",
    "first_shift",
    "qv_bias",
    "out_bias",
    "second_gain",
    "second_shift",
    "up_bias",
    "down_bias",
)
F32 = jnp.float32
MESH = pl.DeviceIdType.MESH
LOG2E = 1.4426950408889634


def dot(a, b):
    return lax.dot_general(a, b, (((1,), (0,)), ((), ())), preferred_element_type=F32)


def dot_nt(a, b):
    return lax.dot_general(a, b, (((1,), (1,)), ((), ())), preferred_element_type=F32)


def dot_tn(a, b):
    return lax.dot_general(a, b, (((0,), (0,)), ((), ())), preferred_element_type=F32)


def flipped(index, bit):
    return index + bit - 2 * bit * lax.rem(index // bit, 2)


class Place:
    def __init__(self):
        self.d = lax.axis_index("dp")
        self.z = lax.axis_index("seq")
        self.c = lax.rem(self.d, 2)
        self.x = lax.rem(self.d // 2, 2)
        self.y = lax.rem(self.d // 4, 2)
        self.zl = lax.rem(self.z, 2)
        self.zh = lax.rem(self.z // 2, 2)
        self.core = (flipped(self.d, 1), self.z)
        self.along_x = (flipped(self.d, 2), self.z)
        self.along_y = (flipped(self.d, 4), self.z)
        self.z_near = (self.d, flipped(self.z, 1))
        self.z_far = (self.d, flipped(self.z, 2))
        self.z_mirror = (self.d, 3 - self.z)
        self.diagonal = (flipped(flipped(self.d, 2), 4), self.z)

    def along_z(self, k):
        return (self.d, self.z + k)


def send(src, dst, sems, index, to):
    copy = pltpu.make_async_remote_copy(
        src_ref=src,
        dst_ref=dst,
        send_sem=sems.at[0, index],
        recv_sem=sems.at[1, index],
        device_id=to,
        device_id_type=MESH,
    )
    return copy


class ReduceScatter:
    def __init__(
        self, place, g, rc, r1, r2, rz1, rz2, core_sems, sems, parts, out, zb=None, columns=None
    ):
        self.p, self.g, self.rc, self.r1, self.r2 = place, g, rc, r1, r2
        self.rz1, self.rz2, self.core_sems, self.sems, self.parts = rz1, rz2, core_sems, sems, parts
        self.count = 4 if parts else 1
        self.out, self.columns = out, columns
        self.zb = g.at[:, place.y, place.x, place.c] if zb is None else zb

    def core_copy(self, k):
        p = self.p
        kh, kl = k // 2, lax.rem(k, 2)
        if self.parts == "yx":
            src, dst = self.g.at[:, kh, kl, 1 - p.c], self.rc.at[:, kh, kl]
        elif self.parts == "z":
            src, dst = self.g.at[:, :, :, 1 - p.c, kh, kl], self.rc.at[:, :, :, kh, kl]
        else:
            src, dst = self.g.at[:, :, :, 1 - p.c], self.rc
        return send(src, dst, self.core_sems, k, p.core)

    def core_start(self, k):
        self.core_copy(k).start()

    def core_sum(self, k):
        p, g, rc = self.p, self.g, self.rc
        kh, kl = k // 2, lax.rem(k, 2)
        self.core_copy(k).wait()
        if self.parts == "yx":
            for h in range(2):
                g[h, kh, kl, p.c] = g[h, kh, kl, p.c] + rc[h, kh, kl]
            return

        def add(i, _):
            h, y, x = i // 4, lax.rem(i // 2, 2), lax.rem(i, 2)
            if self.parts == "z":
                g[h, y, x, p.c, kh, kl] = g[h, y, x, p.c, kh, kl] + rc[h, y, x, kh, kl]
            else:
                g[h, y, x, p.c] = g[h, y, x, p.c] + rc[h, y, x]
            return 0

        lax.fori_loop(0, 8, add, 0)

    def first_x(self, k):
        p, g, r1 = self.p, self.g, self.r1
        kh, kl = k // 2, lax.rem(k, 2)
        if self.parts == "yx":
            return send(g.at[0, kh, 1 - p.x, p.c], r1.at[0, kh], self.sems, kh, p.along_x)
        if self.parts == "z":
            return send(
                g.at[0, :, 1 - p.x, p.c, kh, kl], r1.at[0, :, kh, kl], self.sems, k, p.along_x
            )
        return send(g.at[0, :, 1 - p.x, p.c], r1.at[0], self.sems, 0, p.along_x)

    def first_y(self, k):
        p, g, r1 = self.p, self.g, self.r1
        kh, kl = k // 2, lax.rem(k, 2)
        if self.parts == "yx":
            return send(g.at[1, 1 - p.y, kl, p.c], r1.at[1, kl], self.sems, 4 + kl, p.along_y)
        if self.parts == "z":
            return send(
                g.at[1, 1 - p.y, :, p.c, kh, kl], r1.at[1, :, kh, kl], self.sems, 4 + k, p.along_y
            )
        return send(g.at[1, 1 - p.y, :, p.c], r1.at[1], self.sems, 4, p.along_y)

    def first_start(self, k):
        p = self.p
        if self.parts == "yx":
            pl.when(lax.rem(k, 2) != p.x)(lambda: self.first_x(k).start())
            pl.when(k // 2 != p.y)(lambda: self.first_y(k).start())
        else:
            self.first_x(k).start()
            self.first_y(k).start()

    def first_sum(self):
        p, g = self.p, self.g
        if self.parts == "yx":
            for i in range(2):
                self.first_x(2 * i).wait()
                self.first_y(i).wait()
        else:
            for k in range(self.count):
                self.first_x(k).wait()
                self.first_y(k).wait()
        for i in range(2):
            g[0, i, p.x, p.c] = g[0, i, p.x, p.c] + self.r1[0, i]
            g[1, p.y, i, p.c] = g[1, p.y, i, p.c] + self.r1[1, i]

    def second_copies(self):
        p, g = self.p, self.g
        return (
            send(g.at[0, 1 - p.y, p.x, p.c], self.r2.at[0], self.sems, 8, p.along_y),
            send(g.at[1, p.y, 1 - p.x, p.c], self.r2.at[1], self.sems, 9, p.along_x),
        )

    def second_start(self):
        for copy in self.second_copies():
            copy.start()

    def second_sum(self):
        p, g = self.p, self.g
        for copy in self.second_copies():
            copy.wait()
        for h in range(2):
            total = g[h, p.y, p.x, p.c] + self.r2[h]
            if self.columns is None:
                g[h, p.y, p.x, p.c] = total
            else:
                for z, (first, last) in enumerate(self.columns):
                    self.zb[h, z // 2, z % 2] = total[:, first:last]

    def third_copy(self):
        p = self.p
        return send(self.zb.at[:, :, 1 - p.zl], self.rz1, self.sems, 10, p.z_near)

    def third_start(self):
        self.third_copy().start()

    def third_sum(self):
        p, zb = self.p, self.zb
        self.third_copy().wait()
        for h in range(2):
            for i in range(2):
                zb[h, i, p.zl] = zb[h, i, p.zl] + self.rz1[h, i]

    def fourth_copy(self):
        p = self.p
        return send(self.zb.at[:, 1 - p.zh, p.zl], self.rz2, self.sems, 11, p.z_far)

    def fourth_start(self):
        self.fourth_copy().start()

    def fourth_sum(self):
        p, zb = self.p, self.zb
        self.fourth_copy().wait()
        for h in range(2):
            total = zb[h, p.zh, p.zl].astype(F32) + self.rz2[h].astype(F32)
            if callable(self.out):
                self.out(h, total)
            else:
                self.out[h] = total

    def advance(self, step):
        if step == 0:
            self.core_sum(0)
            self.first_start(0)
        elif step == 1:
            self.first_sum()
            self.second_start()
        elif step == 2:
            self.second_sum()
            self.third_start()
        elif step == 3:
            self.third_sum()
            self.fourth_start()
        else:
            self.fourth_sum()


class SmallSum:
    def __init__(self, place, zin, cin, xin, sems, out, spread):
        self.p, self.zin, self.cin, self.xin, self.sems = place, zin, cin, xin, sems
        self.out, self.spread = out, spread
        self.corner = place.d // 2

    def z_copies(self):
        p, mine = self.p, self.zin.at[self.p.z]
        peers = (p.z_near, p.z_far, p.z_mirror)
        return [send(mine, mine, self.sems, i, to) for i, to in enumerate(peers)]

    def core_copy(self):
        return send(self.cin.at[0], self.cin.at[1], self.sems, 3, self.p.core)

    def xy_copies(self):
        p, mine = self.p, self.xin.at[self.corner]
        peers = (p.along_x, p.along_y, p.diagonal)
        return [send(mine, mine, self.sems, 4 + i, to) for i, to in enumerate(peers)]

    def advance(self, step):
        cin, zin, xin = self.cin, self.zin, self.xin
        if step == 0:
            for copy in self.z_copies():
                copy.start()
        elif step == 1:
            for copy in self.z_copies():
                copy.wait()
            cin[0] = self.spread(zin[0] + zin[1] + zin[2] + zin[3])
            self.core_copy().start()
        elif step == 2:
            self.core_copy().wait()
            xin[self.corner] = cin[0] + cin[1]
            for copy in self.xy_copies():
                copy.start()
        else:
            for copy in self.xy_copies():
                copy.wait()
            self.out[...] = xin[0] + xin[1] + xin[2] + xin[3]


def norm_stats(v):
    mean = jnp.mean(v, axis=-1, keepdims=True)
    centred = v - mean
    inverse = lax.rsqrt(jnp.mean(centred * centred, axis=-1, keepdims=True) + EPSILON)
    return mean, inverse


def norm_back(t, gain, n, inverse):
    u = t * gain
    return inverse * (
        u - jnp.mean(u, axis=-1, keepdims=True) - n * jnp.mean(u * n, axis=-1, keepdims=True)
    )


def column_sum(v):
    return jnp.sum(v, axis=0, keepdims=True)


def layer_kernel(names, *refs):
    r = types.SimpleNamespace(**dict(zip(names, refs)))
    p = Place()
    T, D = r.tokens.shape

    barrier = pltpu.get_barrier_semaphore()
    partners = (p.core, p.along_x, p.along_y, p.diagonal, p.z_near, p.z_far, p.z_mirror)
    for partner in partners:
        pl.semaphore_signal(barrier, inc=1, device_id=partner, device_id_type=MESH)

    pool = r.pool

    def load(src, dst, index):
        return pltpu.make_async_copy(src, dst, r.load_sems.at[index])

    def chunk_of(i):
        flip_y, flip_x = 1 - lax.rem(i, 2), 1 - i // 2
        return 2 * (p.y + flip_y - 2 * flip_y * p.y) + p.x + flip_x - 2 * flip_x * p.x

    def up_load(i):
        src = r.up_weight.at[:, pl.ds(pl.multiple_of(chunk_of(i) * D, D), D)]
        return load(src, pool.at[1 + i], 6 + i)

    def down_load(i):
        src = r.down_weight.at[pl.ds(pl.multiple_of(chunk_of(i) * D, D), D), :]
        return load(src, pool.at[4 + i], 10 + i)

    tokens_load = load(r.tokens, r.tok, 0)
    tokens_load.start()
    vectors = [
        load(getattr(r, name), getattr(r, "v_" + name), 20 + i) for i, name in enumerate(VECTORS)
    ]
    for copy in vectors:
        copy.start()
    qkv_loads = [
        load(r.qkv_weight.at[:, pl.ds(i * D, D)], pool.at[1 + i], 1 + i) for i in range(3)
    ]
    for i in (1, 2, 0):
        qkv_loads[i].start()
    cot_load = load(r.cotangent, r.cot, 4)
    out_load = load(r.out_weight, pool.at[0], 5)
    for copy in [cot_load] + [down_load(i) for i in range(4)] + [out_load]:
        copy.start()

    gid = r.group_ids[0]
    length = r.lengths[0]
    for copy in vectors:
        copy.wait()
    table = r.v_group_table[...]
    group_rows = lax.broadcasted_iota(jnp.int32, table.shape, 0)
    table_row = jnp.sum(jnp.where(group_rows == gid, table, 0.0), axis=0, keepdims=True)
    tokens_load.wait()
    start = r.tok[...].astype(F32) + table_row
    mean, inverse = norm_stats(start)
    nx, nxT = r.nx, r.nxT
    r.norm_two[...] = ((start - mean) * inverse * row_of(r.v_first_gain) + row_of(r.v_first_shift)).astype(BF)

    pl.semaphore_wait(barrier, len(partners))

    def nx_copy(s, half):
        rows = pl.ds(half * (T // 2), T // 2)
        own = isinstance(s, int) and s == 0
        src = r.norm_two.at[rows] if own else nx.at[s - 1, rows]
        return send(src, nx.at[s, rows], r.nx_sems, 2 * s + half, p.along_z(1))

    def nx_pass(s, half):
        rows = pl.ds(half * (T // 2), T // 2)
        here = nx.at[s - 1, rows]
        send(here, here, r.nx_sems, 2 * (s - 1) + half, p.along_z(-1)).wait_recv()
        pl.when((s < 3) & (p.z < 3))(lambda: nx_copy(s, half).start())

    kv, qT, outT, stat, mass = r.kv, r.qT, r.outT, r.stat, r.mass
    qin, doin, stat_in = r.qin, r.doin, r.stat_in
    key_iota = lax.broadcasted_iota(jnp.int32, (T, T), 0)
    query_iota = lax.broadcasted_iota(jnp.int32, (T, T), 1)
    scale2 = HEAD**-0.5 * LOG2E

    def q_copy(t):
        src = qT if t == 0 else qin.at[t - 1]
        return send(src, qin.at[t], r.q_sems, t, p.along_z(-1))

    def q_wait(t):
        send(qT, qin.at[t], r.q_sems, t, p.along_z(1)).wait_recv()

    def q_pass(t):
        q_wait(t)
        q_copy(t + 1).start()

    def head_rows(h):
        return pl.ds(pl.multiple_of(h * HEAD, HEAD), HEAD)

    def masked(scores, block, causal):
        allowed = key_iota < length - block * T
        if causal:
            allowed = allowed & (key_iota <= query_iota)
        return jnp.where(allowed, scores * scale2, NEG_LARGE)

    def attend(s, own):
        def some_heads(g, _):
            heads = [g * GROUP + i for i in range(GROUP)]
            places = [head_rows(h) for h in heads]
            scores = [masked(dot_tn(kv[s, 0, rows], qT[rows]), p.z - s, own) for rows in places]
            highest = [jnp.max(v, axis=0, keepdims=True) for v in scores]
            if not own:
                highest = [jnp.maximum(v, stat[pl.ds(h, 1)]) for v, h in zip(highest, heads)]
                fade = [jnp.exp2(stat[pl.ds(h, 1)] - v) for v, h in zip(highest, heads)]
            weights = [jnp.exp2(v - m) for v, m in zip(scores, highest)]
            total = [column_sum(v) for v in weights]
            value = [dot(kv[s, 1, rows], v.astype(BF)) for v, rows in zip(weights, places)]
            for i, (h, rows) in enumerate(zip(heads, places)):
                if not own:
                    total[i] = total[i] + mass[pl.ds(h, 1)] * fade[i]
                    value[i] = value[i] + outT[rows] * fade[i]
                stat[pl.ds(h, 1)] = highest[i]
                mass[pl.ds(h, 1)] = total[i]
                outT[rows] = value[i]
            return 0

        lax.fori_loop(0, HEADS // GROUP, some_heads, 0)

    def project(s, block, rows):
        kv[s, 0, :, rows] = dot(block, pool[2]).astype(BF).T
        kv[s, 1, :, rows] = (dot(block, pool[3]) + r.v_qv_bias[1:2]).astype(BF).T

    for half in range(2):
        pl.when(p.z < 3)(functools.partial(lambda half: nx_copy(0, half).start(), half))
    nxT[...] = r.norm_two[...].T
    for copy in qkv_loads:
        copy.wait()
    qT[...] = (dot(r.norm_two[...], pool[1]) + r.v_qv_bias[0:1]).astype(BF).T
    pl.when(p.z >= 1)(lambda: q_copy(0).start())
    project(0, r.norm_two[...], slice(0, T))
    attend(0, True)
    cot_load.wait()
    r.cotT[...] = r.cot[...].T
    for k in range(4):
        r.up_rows[k : k + 1] = r.v_up_bias[k * D : (k + 1) * D].reshape(1, D)

    def act_grad(i):
        down_load(i).wait()
        r.act_grad[lax.rem(i, 3)] = dot_nt(r.cot[...], pool[4 + i])

    lax.fori_loop(0, 3, lambda i, _: (act_grad(i), 0)[1], 0)

    def earlier_block(s, _):
        for half in range(2):
            nx_pass(s, half)
            rows = slice(half * (T // 2), (half + 1) * (T // 2))
            project(s, nx[s - 1, rows], rows)
        attend(s, False)
        pl.when((s == 1) & (p.z < 3))(functools.partial(q_pass, 0))
        return 0

    lax.fori_loop(1, p.z + 1, earlier_block, 0)
    for i in (0, 1, 2):
        up_load(i).start()

    def finish(h, _):
        rows = head_rows(h)
        value = outT[rows] * (1.0 / mass[pl.ds(h, 1)])
        outT[rows] = value
        r.attT[rows] = value.astype(BF)
        return 0

    lax.fori_loop(0, HEADS, finish, 0, unroll=True)
    stat[0:HEADS] = stat[0:HEADS] + jnp.log2(mass[...])
    attT = r.attT

    out_load.wait()
    after = r.tok[...].astype(F32) + table_row + dot(attT[...].T, pool[0]) + row_of(r.v_out_bias)
    r.after[...] = after
    mean, inverse = norm_stats(after)
    norm_two = ((after - mean) * inverse * row_of(r.v_second_gain) + row_of(r.v_second_shift)).astype(BF)
    for half in range(2):
        pl.when(p.z < 3)(functools.partial(lambda half: nx_copy(0, half).wait_send(), half))
    r.norm_two[...] = norm_two
    r.norm_twoT[...] = norm_two.T
    r.total[...] = after + row_of(r.v_down_bias)
    r.t[...] = jnp.zeros((T, D), F32)

    g_down, g_up, g_out = r.g_down, r.g_up, r.g_out

    def scatter(name, parts, out, columns=None):
        return ReduceScatter(
            p,
            getattr(r, "g_" + name),
            getattr(r, "rc_" + name),
            getattr(r, "r1_" + name),
            getattr(r, "r2_" + name),
            getattr(r, "rz1_" + name),
            getattr(r, "rz2_" + name),
            getattr(r, "cs_" + name),
            getattr(r, "ss_" + name),
            parts,
            out,
            getattr(r, "zb_" + name, None),
            columns,
        )

    narrow, width = D // 4, D // 2
    down = scatter("down", "yx", r.s_down)
    up = scatter("up", "z", r.s_up)
    out = scatter("out", "", r.s_out, [(z * narrow, (z + 1) * narrow) for z in range(4)])
    queries, keys, values = [(i * width, (i + 1) * width) for i in range(3)]
    projs = [
        scatter("p0", "", lambda h, v: lay_out(0, h, v), (queries, keys, values, values)),
        scatter("p1", "", lambda h, v: lay_out(1, h, v), (queries, queries, keys, values)),
    ]
    layouts = (
        ((0, width, 0), (0, width, narrow), (0, narrow, width), (narrow, width, 0)),
        ((0, narrow, width), (narrow, width, 0), (0, width, 0), (0, width, narrow)),
    )

    def lay_out(chunk, h, value):
        for z, (first, last, at) in enumerate(layouts[chunk]):

            def store(first=first, last=last, at=at):
                r.s_qkv[h, :, at : at + last - first] = value[:, first:last]

            pl.when(p.z == z)(store)


    def spread(rows):
        table_grad = jnp.where(group_rows == gid, rows[0:1], 0.0)
        return jnp.concatenate([table_grad, rows[1:5]], axis=0)

    early = SmallSum(
        p, r.early_z, r.early_c, r.early_x, r.early_sems, r.early_out, lambda rows: rows
    )
    late = SmallSum(p, r.late_z, r.late_c, r.late_x, r.late_sems, r.late_out, spread)
    small = r.early_z.at[p.z]
    gelu_c = math.sqrt(2.0 / math.pi)

    def pass_on(k):
        down.core_sum(k)
        down.first_start(k)
        up.core_sum(k)
        up.first_start(k)

    def chunk(i, _):
        k = chunk_of(i)
        kh, kl = k // 2, lax.rem(k, 2)
        up_load(i).wait()
        pl.when(i >= 3)(lambda: act_grad(i))
        weight = pool[1 + i]
        weight_down = pool[4 + i]
        hidden = dot(r.norm_two[...], weight) + r.up_rows[pl.ds(k, 1), :]
        square = hidden * hidden
        th = jnp.tanh(gelu_c * hidden * (1.0 + 0.044715 * square))
        half = 0.5 + 0.5 * th
        act = (hidden * half).astype(BF)
        slope = half + 0.5 * hidden * (1.0 - th * th) * gelu_c * (1.0 + 3 * 0.044715 * square)
        grad = r.act_grad[lax.rem(i, 3)] * slope
        small[pl.ds(4 + k, 1), :] = column_sum(grad)
        low = grad.astype(BF)
        piece = D // 2
        for cc in range(2):
            rows = dot(r.cotT[...], act[:, cc * piece : (cc + 1) * piece]).astype(BF)
            part = D // 4
            for z in range(4):
                for h in range(2):
                    at = z * part + h * (part // 2)
                    g_down[h, kh, kl, cc, z // 2, z % 2] = rows[at : at + part // 2]
        down.core_start(k)
        part = D // 8
        for y in range(2):
            rows = dot(r.norm_twoT[y * 4 * part : (y + 1) * 4 * part], low).astype(BF)
            for d in range(4):
                for h in range(2):
                    at = d * part + h * (part // 2)
                    g_up[h, y, d // 2, d % 2, kh, kl] = rows[at : at + part // 2]
        up.core_start(k)
        pl.when(i > 0)(lambda: pass_on(chunk_of(i - 1)))
        r.total[...] += dot(act, weight_down)
        r.t[...] += dot_nt(low, weight)
        pl.when(i == 0)(lambda: up_load(3).start())
        return 0

    lax.fori_loop(0, 4, chunk, 0)
    pass_on(chunk_of(3))
    pl.when(p.z == 1)(functools.partial(q_pass, 1))

    qkv_loads = [
        load(r.qkv_weight.at[:, pl.ds(i * D, D)], pool.at[1 + i], 14 + i) for i in range(3)
    ]
    for copy in qkv_loads:
        copy.start()

    nx[2] = r.total[...].astype(BF)
    result_store = pltpu.make_async_copy(nx.at[2], r.result, r.load_sems.at[17])
    result_store.start()
    cot = r.cot[...].astype(F32)
    after = r.after[...]
    mean, inverse = norm_stats(after)
    n = (after - mean) * inverse
    t = r.t[...]
    after_grad = cot + norm_back(t, row_of(r.v_second_gain), n, inverse)
    r.after[...] = after_grad
    after_low = after_grad.astype(BF)
    doT = r.doT
    doT[...] = dot_nt(pool[0], after_low).astype(BF)
    for h in range(HEADS):
        rows = slice(h * HEAD, (h + 1) * HEAD)
        stat[HEADS + h : HEADS + h + 1] = column_sum(doT[rows].astype(F32) * outT[rows])
    def group_rows_of(group):
        return pl.ds(pl.multiple_of(group * width, width), width)

    def do_copy(t, group):
        rows = group_rows_of(group)
        src = doT.at[rows] if isinstance(t, int) and t == 0 else doin.at[t - 1, rows]
        return send(src, doin.at[t, rows], r.do_sems, 2 * t + group, p.along_z(-1))

    def stat_copy(t):
        src = stat if isinstance(t, int) and t == 0 else stat_in.at[t - 1]
        return send(src, stat_in.at[t], r.stat_sems, t, p.along_z(-1))

    def do_send(t, group):
        pl.when(group == 0)(lambda: stat_copy(t).start())
        do_copy(t, group).start()

    def stat_wait(t):
        send(stat, stat_in.at[t], r.stat_sems, t, p.along_z(1)).wait_recv()

    def do_wait(t, group):
        rows = group_rows_of(group)
        send(doT.at[rows], doin.at[t, rows], r.do_sems, 2 * t + group, p.along_z(1)).wait_recv()
        pl.when(group == 0)(lambda: stat_wait(t))

    for group in range(2):
        pl.when(p.z >= 1)(functools.partial(do_send, 0, group))
    small[pl.ds(0, 1), :] = column_sum(after_grad)
    small[pl.ds(1, 1), :] = column_sum(t * n)
    small[pl.ds(2, 1), :] = column_sum(t)
    small[pl.ds(3, 1), :] = column_sum(cot)
    rows = dot(attT[...], after_low).astype(BF)
    part = D // 8
    for d in range(8):
        for h in range(2):
            at = d * part + h * (part // 2)
            g_out[h, d // 4, (d // 2) % 2, d % 2] = rows[at : at + part // 2]
    out.core_start(0)

    outT[...] = jnp.zeros((D, T), F32)
    key_grad, value_grad = r.key_grad, r.value_grad
    mixed = (kv.at[1, 0], kv.at[1, 1], kv.at[2, 0])

    def grads_of(s, group, queries, out_grads, sums, causal, for_queries, for_keys):
        heads = [group * GROUP + i for i in range(GROUP)]
        places = [head_rows(h) for h in heads]
        scores = [dot_tn(kv[s, 0, rows], queries[rows]) for rows in places]
        prob_grad = [dot_tn(kv[s, 1, rows], out_grads[rows]) for rows in places]
        scores = [masked(v, p.z - s, causal) for v in scores]
        probs = [jnp.exp2(v - sums[pl.ds(h, 1)]) for v, h in zip(scores, heads)]
        score_grad = [
            (v * (w - sums[pl.ds(HEADS + h, 1)])).astype(BF)
            for v, w, h in zip(probs, prob_grad, heads)
        ]
        if for_queries:
            query_add = [dot(kv[s, 0, rows], v) for v, rows in zip(score_grad, places)]
        if for_keys:
            probs = [v.astype(BF) for v in probs]
            key_add = [dot_nt(queries[rows], v) for v, rows in zip(score_grad, places)]
            value_add = [dot_nt(out_grads[rows], v) for v, rows in zip(probs, places)]
        for i, rows in enumerate(places):
            if for_queries:
                outT[rows] = outT[rows] + query_add[i]
            if for_keys and for_queries:
                key_grad[rows] = key_add[i]
                value_grad[rows] = value_add[i]
            elif for_keys:
                key_grad[rows] = key_grad[rows] + key_add[i]
                value_grad[rows] = value_grad[rows] + value_add[i]

    def query_step(i, _):
        grads_of(p.z - i // 2, lax.rem(i, 2), qT, doT, stat, False, True, False)
        return 0

    def own_step(group, _):
        grads_of(0, group, qT, doT, stat, True, True, True)
        return 0

    def key_step(t, group):
        pl.when((p.z == 0) & (group == 0))(lambda: q_wait(t))
        do_wait(t, group)
        pl.when(p.z >= 1)(lambda: do_send(t + 1, group))
        grads_of(0, group, qin.at[t], doin.at[t], stat_in.at[t], False, False, True)

    def proj_grad(group):
        rows = slice(group * width, (group + 1) * width)
        mixed[0][rows] = (outT[rows] * HEAD**-0.5).astype(BF)
        mixed[1][rows] = (key_grad[rows] * HEAD**-0.5).astype(BF)
        mixed[2][rows] = value_grad[rows].astype(BF)
        target = (r.g_p0, r.g_p1)[group]
        part = D // 8
        for i in range(3):
            piece = dot_nt(nxT[...], mixed[i][rows]).astype(BF)
            for d in range(8):
                for h in range(2):
                    at = d * part + h * (part // 2)
                    target[h, d // 4, (d // 2) % 2, d % 2, :, i * width : (i + 1) * width] = piece[
                        at : at + part // 2
                    ]
        projs[group].core_start(0)

    def norm_back_one():
        outT[...] = sum(dot(pool[1 + i], mixed[i][...]) for i in range(3))
        ones = jnp.ones((8, T), BF)
        rows = r.late_z.at[p.z]
        rows[pl.ds(3, 1), :] = dot_nt(ones, mixed[0][...])[0:1]
        rows[pl.ds(4, 1), :] = dot_nt(ones, mixed[2][...])[0:1]
        t1 = outT[...].T
        start = r.tok[...].astype(F32) + table_row
        mean, inverse = norm_stats(start)
        n = (start - mean) * inverse
        start_grad = r.after[...] + norm_back(t1, row_of(r.v_first_gain), n, inverse)
        r.norm_two[...] = start_grad.astype(BF)
        tokens_store.start()
        rows[pl.ds(0, 1), :] = column_sum(start_grad)
        rows[pl.ds(1, 1), :] = column_sum(t1 * n)
        rows[pl.ds(2, 1), :] = column_sum(t1)
        late.advance(0)

    tokens_store = pltpu.make_async_copy(r.norm_two, r.grad_tokens, r.load_sems.at[18])

    for copy in qkv_loads:
        copy.wait()
    lax.fori_loop(0, 2 * p.z, query_step, 0)
    lax.fori_loop(0, 2, own_step, 0)
    step = functools.partial

    ahead = (
        (
            (1, step(up.advance, 1)),
            (1, step(down.advance, 1)),
            (3, step(out.advance, 0)),
            (3, step(down.advance, 2)),
            (5, step(proj_grad, 0)),
        ),
        (
            (2, step(down.advance, 1)),
        ),
        (
        ),
        (
        ),
    )
    rest = (
        ((0, 1), step(down.advance, 1)),
        ((0,), step(up.advance, 1)),
        ((), step(early.advance, 0)),
        ((0,), step(proj_grad, 0)),
        ((0,), step(down.advance, 2)),
        ((), step(projs[0].advance, 0)),
        ((), step(proj_grad, 1)),
        ((), step(up.advance, 2)),
        ((), step(projs[1].advance, 0)),
        ((), norm_back_one),
        ((), step(projs[0].advance, 1)),
        ((), step(down.advance, 3)),
        ((), step(early.advance, 1)),
        ((), step(projs[1].advance, 1)),
        ((0,), step(out.advance, 0)),
        ((), step(up.advance, 3)),
        ((), step(early.advance, 2)),
        ((), step(projs[0].advance, 2)),
        ((), step(late.advance, 1)),
        ((), step(projs[1].advance, 2)),
        ((), step(down.advance, 4)),
        ((), step(out.advance, 1)),
        ((), step(projs[0].advance, 3)),
        ((), step(late.advance, 2)),
        ((), step(out.advance, 2)),
        ((), step(projs[1].advance, 3)),
        ((), step(early.advance, 3)),
        ((), step(late.advance, 3)),
        ((), step(up.advance, 4)),
        ((), step(out.advance, 3)),
        ((), step(projs[1].advance, 4)),
        ((), step(projs[0].advance, 4)),
        ((), step(out.advance, 4)),
    )

    def half_round(i, _):
        for z in range(3):
            for at, one in ahead[z]:
                pl.when((p.z == z) & (i == at))(one)
        pl.when(p.z + i // 2 < 3)(lambda: key_step(i // 2, lax.rem(i, 2)))
        return 0

    for _, one in ahead[3]:
        pl.when(p.z == 3)(one)
    lax.fori_loop(0, 7, half_round, 0)
    for done, one in rest:
        if len(done) == 0:
            one()
        else:
            planes = [z for z in range(4) if z not in done]
            if planes:
                pl.when(functools.reduce(jnp.logical_or, [p.z == z for z in planes]))(one)
    for s in (1, 2):
        for half in range(2):
            pl.when((p.z < 3) & (p.z >= s))(lambda s=s, half=half: nx_copy(s, half).wait_send())
    def sent(t):
        q_copy(t).wait_send()
        stat_copy(t).wait_send()
        do_copy(t, 0).wait_send()
        do_copy(t, 1).wait_send()

    for t in range(3):
        pl.when((p.z >= 1) & (p.z + t <= 3))(functools.partial(sent, t))
    result_store.wait()
    tokens_store.wait()

def row_of(ref):
    return ref[...].reshape(1, ref.shape[0])


def outputs_kernel(result, grad_tokens, early, late, s_qkv, s_out, s_up, s_down, *outs):
    (
        o_result,
        o_tokens,
        o_table,
        o_first_gain,
        o_first_shift,
        o_qkv,
        o_qv_bias,
        o_out,
        o_out_bias,
        o_second_gain,
        o_second_shift,
        o_up,
        o_up_bias,
        o_down,
        o_down_bias,
    ) = outs
    D = early.shape[1]
    o_result[...] = result[...].reshape(o_result.shape)
    o_tokens[...] = grad_tokens[...].reshape(o_tokens.shape)
    o_table[...] = late[0:16]
    o_first_gain[...] = late[16]
    o_first_shift[...] = late[17]
    o_out_bias[...] = early[0]
    o_second_gain[...] = early[1]
    o_second_shift[...] = early[2]
    o_down_bias[...] = early[3]
    for k in range(4):
        o_up_bias[pl.ds(k * D, D)] = early[4 + k]
    o_qv_bias[...] = late[18:20]
    for ref, value in ((o_qkv, s_qkv), (o_out, s_out), (o_up, s_up), (o_down, s_down)):
        half = value.shape[1]
        for h in range(2):
            ref[h * half : (h + 1) * half] = value[h]


def fused(
    tokens,
    group_ids,
    lengths,
    cotangent,
    group_table,
    first_gain,
    first_shift,
    qkv_weight,
    query_value_bias,
    out_weight,
    out_bias,
    second_gain,
    second_shift,
    up_weight,
    up_bias,
    down_weight,
    down_bias,
):
    _, T, D = tokens.shape
    F = up_weight.shape[1]
    any_spec = pl.BlockSpec(memory_space=pl.ANY)
    vmem = pl.BlockSpec(memory_space=pltpu.VMEM)
    smem = pl.BlockSpec(memory_space=pltpu.SMEM)
    inputs = dict(
        tokens=(tokens.reshape(T, D), any_spec),
        group_ids=(group_ids, smem),
        lengths=(lengths, smem),
        cotangent=(cotangent.reshape(T, D), any_spec),
        group_table=(group_table, any_spec),
        first_gain=(first_gain, any_spec),
        first_shift=(first_shift, any_spec),
        qkv_weight=(qkv_weight, any_spec),
        qv_bias=(query_value_bias, any_spec),
        out_weight=(out_weight, any_spec),
        out_bias=(out_bias, any_spec),
        second_gain=(second_gain, any_spec),
        second_shift=(second_shift, any_spec),
        up_weight=(up_weight, any_spec),
        up_bias=(up_bias, any_spec),
        down_weight=(down_weight, any_spec),
        down_bias=(down_bias, any_spec),
    )
    shares = dict(
        down=(D // 8, F // 8),
        up=(D // 16, F // 4),
        out=(D // 16, D // 4),
        qkv=(D // 16, 3 * D // 4),
    )
    outputs = dict(
        result=((T, D), BF),
        grad_tokens=((T, D), BF),
        early_out=((8, D), F32),
        late_out=((20, D), F32),
    )
    outputs.update({"s_" + k: ((2,) + shares[k], F32) for k in ("qkv", "out", "up", "down")})
    dma = pltpu.SemaphoreType.DMA
    scratch = dict(
        pool=pltpu.VMEM((8, D, D), BF),
        v_group_table=pltpu.VMEM(group_table.shape, F32),
        v_first_gain=pltpu.VMEM((D,), F32),
        v_first_shift=pltpu.VMEM((D,), F32),
        v_qv_bias=pltpu.VMEM((2, D), F32),
        v_out_bias=pltpu.VMEM((D,), F32),
        v_second_gain=pltpu.VMEM((D,), F32),
        v_second_shift=pltpu.VMEM((D,), F32),
        v_up_bias=pltpu.VMEM((F,), F32),
        v_down_bias=pltpu.VMEM((D,), F32),
        tok=pltpu.VMEM((T, D), BF),
        cot=pltpu.VMEM((T, D), BF),
        cotT=pltpu.VMEM((D, T), BF),
        nx=pltpu.VMEM((3, T, D), BF),
        nxT=pltpu.VMEM((D, T), BF),
        qT=pltpu.VMEM((D, T), BF),
        kv=pltpu.VMEM((4, 2, D, T), BF),
        outT=pltpu.VMEM((D, T), F32),
        stat=pltpu.VMEM((2 * HEADS, T), F32),
        mass=pltpu.VMEM((HEADS, T), F32),
        qin=pltpu.VMEM((3, D, T), BF),
        doin=pltpu.VMEM((3, D, T), BF),
        stat_in=pltpu.VMEM((3, 2 * HEADS, T), F32),
        key_grad=pltpu.VMEM((D, T), F32),
        value_grad=pltpu.VMEM((D, T), F32),
        attT=pltpu.VMEM((D, T), BF),
        after=pltpu.VMEM((T, D), F32),
        norm_two=pltpu.VMEM((T, D), BF),
        norm_twoT=pltpu.VMEM((D, T), BF),
        act_grad=pltpu.VMEM((3, T, D), F32),
        total=pltpu.VMEM((T, D), F32),
        t=pltpu.VMEM((T, D), F32),
        doT=pltpu.VMEM((D, T), BF),
        up_rows=pltpu.VMEM((4, D), F32),
        early_z=pltpu.VMEM((4, 8, D), F32),
        early_c=pltpu.VMEM((2, 8, D), F32),
        early_x=pltpu.VMEM((4, 8, D), F32),
        late_z=pltpu.VMEM((4, 5, D), F32),
        late_c=pltpu.VMEM((2, 20, D), F32),
        late_x=pltpu.VMEM((4, 20, D), F32),
        load_sems=dma((29,)),
        nx_sems=dma((2, 6)),
        q_sems=dma((2, 3)),
        do_sems=dma((2, 6)),
        stat_sems=dma((2, 3)),
        early_sems=dma((2, 7)),
        late_sems=dma((2, 7)),
    )
    places = dict(
        down=(2, 2, D // 8, F // 8),
        up=(2, 2, D // 16, F // 4),
        out=(D // 16, D),
        p0=(D // 16, 3 * D // 2),
        p1=(D // 16, 3 * D // 2),
    )
    columns_of = dict(shares, p0=(D // 16, D // 2), p1=(D // 16, D // 2))
    for name, place in places.items():
        rows, columns = columns_of[name]
        extra = {
            "g_" + name: pltpu.VMEM((2, 2, 2, 2) + place, BF),
            "rc_" + name: pltpu.VMEM((2, 2, 2) + place, BF),
            "r1_" + name: pltpu.VMEM((2, 2) + place, BF),
            "r2_" + name: pltpu.VMEM((2,) + place, BF),
            "rz1_" + name: pltpu.VMEM((2, 2, rows, columns), BF),
            "rz2_" + name: pltpu.VMEM((2, rows, columns), BF),
            "cs_" + name: dma((2, 4)),
            "ss_" + name: dma((2, 12)),
        }
        if len(place) == 2:
            extra["zb_" + name] = pltpu.VMEM((2, 2, 2, rows, columns), BF)
        scratch.update(extra)
    names = list(inputs) + list(outputs) + list(scratch)
    done = pl.pallas_call(
        functools.partial(layer_kernel, names),
        name="layer",
        out_shape=[jax.ShapeDtypeStruct(*o) for o in outputs.values()],
        in_specs=[i[1] for i in inputs.values()],
        out_specs=[any_spec] * 2 + [vmem] * (len(outputs) - 2),
        scratch_shapes=list(scratch.values()),
        compiler_params=pltpu.CompilerParams(
            collective_id=0, has_side_effects=True, vmem_limit_bytes=VMEM_LIMIT
        ),
    )(*[i[0] for i in inputs.values()])
    shape = jax.ShapeDtypeStruct
    outs = pl.pallas_call(
        outputs_kernel,
        name="outputs",
        out_shape=[
            shape((1, T, D), BF),
            shape((1, T, D), BF),
            shape((16, D), F32),
            shape((D,), F32),
            shape((D,), F32),
            shape((D // 8, 3 * D // 4), F32),
            shape((2, D), F32),
            shape((D // 8, D // 4), F32),
            shape((D,), F32),
            shape((D,), F32),
            shape((D,), F32),
            shape((D // 8, F // 4), F32),
            shape((F,), F32),
            shape((D // 4, F // 8), F32),
            shape((D,), F32),
        ],
        in_specs=[vmem] * len(done),
        out_specs=[vmem] * 15,
    )(*done)
    return (*outs[:13], outs[13].T, outs[14])


def shifted(array, axis, by):
    devices = lax.axis_size(axis)
    pairs = [(i, i + by) for i in range(devices) if 0 <= i + by < devices]
    return lax.ppermute(array, axis, pairs)


def as_sent(array):
    return jax.tree.map(lambda a: a.astype(jnp.bfloat16) if a.dtype == jnp.float32 else a, array)


def shifted_2(block, axis, distance):
    devices = range(lax.axis_size(axis))
    route = [((i - distance) % len(devices), i) for i in devices]
    return lax.ppermute(block, axis, route)


def layer_norm(inputs, norm_gain, norm_shift):
    average = jnp.mean(inputs, -1, keepdims=True)
    centred = inputs - average
    inverse = lax.rsqrt(jnp.mean(centred * centred, -1, keepdims=True) + EPSILON)
    return centred * inverse * norm_gain + norm_shift


def tanh_gelu(inputs):
    return jax.nn.gelu(inputs, approximate=True)


def keep_same(state_value):
    return state_value


def scores_of(queries, key_piece, key_start, query_start, lengths):
    sequences, block_len = (queries.shape[0], queries.shape[1])
    key_heads = key_piece.reshape(sequences, key_piece.shape[1], HEADS, HEAD)
    raw_scores = jnp.einsum(
        "gqhe,gkhe->ghqk", queries, key_heads, preferred_element_type=jnp.float32
    ) * HEAD ** (-0.5)
    key_pos = key_start + jnp.arange(key_piece.shape[1])
    query_pos = query_start + jnp.arange(block_len)
    allowed = (query_pos[:, None] >= key_pos[None, :])[None] & (
        key_pos[None, None, :] < lengths[:, None, None]
    )
    return (raw_scores, allowed[:, None])


def plain(
    tokens,
    group_ids,
    lengths,
    cotangent,
    group_table,
    first_gain,
    first_shift,
    qkv_weight,
    query_value_bias,
    out_weight,
    out_bias,
    second_gain,
    second_shift,
    up_weight,
    up_bias,
    down_weight,
    down_bias,
):
    sequences, block_len, features = tokens.shape
    token_rows = sequences * block_len
    seq_count = lax.axis_size("seq")
    seq_index = lax.axis_index("seq")
    query_start = seq_index * block_len
    score_scale = HEAD ** (-0.5)
    one_hot = (group_ids[:, None] == jnp.arange(group_table.shape[0])[None, :]).astype(jnp.float32)
    table_rows = jnp.dot(one_hot, group_table, precision=EXACT)
    start_rows = (tokens.astype(jnp.float32) + table_rows[:, None, :]).reshape(token_rows, features)
    norm_one, pull_one = jax.vjp(layer_norm, start_rows, first_gain, first_shift)
    norm_one_low = norm_one.astype(jnp.bfloat16)
    full_bias = jnp.concatenate(
        [query_value_bias[0], jnp.zeros((features,), jnp.float32), query_value_bias[1]]
    )
    mixed_rows = (
        jnp.dot(norm_one_low, qkv_weight, preferred_element_type=jnp.float32) + full_bias
    ).astype(jnp.bfloat16)
    mixed_rows = mixed_rows.reshape(sequences, block_len, 3 * features)
    queries = mixed_rows[:, :, :features].reshape(sequences, block_len, HEADS, HEAD)
    key_rows = mixed_rows[:, :, features : 2 * features]
    values = mixed_rows[:, :, 2 * features :]
    pieces = []
    current = (key_rows, values)
    for cycle_step in range(seq_count):
        if cycle_step > 0:
            current = shifted((current[0], current[1]), "seq", 1)
        anchor = (seq_index - cycle_step) % seq_count
        pieces.append((current[0], current[1], anchor * block_len, cycle_step <= seq_index))
    shape_rows = (sequences, HEADS, block_len)
    row_max = jnp.full(shape_rows, NEG_LARGE, jnp.float32)
    row_sum = jnp.zeros(shape_rows, jnp.float32)
    stored = []
    for key_piece, value_piece, key_start, active in pieces:

        def visit_block(state_pair, key_piece=key_piece, key_start=key_start):
            raw_scores, allowed = scores_of(queries, key_piece, key_start, query_start, lengths)
            masked_scores = jnp.where(allowed, raw_scores, NEG_LARGE)
            new_max = jnp.maximum(state_pair[0], jnp.max(masked_scores, -1))
            weights = jnp.where(allowed, jnp.exp(masked_scores - new_max[..., None]), 0.0)
            return (
                new_max,
                state_pair[1] * jnp.exp(state_pair[0] - new_max) + jnp.sum(weights, -1),
                masked_scores,
            )

        def pass_block(state_pair):
            return (
                state_pair[0],
                state_pair[1],
                jnp.full(shape_rows + (block_len,), NEG_LARGE, jnp.float32),
            )

        row_max, row_sum, masked_scores = lax.cond(
            active, visit_block, pass_block, (row_max, row_sum)
        )
        stored.append(masked_scores)
    log_sum = row_max + jnp.log(row_sum)
    attended = jnp.zeros((sequences, block_len, HEADS, HEAD), jnp.float32)
    for piece_data, masked_scores in zip(pieces, stored):

        def attend_block(total_out, value_piece=piece_data[1], masked_scores=masked_scores):
            probs = jnp.exp(masked_scores - log_sum[..., None]).astype(jnp.bfloat16)
            value_heads = value_piece.reshape(sequences, block_len, HEADS, HEAD)
            return total_out + jnp.einsum(
                "ghqk,gkhe->gqhe", probs, value_heads, preferred_element_type=jnp.float32
            )

        attended = lax.cond(piece_data[3], attend_block, keep_same, attended)
    attended_low = attended.reshape(token_rows, features).astype(jnp.bfloat16)
    after_attn = (
        start_rows
        + jnp.dot(attended_low, out_weight, preferred_element_type=jnp.float32)
        + out_bias
    )
    norm_two, pull_two = jax.vjp(layer_norm, after_attn, second_gain, second_shift)
    norm_two_low = norm_two.astype(jnp.bfloat16)
    up_rows = jnp.dot(norm_two_low, up_weight, preferred_element_type=jnp.float32) + up_bias
    activated, pull_gelu = jax.vjp(tanh_gelu, up_rows)
    activated_low = activated.astype(jnp.bfloat16)
    result_rows = (
        after_attn
        + jnp.dot(activated_low, down_weight, preferred_element_type=jnp.float32)
        + down_bias
    )
    result = result_rows.astype(jnp.bfloat16).reshape(tokens.shape)
    outer_low = cotangent.reshape(token_rows, features)
    outer_grad = outer_low.astype(jnp.float32)
    grad_down_weight = jnp.dot(activated_low.T, outer_low, preferred_element_type=jnp.float32)
    grad_down_bias = jnp.sum(outer_grad, 0)
    up_grad = pull_gelu(jnp.dot(outer_low, down_weight.T, preferred_element_type=jnp.float32))[0]
    grad_up_bias = jnp.sum(up_grad, 0)
    up_low = up_grad.astype(jnp.bfloat16)
    grad_up_weight = jnp.dot(norm_two_low.T, up_low, preferred_element_type=jnp.float32)
    part_after, grad_second_gain, grad_second_shift = pull_two(
        jnp.dot(up_low, up_weight.T, preferred_element_type=jnp.float32)
    )
    after_grad = outer_grad + part_after
    grad_out_bias = jnp.sum(after_grad, 0)
    after_low = after_grad.astype(jnp.bfloat16)
    grad_out_weight = jnp.dot(attended_low.T, after_low, preferred_element_type=jnp.float32)
    out_grad = jnp.dot(after_low, out_weight.T, preferred_element_type=jnp.float32).astype(
        jnp.bfloat16
    )
    out_grad = out_grad.reshape(sequences, block_len, HEADS, HEAD)
    delta = jnp.transpose(jnp.sum(out_grad.astype(jnp.float32) * attended, -1), (0, 2, 1))

    def back_block(query_grad, key_piece, value_piece, key_start):
        raw_scores, allowed = scores_of(queries, key_piece, key_start, query_start, lengths)
        probs = jnp.where(allowed, jnp.exp(raw_scores - log_sum[..., None]), 0.0)
        value_heads = value_piece.reshape(sequences, block_len, HEADS, HEAD)
        key_heads = key_piece.reshape(sequences, block_len, HEADS, HEAD)
        prob_grad = jnp.einsum(
            "gqhe,gkhe->ghqk", out_grad, value_heads, preferred_element_type=jnp.float32
        )
        score_grad = (probs * (prob_grad - delta[..., None])).astype(jnp.bfloat16)
        query_grad = (
            query_grad
            + jnp.einsum(
                "ghqk,gkhe->gqhe", score_grad, key_heads, preferred_element_type=jnp.float32
            )
            * score_scale
        )
        key_add = (
            jnp.einsum("ghqk,gqhe->gkhe", score_grad, queries, preferred_element_type=jnp.float32)
            * score_scale
        )
        value_add = jnp.einsum(
            "ghqk,gqhe->gkhe",
            probs.astype(jnp.bfloat16),
            out_grad,
            preferred_element_type=jnp.float32,
        )
        return (
            query_grad,
            key_add.reshape(sequences, block_len, features),
            value_add.reshape(sequences, block_len, features),
        )

    empty_rows = jnp.zeros((sequences, block_len, features), jnp.float32)

    def skip_back(query_grad):
        return (query_grad, empty_rows, empty_rows)

    query_grad = jnp.zeros((sequences, block_len, HEADS, HEAD), jnp.float32)
    carried = (empty_rows, empty_rows)
    for cycle_step in range(seq_count):
        piece_data = pieces[cycle_step]

        def visit_back(state_grad, piece_data=piece_data):
            return back_block(state_grad, piece_data[0], piece_data[1], piece_data[2])

        query_grad, key_add, value_add = lax.cond(piece_data[3], visit_back, skip_back, query_grad)
        carried = shifted_2(
            (as_sent(carried[0] + key_add), as_sent(carried[1] + value_add)), "seq", 1
        )
    key_grad, value_grad = carried
    query_flat = query_grad.reshape(token_rows, features)
    key_flat = key_grad.reshape(token_rows, features)
    value_flat = value_grad.reshape(token_rows, features)
    grad_query_value_bias = jnp.stack([jnp.sum(query_flat, 0), jnp.sum(value_flat, 0)])
    mixed_grad = jnp.concatenate([query_flat, key_flat, value_flat], -1).astype(jnp.bfloat16)
    grad_qkv_weight = jnp.dot(norm_one_low.T, mixed_grad, preferred_element_type=jnp.float32)
    part_start, grad_first_gain, grad_first_shift = pull_one(
        jnp.dot(mixed_grad, qkv_weight.T, preferred_element_type=jnp.float32)
    )
    start_grad = after_grad + part_start
    grad_tokens = start_grad.astype(jnp.bfloat16).reshape(tokens.shape)
    grad_group_table = jnp.dot(
        one_hot.T, jnp.sum(start_grad.reshape(sequences, block_len, features), 1), precision=EXACT
    )
    small_sums = lax.psum(
        (
            grad_group_table,
            grad_first_gain,
            grad_first_shift,
            grad_query_value_bias,
            grad_out_bias,
            grad_second_gain,
            grad_second_shift,
            grad_up_bias,
            grad_down_bias,
        ),
        ("dp", "seq"),
    )
    matrices = (grad_qkv_weight, grad_out_weight, grad_up_weight, grad_down_weight)
    shares = (
        lax.psum_scatter(
            matrices[0].astype(jnp.bfloat16), "seq", scatter_dimension=1, tiled=True
        ).astype(jnp.float32),
        lax.psum_scatter(
            matrices[1].astype(jnp.bfloat16), "seq", scatter_dimension=1, tiled=True
        ).astype(jnp.float32),
        lax.psum_scatter(
            matrices[2].astype(jnp.bfloat16), "seq", scatter_dimension=1, tiled=True
        ).astype(jnp.float32),
        lax.psum_scatter(
            matrices[3].astype(jnp.bfloat16), "seq", scatter_dimension=1, tiled=True
        ).astype(jnp.float32),
    )
    shares = (
        lax.psum_scatter(
            shares[0].astype(jnp.bfloat16), "dp", scatter_dimension=0, tiled=True
        ).astype(jnp.float32),
        lax.psum_scatter(
            shares[1].astype(jnp.bfloat16), "dp", scatter_dimension=0, tiled=True
        ).astype(jnp.float32),
        lax.psum_scatter(
            shares[2].astype(jnp.bfloat16), "dp", scatter_dimension=0, tiled=True
        ).astype(jnp.float32),
        lax.psum_scatter(
            shares[3].astype(jnp.bfloat16), "dp", scatter_dimension=0, tiled=True
        ).astype(jnp.float32),
    )
    return (
        result,
        grad_tokens,
        small_sums[0],
        small_sums[1],
        small_sums[2],
        shares[0],
        small_sums[3],
        shares[1],
        small_sums[4],
        small_sums[5],
        small_sums[6],
        shares[2],
        small_sums[7],
        shares[3],
        small_sums[8],
    )


def solution(mesh):
    in_specs = (
        P("dp", "seq", None),
        P("dp"),
        P("dp"),
        P("dp", "seq", None),
        P(),
        P(),
        P(),
        P(),
        P(),
        P(),
        P(),
        P(),
        P(),
        P(),
        P(),
        P(),
        P(),
    )
    out_specs = (
        P("dp", "seq", None),
        P("dp", "seq", None),
        P(),
        P(),
        P(),
        P("dp", "seq"),
        P(),
        P("dp", "seq"),
        P(),
        P(),
        P(),
        P("dp", "seq"),
        P(),
        P("dp", "seq"),
        P(),
    )
    def shards(*arrays):
        sizes = (mesh.shape["dp"], mesh.shape["seq"]) + arrays[0].shape
        return (fused if sizes == (8, 4, 1, 256, 768) else plain)(*arrays)

    return jax.shard_map(shards, mesh=mesh, in_specs=in_specs, out_specs=out_specs, check_vma=False)
```
